32 devices in a mesh: dp: 8 (over y, x, core), seq: 4 (over z).
Axes of the slice: x: 2, y: 2, z: 4, core: 2. Of those that a mesh axis runs over, the one named last changes fastest.
Arguments:
- tokens: bfloat16 [64, 512, 768], P('dp', 'seq'), may hold values from -6 to 6
- cotangent: bfloat16 [64, 512, 768], P('dp', 'seq'), may hold values from -6 to 6
- lengths: int32 [64], P('dp'), may hold values from 64 to 512, as said below
- owner: int32 [72], replicated, may hold values from 0 to 143, as said below
- master: float32 [144, 128, 768], P('dp'), as said below
- moment: float32 [144, 128, 768], P('dp'), may hold values from -56 to 56
- second: float32 [144, 128, 768], P('dp'), may hold values from 81.92 to 1310.72
- vec_master: float32 [12, 768], replicated
- vec_moment: float32 [12, 768], replicated, may hold values from -320 to 320
- vec_second: float32 [12, 768], replicated, may hold values from 3276.8 to 32768
Outputs:
- layer_out: bfloat16 [64, 512, 768], P('dp', 'seq')
- input_grad: float32 [64, 512, 768], P('dp', 'seq')
- residual_mid: float32 [64, 512, 768], P('dp', 'seq')
- sublayer_rms: float32 [64, 2], P('dp')
- grad_pool: float32 [144, 128, 768], P('dp')
- moment_new: float32 [144, 128, 768], P('dp')
- second_new: float32 [144, 128, 768], P('dp')
- master_new: float32 [144, 128, 768], P('dp')
- vec_grad: float32 [12, 768], replicated
- vec_moment_new: float32 [12, 768], replicated
- vec_second_new: float32 [12, 768], replicated
- vec_master_new: float32 [12, 768], replicated
The draws below stay inside these ranges and needn't reach their ends.
Inputs may be any that keep to these rules, and one draw needn't show every extreme that they name: `lengths`: one sequence of each index of dp has length 512. Distinct slot numbers; block b lives in slot owner[b]. `master`: slots not named by owner hold values that only their own update reads.
All inputs are finite; a program needn't handle non-finite values.
Results may differ from the reference program's by a relative error of at most 0.025.
Values may be sent and summed in bfloat16 or wider, within the bound.
A program may use at most 320 MiB of HBM per device.

```python
import math
import jax
import jax.numpy as jnp
from jax import lax

D = 768
H = 12
DH = 64
FF = 3072
SEQLEN = 512
SEQS = 8
BLK = 128
STEP = 5
NBLK = 72
VEC = 12
POOL = 144
NSEQ = 64
TOKENS = 32768


def owner_slots(key):
    inner = jax.random.permutation(jax.random.fold_in(key, 11), POOL - 2) + 1
    chosen = jnp.concatenate([jnp.array([0, POOL - 1], jnp.int32), inner[:NBLK - 2].astype(jnp.int32)])
    order = jax.random.permutation(jax.random.fold_in(key, 12), NBLK)
    return chosen[order].astype(jnp.int32)


def draw_owner(key, part):
    return owner_slots(key)


def draw_master(key, part):
    slots = owner_slots(key)
    key = jax.random.fold_in(key, 2)
    square_count = D // BLK
    wide_count = FF // BLK
    base = D ** (-0.5)
    block_scale = jnp.concatenate([jnp.full((3 * square_count,), base, jnp.float32), jnp.full((square_count,), base * SEQLEN ** 0.5 / 3.0, jnp.float32), jnp.full((wide_count,), base, jnp.float32), jnp.full((wide_count,), FF ** (-0.5), jnp.float32)])
    slot_scale = jnp.full((POOL,), base, jnp.float32).at[slots].set(block_scale)
    noise_draw = jax.random.normal(key, (POOL, BLK, D), jnp.float32)
    return noise_draw * slot_scale[:, None, None]


def draw_lengths(key, part):
    key = jax.random.fold_in(key, 3)
    groups = NSEQ // SEQS
    base = jax.random.randint(key, (groups, SEQS), SEQLEN // 8, SEQLEN + 1)
    picked = jax.random.randint(jax.random.fold_in(key, 4), (groups, 1), 0, SEQS)
    longest = jnp.arange(SEQS)[None, :] == picked
    return jnp.where(longest, SEQLEN, base).reshape(NSEQ).astype(jnp.int32)


def draw_vec_master(key, part):
    key = jax.random.fold_in(key, 5)
    noise_draw = jax.random.normal(key, (VEC, D), jnp.float32)
    row_index = jnp.arange(VEC)[:, None]
    gains = (row_index == 4) | (row_index == 6)
    return jnp.where(gains, 1.0 + 0.1 * noise_draw, 0.3 * noise_draw)


def steps_of(key, extent, cuts, low, high):
    level = 1.0
    for dim, parts in cuts:
        steps = jax.random.uniform(jax.random.fold_in(jax.random.fold_in(key, 6), dim), (parts,), jnp.float32, low / len(cuts), high / len(cuts))
        level = level * jnp.repeat(jnp.exp(steps), extent[dim] // parts).reshape((-1,) + (1,) * (len(extent) - 1 - dim))
    return level


def gaussian(own_key, shape, scale, most, shards=(), kind=jnp.bfloat16):
    values = jax.random.normal(own_key, shape, jnp.float32) * scale
    if len(shards) > 0:
        values = steps_of(own_key, shape, shards, -0.22, 0.18) * values
    return jnp.clip(values, min=-most, max=most).astype(kind)


def setup_inputs(seed: int = 0) -> dict:
    key_of = jax.random.split(jax.random.key(seed), 11)
    tokens = gaussian(key_of[0], (NSEQ, SEQLEN, D), 1.0, 6.0, ((0, 8), (1, 4)))
    cotangent = gaussian(key_of[1], (NSEQ, SEQLEN, D), 1.0, 6.0, ((0, 8), (1, 4)))
    lengths = draw_lengths(jax.random.fold_in(key_of[10], 71), 0)
    owner = draw_owner(jax.random.fold_in(key_of[10], 71), 0)
    master = draw_master(jax.random.fold_in(key_of[10], 71), 0)
    moment = gaussian(key_of[5], (POOL, BLK, D), (0.05 * TOKENS ** 0.5), 56.0, ((0, 8),), jnp.float32)
    second = jnp.clip(jnp.exp(math.log(1310.72) - 2.7725887 * jax.random.uniform(key_of[6], (POOL, BLK, D), jnp.float32) ** steps_of(key_of[6], (POOL, BLK, D), ((0, 8),), -0.2, 0.2)), 81.92, 1310.72)
    vec_master = draw_vec_master(jax.random.fold_in(key_of[10], 71), 0)
    vec_moment = gaussian(key_of[8], (VEC, D), (0.3 * TOKENS ** 0.5), 320.0, (), jnp.float32)
    vec_second = jnp.clip(jnp.exp(jax.random.uniform(key_of[9], (VEC, D), jnp.float32, math.log(3276.8), math.log(32768.0))), 3276.8, 32768.0)
    return {"tokens": tokens, "cotangent": cotangent, "lengths": lengths, "owner": owner, "master": master, "moment": moment, "second": second, "vec_master": vec_master, "vec_moment": vec_moment, "vec_second": vec_second}


@jax.custom_vjp
def low(v):
    return lax.optimization_barrier(v.astype(jnp.bfloat16)).astype(jnp.float32)

@jax.custom_vjp
def low_back(v):
    return v

def low_keep(v):
    return (low(v), None)

def low_pass(kept, grad):
    return (grad,)

def back_keep(v):
    return (v, None)

def back_low(kept, grad):
    return (low(grad),)
low.defvjp(low_keep, low_pass)
low_back.defvjp(back_keep, back_low)
first_decay = 0.5
second_decay = 0.5
matrix_rate = 0.02
vector_rate = 0.2
weight_decay = 0.01
adam_epsilon = 1e-08

def product(left, right):
    return jnp.dot(left, right, precision=lax.Precision.HIGHEST, preferred_element_type=jnp.float32)

def norm_rows(resid, gain, shift):
    center = resid - lax.optimization_barrier(jnp.mean(resid, axis=-1, keepdims=True))
    spread = lax.optimization_barrier(jnp.mean(center * center, axis=-1, keepdims=True))
    return center * lax.rsqrt(spread + 1e-05) * gain + shift

def attend_one(queries, key_rows, value_rows, length):
    raw_scores = jnp.einsum('qhe,khe->hqk', queries, key_rows, precision=lax.Precision.HIGHEST)
    scores = low_back(raw_scores) * 0.125
    valid_keys = jnp.arange(SEQLEN) < length
    scores = jnp.where(valid_keys[None, None, :], scores, -1e+30)
    log_total = jax.nn.logsumexp(scores, axis=-1, keepdims=True)
    probs = low(jnp.exp(scores - log_total))
    return jnp.einsum('hqk,khe->qhe', probs, value_rows, precision=lax.Precision.HIGHEST)

def attend_packed(packed):
    return jax.checkpoint(attend_one)(packed[0], packed[1], packed[2], packed[3])

def split_blocks(flat):
    square_count = D // BLK
    wide_count = FF // BLK
    squares = [flat[number * square_count:(number + 1) * square_count].reshape(D, D) for number in range(4)]
    offset = 4 * square_count
    w_up = flat[offset:offset + wide_count].reshape(FF, D)
    w_down = flat[offset + wide_count:].reshape(FF, D)
    return (squares[0], squares[1], squares[2], squares[3], w_up, w_down)

def layer_forward(mats, vectors, inputs, lengths):
    w_query, w_key, w_value, w_out, w_up, w_down = [low(matrix) for matrix in mats]
    seq_count = inputs.shape[0]
    token_rows = inputs.reshape(-1, D)
    bias_up = vectors[8:].reshape(FF)
    queries = low_back(low(product(token_rows, w_query) + vectors[0]))
    key_rows = low_back(low(product(token_rows, w_key)))
    value_rows = low_back(low(product(token_rows, w_value) + vectors[1]))
    shaped = (seq_count, SEQLEN, H, DH)
    context = lax.map(attend_packed, (queries.reshape(shaped), key_rows.reshape(shaped), value_rows.reshape(shaped), lengths))
    context = low_back(low(context.reshape(-1, D)))
    branch = low_back(product(context, w_out) + vectors[2])
    middle = norm_rows(token_rows + branch, vectors[4], vectors[5])
    inner = low_back(product(low(middle), w_up.T) + bias_up)
    feed = low_back(product(low(jax.nn.gelu(inner, approximate=False)), w_down) + vectors[3])
    result = norm_rows(middle + feed, vectors[6], vectors[7])
    return (result, (middle, branch, feed))

def adam_step(gradient, moment, second, weight, rate):
    moment_new = first_decay * moment + (1.0 - first_decay) * gradient
    second_new = second_decay * second + (1.0 - second_decay) * gradient * gradient
    moment_hat = moment_new / (1.0 - first_decay ** STEP)
    second_hat = second_new / (1.0 - second_decay ** STEP)
    weight_new = weight - rate * (moment_hat / (jnp.sqrt(second_hat) + adam_epsilon) + weight_decay * weight)
    return (moment_new, second_new, weight_new)

def reference(tokens, cotangent, lengths, owner, master, moment, second, vec_master, vec_moment, vec_second):
    mats = split_blocks(master[owner])
    groups = tokens.shape[0] // SEQS

    def group_step(carry, item):
        inputs, upstream, group_len = item
        inputs = inputs.astype(jnp.float32)

        def bound(mat_list, vectors, values):
            return layer_forward(mat_list, vectors, values, group_len)
        result, backward, extras = jax.vjp(bound, mats, vec_master, inputs, has_aux=True)
        positions = jnp.arange(SEQLEN)[None, :] < group_len[:, None]
        row_mask = positions.astype(jnp.float32).reshape(-1, 1)
        grad_mats, grad_vec, grad_in = backward(upstream.astype(jnp.float32).reshape(-1, D) * row_mask)
        middle, branch, feed = extras
        sums = jnp.stack([lax.optimization_barrier(jnp.sum((branch * branch * row_mask).reshape(SEQS, -1), axis=1)), lax.optimization_barrier(jnp.sum((feed * feed * row_mask).reshape(SEQS, -1), axis=1))], axis=1)
        sub_rms = jnp.sqrt(sums / (group_len[:, None].astype(jnp.float32) * D))
        carry = (jax.tree.map(jnp.add, carry[0], grad_mats), carry[1] + grad_vec)
        return (carry, (result.astype(jnp.bfloat16).reshape(SEQS, SEQLEN, D), grad_in, middle.reshape(SEQS, SEQLEN, D), sub_rms))
    start = (tuple((jnp.zeros_like(matrix) for matrix in mats)), jnp.zeros_like(vec_master))
    items = (tokens.reshape(groups, SEQS, SEQLEN, D), cotangent.reshape(groups, SEQS, SEQLEN, D), lengths.reshape(groups, SEQS))
    sums_all, outputs = lax.scan(group_step, start, items)
    grad_mats, vec_grad = sums_all
    layer_out = outputs[0].reshape(-1, SEQLEN, D)
    input_grad = outputs[1].reshape(-1, SEQLEN, D)
    residual_mid = outputs[2].reshape(-1, SEQLEN, D)
    sublayer_rms = outputs[3].reshape(-1, 2)
    flat = jnp.concatenate([matrix.reshape(-1, BLK, D) for matrix in grad_mats], axis=0)
    grad_pool = jnp.zeros_like(master).at[owner].set(flat)
    moment_new, second_new, master_new = adam_step(grad_pool, moment, second, master, matrix_rate)
    vec_moment_new, vec_second_new, vec_master_new = adam_step(vec_grad, vec_moment, vec_second, vec_master, vector_rate)
    return (layer_out, input_grad, residual_mid, sublayer_rms, grad_pool, moment_new, second_new, master_new, vec_grad, vec_moment_new, vec_second_new, vec_master_new)
```

```python
from functools import partial

import jax
import jax.numpy as jnp
from jax import lax
from jax.experimental import pallas as pl
from jax.experimental.pallas import tpu as pltpu
from jax.sharding import PartitionSpec as P

D = 768
H = 12
DH = 64
FF = 3072
BLK = 128
SEQLEN = 512
STEP = 5


first_decay = 0.5
second_decay = 0.5
matrix_rate = 0.02
vector_rate = 0.2
weight_decay = 0.01
adam_epsilon = 1e-08


def adam_step(gradient, moment, second, weight, rate):
    moment_new = first_decay * moment + (1.0 - first_decay) * gradient
    second_new = second_decay * second + (1.0 - second_decay) * gradient * gradient
    moment_hat = moment_new * (1.0 / (1.0 - first_decay**STEP))
    second_hat = second_new * (1.0 / (1.0 - second_decay**STEP))
    root = second_hat * lax.rsqrt(second_hat) + adam_epsilon
    inverse = pltpu.reciprocal(root, approx=True)
    inverse = inverse * (2.0 - root * inverse)
    weight_new = weight - rate * (moment_hat * inverse + weight_decay * weight)
    return (moment_new, second_new, weight_new)


def seq_swap(parts, axis):
    size = lax.axis_size(axis)
    me = lax.axis_index(axis)
    stacked = parts
    got = [None] * size
    mine = lax.dynamic_index_in_dim(stacked, me, 0, keepdims=False)
    out = [mine]
    for hop in range(1, size):
        there = jnp.bitwise_xor(me, hop)
        piece = lax.dynamic_index_in_dim(stacked, there, 0, keepdims=False)
        route = [(i, i ^ hop) for i in range(size)]
        out.append(lax.ppermute(piece, axis, route))
    return out


def from_hops(pieces, axis):
    size = lax.axis_size(axis)
    me = lax.axis_index(axis)
    stacked = jnp.stack(pieces, axis=0)
    order = jnp.bitwise_xor(jnp.arange(size, dtype=jnp.int32), me)
    return jnp.take(stacked, order, axis=0)


def to_whole(block, axis):
    size = lax.axis_size(axis)
    count, length, width = block.shape
    pieces = seq_swap(block.reshape(size, count // size, length, width), axis)
    stacked = from_hops(pieces, axis)
    return jnp.swapaxes(stacked, 0, 1).reshape(count // size, size * length, width)


def to_split(whole, axis):
    size = lax.axis_size(axis)
    own, full, width = whole.shape
    parts = jnp.swapaxes(whole.reshape(own, size, full // size, width), 0, 1)
    pieces = seq_swap(parts, axis)
    return from_hops(pieces, axis).reshape(size * own, full // size, width)


LANES = 128
PAIRS = D // LANES
CHUNKS = FF // D
MASKED = -1e30
NT = (((1,), (1,)), ((), ()))
TN = (((0,), (0,)), ((), ()))
MIB = 1 << 20


def mm(left, right):
    return jnp.dot(left, right, preferred_element_type=jnp.float32)


def mm_nt(left, right):
    return lax.dot_general(left, right, NT, preferred_element_type=jnp.float32)


def mm_tn(left, right):
    return lax.dot_general(left, right, TN, preferred_element_type=jnp.float32)


def load_blocks(pool_ref, place_ref, first, into_ref, sem):
    def start(i, _):
        pltpu.make_async_copy(
            pool_ref.at[place_ref[first + i]], into_ref.at[pl.ds(i * BLK, BLK)], sem
        ).start()
        return 0

    lax.fori_loop(0, into_ref.shape[0] // BLK, start, 0)


def wait_whole(ref, sem):
    pltpu.make_async_copy(ref, ref, sem).wait()


def spare_lanes(rows, half, bias_column):
    lane = lax.broadcasted_iota(jnp.int32, (rows, LANES), 1)
    first = DH * (1 - half)
    spare = jnp.where(lane == first, bias_column, jnp.where(lane < first + 4, 1.0, 0.0))
    inside = (lane >= DH * half) & (lane < DH * half + DH)
    return inside, spare.astype(jnp.bfloat16)


def split3(row):
    one = row.astype(jnp.bfloat16)
    rest = row - one.astype(jnp.float32)
    two = rest.astype(jnp.bfloat16)
    three = (rest - two.astype(jnp.float32)).astype(jnp.bfloat16)
    return one, two, three


def beside(head_rows, extra, half):
    columns = head_rows.shape[1]
    pad = jnp.zeros((DH - extra.shape[0], columns), jnp.bfloat16)
    parts = [extra.astype(jnp.bfloat16), pad]
    order = [head_rows] + parts if half == 0 else parts + [head_rows]
    return jnp.concatenate(order, axis=0)


def forward_pair(q_ref, k_ref, v_ref, ctx_ref, lse_ref, seq, p, bias):
    rows = q_ref.shape[0]
    cols = pl.ds(pl.multiple_of(p * LANES, LANES), LANES)
    row8 = lax.broadcasted_iota(jnp.int32, (16, rows), 0)
    q2t = q_ref[:, cols].T
    k2 = k_ref[:, cols]
    v2t = v_ref[:, cols].T
    outs = []
    for half in range(2):
        inside, spare = spare_lanes(rows, half, bias)
        k_aug = jnp.where(inside, k2, spare)
        head = slice(half * DH, half * DH + DH)
        q_aug = beside(q2t[head], jnp.where(row8 == 0, 1.0, 0.0), half)
        scores = mm(k_aug, q_aug)
        top = jnp.max(scores, axis=0, keepdims=True)
        expos = jnp.exp(scores - top).astype(jnp.bfloat16)
        v_aug = jnp.concatenate([v2t[head], jnp.ones((16, rows), jnp.bfloat16)], axis=0)
        both = mm(v_aug, expos)
        total = both[DH : DH + 1]
        outs.append(both[0:DH] / total)
        lse_ref[seq, pl.ds(2 * p + half, 1), :] = top + jnp.log(total)
    ctx_ref[:, cols] = jnp.concatenate(outs, axis=0).T.astype(jnp.bfloat16)


def attend_kernel(
    place_ref, lengths_ref, tokens_ref, pool_ref, vec_ref,
    q_ref, k_ref, v_ref, ctx_ref, lse_ref, w_scr,
    sem,
):
    seq = pl.program_id(0)
    rows = tokens_ref.shape[0]

    @pl.when(seq == 0)
    def _():
        load_blocks(pool_ref, place_ref, 0, w_scr, sem)
        wait_whole(w_scr, sem)

    tokens = tokens_ref[...]
    q_ref[...] = ((mm(tokens, w_scr[0:D, :]) + vec_ref[0:1, :]).astype(jnp.bfloat16) * 0.125).astype(jnp.bfloat16)
    k_ref[...] = mm(tokens, w_scr[D : 2 * D, :]).astype(jnp.bfloat16)
    v_ref[...] = (mm(tokens, w_scr[2 * D :, :]) + vec_ref[1:2, :]).astype(jnp.bfloat16)
    key = lax.broadcasted_iota(jnp.int32, (rows, 1), 0)
    bias = jnp.where(key < lengths_ref[seq], 0.0, MASKED)

    def pair(p, _):
        forward_pair(q_ref, k_ref, v_ref, ctx_ref, lse_ref, 0, p, bias)
        return 0

    lax.fori_loop(0, PAIRS, pair, 0)


def attend(place, lengths, tokens, pool, vec):
    seqs, rows, _ = tokens.shape
    flat = tokens.reshape(seqs * rows, D)
    row_spec = pl.BlockSpec((rows, D), lambda s, *_: (s, 0))
    any_spec = pl.BlockSpec(memory_space=pl.ANY)
    low = jax.ShapeDtypeStruct((seqs * rows, D), jnp.bfloat16)
    return pl.pallas_call(
        attend_kernel,
        grid_spec=pltpu.PrefetchScalarGridSpec(
            num_scalar_prefetch=2,
            grid=(seqs,),
            in_specs=[row_spec, any_spec, pl.BlockSpec(vec.shape, lambda s, *_: (0, 0))],
            out_specs=[row_spec] * 4
            + [
                pl.BlockSpec((1, 16, rows), lambda s, *_: (s, 0, 0)),
                pl.BlockSpec((3 * D, D), lambda s, *_: (0, 0)),
            ],
            scratch_shapes=[pltpu.SemaphoreType.DMA],
        ),
        out_shape=[low] * 4
        + [
            jax.ShapeDtypeStruct((seqs, 16, rows), jnp.float32),
            jax.ShapeDtypeStruct((3 * D, D), jnp.bfloat16),
        ],
        compiler_params=pltpu.CompilerParams(vmem_limit_bytes=48 * MIB),
        cost_estimate=pl.CostEstimate(
            flops=6 * seqs * rows * D * D + 4 * seqs * rows * rows * D,
            bytes_accessed=10 * seqs * rows * D + 6 * D * D,
            transcendentals=seqs * rows * rows * H,
        ),
        name="attend",
    )(place, lengths, flat, pool, vec)


def gelu_parts(x):
    z = jnp.abs(x) * 0.7071067811865476
    t_in = 1.0 + 0.3275911 * z
    t = pltpu.reciprocal(t_in, approx=True)
    t = t * (2.0 - t_in * t)
    e = jnp.exp(-0.5 * (x * x))
    poly = 1.061405429 * t - 1.453152027
    poly = poly * t + 1.421413741
    poly = poly * t - 0.284496736
    poly = poly * t + 0.254829592
    tail = (0.5 * t) * poly * e
    dist = jnp.where(x >= 0, 1.0 - tail, tail)
    return dist, x * e * 0.3989422804014327


def norm_stats(resid):
    center = resid - jnp.mean(resid, axis=-1, keepdims=True)
    scale = lax.rsqrt(jnp.mean(center * center, axis=-1, keepdims=True) + 1e-05)
    return center * scale, scale


def norm_back(d_out, gain, hat, scale):
    d_hat = d_out * gain
    mean_one = jnp.mean(d_hat, axis=-1, keepdims=True)
    mean_hat = jnp.mean(d_hat * hat, axis=-1, keepdims=True)
    return scale * (d_hat - mean_one - hat * mean_hat)


def feed_kernel(
    place_ref, lengths_ref, tokens_ref, ctx_ref, cot_ref, pool_ref, vec_ref,
    wide_mid_ref, mid_ref, out_ref, act_ref, dinner_ref, dfeed_ref, dbranch_ref, dres_ref, dctx_ref, grad_ref, sq_ref,
    w_out, w_up, w_down, slope_scr, sem, *, seq_rows,
):
    step = pl.program_id(0)
    rows = tokens_ref.shape[0]
    tiles = sq_ref.shape[0]
    first = 3 * D // BLK

    @pl.when(step == 0)
    def _():
        load_blocks(pool_ref, place_ref, first, w_out, sem.at[0])
        load_blocks(pool_ref, place_ref, first + D // BLK, w_up, sem.at[1])
        load_blocks(pool_ref, place_ref, first + (D + FF) // BLK, w_down, sem.at[2])
        wait_whole(w_out, sem.at[0])
        grad_ref[...] = jnp.zeros_like(grad_ref)

    def add_row(row, value):
        grad_ref[row : row + 1, :] += jnp.sum(value, axis=0, keepdims=True)

    segment = min(rows, seq_rows)
    row = lax.broadcasted_iota(jnp.int32, (rows, 1), 0)
    length = jnp.zeros((rows, 1), jnp.int32)
    for j in range(rows // segment):
        length = jnp.where(row // segment == j, lengths_ref[(step * rows + j * segment) // seq_rows], length)
    place_in = (step * rows + row) % seq_rows
    if seq_rows < SEQLEN:
        place_in += lax.axis_index("seq") * seq_rows
    valid = (place_in < length).astype(jnp.float32)

    def square_sums(which, value):
        square = value * value * valid
        for j in range(rows // segment):
            sq_ref[0, 2 * j + which : 2 * j + which + 1, :] = jnp.sum(
                square[j * segment : (j + 1) * segment], axis=0, keepdims=True
            )

    branch = mm(ctx_ref[...], w_out[...]) + vec_ref[2:3, :]
    square_sums(0, branch)
    hat1, scale1 = norm_stats(tokens_ref[...].astype(jnp.float32) + branch)
    middle = hat1 * vec_ref[4:5, :] + vec_ref[5:6, :]
    wide_mid_ref[...] = middle
    mid_ref[...] = middle.astype(jnp.bfloat16)
    mid_low = mid_ref[...]

    @pl.when(step == 0)
    def _():
        wait_whole(w_up, sem.at[1])
        wait_whole(w_down, sem.at[2])

    feed = jnp.zeros((rows, D), jnp.float32) + vec_ref[3:4, :]
    for c in range(CHUNKS):
        part = slice(c * D, (c + 1) * D)
        inner = mm_nt(mid_low, w_up[part, :]) + vec_ref[8 + c : 9 + c, :]
        dist, bell = gelu_parts(inner)
        act = (inner * dist).astype(jnp.bfloat16)
        act_ref[:, part] = act
        slope_scr[:, part] = dist + bell
        feed += mm(act, w_down[part, :])
    square_sums(1, feed)
    hat2, scale2 = norm_stats(middle + feed)
    gain2 = vec_ref[6:7, :]
    out_ref[...] = (hat2 * gain2 + vec_ref[7:8, :]).astype(jnp.bfloat16)
    upstream = cot_ref[...].astype(jnp.float32) * valid
    add_row(6, upstream * hat2)
    add_row(7, upstream)
    d_res2 = norm_back(upstream, gain2, hat2, scale2)
    d_feed = d_res2.astype(jnp.bfloat16)
    dfeed_ref[...] = d_feed
    add_row(3, d_feed.astype(jnp.float32))
    d_mid = d_res2
    for c in range(CHUNKS):
        part = slice(c * D, (c + 1) * D)
        d_inner = (mm_nt(d_feed, w_down[part, :]) * slope_scr[:, part]).astype(jnp.bfloat16)
        dinner_ref[:, part] = d_inner
        add_row(8 + c, d_inner.astype(jnp.float32))
        d_mid += mm(d_inner, w_up[part, :])
    add_row(4, d_mid * hat1)
    add_row(5, d_mid)
    d_res1 = norm_back(d_mid, vec_ref[4:5, :], hat1, scale1)
    dres_ref[...] = d_res1
    d_branch = d_res1.astype(jnp.bfloat16)
    dbranch_ref[...] = d_branch
    add_row(2, d_branch.astype(jnp.float32))
    dctx_ref[...] = mm_nt(d_branch, w_out[...]).astype(jnp.bfloat16)


def feed_both(place, lengths, seq_rows, tokens, ctx, cot, pool, vec, tile=256):
    total = tokens.shape[0]
    steps = total // tile
    row_spec = pl.BlockSpec((tile, D), lambda s, *_: (s, 0))
    wide_spec = pl.BlockSpec((tile, FF), lambda s, *_: (s, 0))
    any_spec = pl.BlockSpec(memory_space=pl.ANY)
    low = jax.ShapeDtypeStruct((total, D), jnp.bfloat16)
    wide = jax.ShapeDtypeStruct((total, FF), jnp.bfloat16)
    return pl.pallas_call(
        partial(feed_kernel, seq_rows=seq_rows),
        grid_spec=pltpu.PrefetchScalarGridSpec(
            num_scalar_prefetch=2,
            grid=(steps,),
            in_specs=[row_spec] * 3 + [any_spec, pl.BlockSpec(vec.shape, lambda s, *_: (0, 0))],
            out_specs=[row_spec, row_spec, row_spec, wide_spec, wide_spec, row_spec, row_spec, row_spec, row_spec,
                pl.BlockSpec((16, D), lambda s, *_: (0, 0)),
                pl.BlockSpec((1, 8, D), lambda s, *_: (s, 0, 0))],
            scratch_shapes=[
                pltpu.VMEM((D, D), jnp.bfloat16),
                pltpu.VMEM((FF, D), jnp.bfloat16),
                pltpu.VMEM((FF, D), jnp.bfloat16),
                pltpu.VMEM((tile, FF), jnp.float32),
                pltpu.SemaphoreType.DMA((3,)),
            ],
        ),
        out_shape=[jax.ShapeDtypeStruct((total, D), jnp.float32), low, low, wide, wide, low, low, jax.ShapeDtypeStruct((total, D), jnp.float32), low,
            jax.ShapeDtypeStruct((16, D), jnp.float32),
            jax.ShapeDtypeStruct((steps, 8, D), jnp.float32)],
        compiler_params=pltpu.CompilerParams(vmem_limit_bytes=56 * MIB),
        cost_estimate=pl.CostEstimate(
            flops=8 * total * D * FF + 4 * total * D * D,
            bytes_accessed=total * (16 * D + 4 * FF) + 12 * FF * D,
            transcendentals=total * FF,
        ),
        name="feed_both",
    )(place, lengths, tokens, ctx, cot, pool, vec)


def send_blocks(value, held, slot, first, place_ref, out_ref, sem):
    held[slot] = value.astype(jnp.bfloat16).reshape(D // BLK, BLK, D)
    for i in range(D // BLK):
        pltpu.make_async_copy(
            held.at[slot, i], out_ref.at[place_ref[first + i]], sem.at[slot]
        ).start()


def feed_grads_kernel(
    place_ref, ctx_ref, dbranch_ref, dinner_ref, mid_ref, act_ref, dfeed_ref, out_ref, held, sem
):
    step = pl.program_id(0)
    slot = lax.rem(step, 2)
    base = 3 * D // BLK

    @pl.when(step >= 2)
    def _():
        wait_whole(held.at[slot], sem.at[slot])

    first = base + step * (D // BLK)

    @pl.when(step == 0)
    def _():
        send_blocks(mm_tn(ctx_ref[...], dbranch_ref[...]), held, slot, first, place_ref, out_ref, sem)

    @pl.when((step >= 1) & (step <= CHUNKS))
    def _():
        send_blocks(mm_tn(dinner_ref[...], mid_ref[...]), held, slot, first, place_ref, out_ref, sem)

    @pl.when(step > CHUNKS)
    def _():
        send_blocks(mm_tn(act_ref[...], dfeed_ref[...]), held, slot, first, place_ref, out_ref, sem)

    @pl.when(step == 2 * CHUNKS)
    def _():
        wait_whole(held.at[slot], sem.at[slot])
        wait_whole(held.at[1 - slot], sem.at[1 - slot])


def feed_grads(place, places, ctx, d_branch, d_inner, mid, act, d_feed):
    total = ctx.shape[0]
    whole = pl.BlockSpec((total, D), lambda s, *_: (0, 0))
    return pl.pallas_call(
        feed_grads_kernel,
        grid_spec=pltpu.PrefetchScalarGridSpec(
            num_scalar_prefetch=1,
            grid=(1 + 2 * CHUNKS,),
            in_specs=[
                whole,
                whole,
                pl.BlockSpec((total, D), lambda s, *_: (0, jnp.clip(s - 1, 0, CHUNKS - 1))),
                whole,
                pl.BlockSpec((total, D), lambda s, *_: (0, jnp.clip(s - 1 - CHUNKS, 0, CHUNKS - 1))),
                whole,
            ],
            out_specs=pl.BlockSpec(memory_space=pl.ANY),
            scratch_shapes=[
                pltpu.VMEM((2, D // BLK, BLK, D), jnp.bfloat16),
                pltpu.SemaphoreType.DMA((2,)),
            ],
        ),
        out_shape=jax.ShapeDtypeStruct((places, BLK, D), jnp.bfloat16),
        compiler_params=pltpu.CompilerParams(vmem_limit_bytes=48 * MIB),
        cost_estimate=pl.CostEstimate(
            flops=4 * total * D * FF + 2 * total * D * D,
            bytes_accessed=total * (8 * D + 4 * FF) + 4 * FF * D,
            transcendentals=0,
        ),
        name="feed_grads",
    )(place, ctx, d_branch, d_inner, mid, act, d_feed)


def attend_back_kernel(
    place_w_ref, place_ref, lengths_ref, tokens_ref, q_ref, k_ref, v_ref, ctx_ref, dctx_ref, lse_ref, dres_ref, pool_ref, held_in,
    ingrad_ref, vec_ref, out_ref,
    w_scr, dq_scr, dk_scr, dv_scr, total_scr, held, sem, w_sem,
):
    seq = pl.program_id(0)
    last = pl.num_programs(0) - 1
    rows = tokens_ref.shape[0]

    @pl.when(seq == 0)
    def _():
        load_blocks(pool_ref, place_w_ref, 0, w_scr, w_sem)
        vec_ref[...] = jnp.zeros_like(vec_ref)

    key = lax.broadcasted_iota(jnp.int32, (rows, 1), 0)
    bias = jnp.where(key < lengths_ref[seq], 0.0, MASKED)

    def pair(p, _):
        cols, d_query, d_key, d_value = back_pair(q_ref, k_ref, v_ref, ctx_ref, dctx_ref, lse_ref, 0, p, bias)
        dq_scr[:, cols] = d_query
        dk_scr[:, cols] = d_key
        dv_scr[:, cols] = d_value
        return 0

    lax.fori_loop(0, PAIRS, pair, 0)

    @pl.when(seq == 0)
    def _():
        wait_whole(w_scr, w_sem)

    dq, dk, dv = dq_scr[...], dk_scr[...], dv_scr[...]
    vec_ref[0:1, :] += jnp.sum(dq.astype(jnp.float32), axis=0, keepdims=True)
    vec_ref[1:2, :] += jnp.sum(dv.astype(jnp.float32), axis=0, keepdims=True)
    ingrad = dres_ref[...] + mm_nt(dq, w_scr[0:D, :])
    ingrad += mm_nt(dk, w_scr[D : 2 * D, :])
    ingrad += mm_nt(dv, w_scr[2 * D :, :])
    ingrad_ref[...] = ingrad.astype(jnp.bfloat16)
    tokens = tokens_ref[...]
    for i, right in enumerate((dq, dk, dv)):
        part = slice(i * D, (i + 1) * D)

        @pl.when(seq == 0)
        def _():
            total_scr[part, :] = mm_tn(tokens, right)

        @pl.when(seq > 0)
        def _():
            total_scr[part, :] += mm_tn(tokens, right)

    @pl.when(seq == last)
    def _():
        for i in range(3):
            send_blocks(total_scr[i * D : (i + 1) * D, :], held, i, i * (D // BLK), place_ref, out_ref, sem)
        for i in range(3):
            wait_whole(held.at[i], sem.at[i])


def attend_back(place_w, place, lengths, tokens, q, k, v, ctx, d_ctx, lse, d_res, pool, held):
    seqs, rows, _ = tokens.shape
    flat = tokens.reshape(seqs * rows, D)
    row_spec = pl.BlockSpec((rows, D), lambda s, *_: (s, 0))
    any_spec = pl.BlockSpec(memory_space=pl.ANY)
    return pl.pallas_call(
        attend_back_kernel,
        grid_spec=pltpu.PrefetchScalarGridSpec(
            num_scalar_prefetch=3,
            grid=(seqs,),
            in_specs=[row_spec] * 6
            + [pl.BlockSpec((1, 16, rows), lambda s, *_: (s, 0, 0)), row_spec, any_spec, any_spec],
            out_specs=[row_spec, pl.BlockSpec((8, D), lambda s, *_: (0, 0)), any_spec],
            scratch_shapes=[
                pltpu.VMEM((3 * D, D), jnp.bfloat16),
                pltpu.VMEM((rows, D), jnp.bfloat16),
                pltpu.VMEM((rows, D), jnp.bfloat16),
                pltpu.VMEM((rows, D), jnp.bfloat16),
                pltpu.VMEM((3 * D, D), jnp.float32),
                pltpu.VMEM((3, D // BLK, BLK, D), jnp.bfloat16),
                pltpu.SemaphoreType.DMA((3,)),
                pltpu.SemaphoreType.DMA,
            ],
        ),
        out_shape=[
            jax.ShapeDtypeStruct((seqs * rows, D), jnp.bfloat16),
            jax.ShapeDtypeStruct((8, D), jnp.float32),
            jax.ShapeDtypeStruct(held.shape, held.dtype),
        ],
        input_output_aliases={12: 2},
        compiler_params=pltpu.CompilerParams(vmem_limit_bytes=56 * MIB),
        cost_estimate=pl.CostEstimate(
            flops=12 * seqs * rows * D * D + 10 * seqs * rows * rows * D,
            bytes_accessed=20 * seqs * rows * D + 12 * D * D,
            transcendentals=seqs * rows * rows * H,
        ),
        name="attend_back",
    )(place_w, place, lengths, flat, q, k, v, ctx, d_ctx, lse, d_res, pool, held)


def adam_kernel(
    place_ref, has_ref, grad_a, grad_b, moment_ref, second_ref, master_ref,
    dres_ref, part_ref, rms_ref, vec_ref, vec_moment_ref, vec_second_ref, vec_master_ref,
    ingrad_out, rms_out, grad_out, moment_out, second_out, master_out,
    vec_out, vec_moment_out, vec_second_out, vec_master_out,
):
    step = pl.program_id(0)
    for j, grad_in in enumerate((grad_a, grad_b)):
        got = grad_in[0].astype(jnp.float32)
        gradient = jnp.where(has_ref[2 * step + j] > 0, got, jnp.zeros_like(got))
        grad_out[j] = gradient
        moment_out[j], second_out[j], master_out[j] = adam_step(
            gradient, moment_ref[j], second_ref[j], master_ref[j], matrix_rate
        )
    ingrad_out[...] = dres_ref[...] + part_ref[...].astype(jnp.float32)

    @pl.when(step == 0)
    def _():
        rms_out[...] = rms_ref[:, 0:2]
        gradient = vec_ref[0 : vec_out.shape[0], :]
        vec_out[...] = gradient
        vec_moment_out[...], vec_second_out[...], vec_master_out[...] = adam_step(
            gradient, vec_moment_ref[...], vec_second_ref[...], vec_master_ref[...], vector_rate
        )


def adam_all(place, has, reduced, moment, second, master, d_res, part, rms, vec, vec_moment, vec_second, vec_master):
    slots = master.shape[0]
    steps = slots // 2
    total = d_res.shape[0]
    pieces = 1
    while 2 * pieces <= steps:
        pieces *= 2
    pair = pl.BlockSpec((2, BLK, D), lambda s, *_: (s, 0, 0))
    rows = pl.BlockSpec((total // pieces, D), lambda s, *_: (jnp.minimum(s, pieces - 1), 0))

    def whole(shape):
        return pl.BlockSpec(shape, lambda s, *_: (0, 0))

    full = jax.ShapeDtypeStruct(master.shape, jnp.float32)
    vec_full = jax.ShapeDtypeStruct(vec_master.shape, jnp.float32)
    return pl.pallas_call(
        adam_kernel,
        grid_spec=pltpu.PrefetchScalarGridSpec(
            num_scalar_prefetch=2,
            grid=(steps,),
            in_specs=[
                pl.BlockSpec((1, BLK, D), lambda s, place, has: (place[2 * s], 0, 0)),
                pl.BlockSpec((1, BLK, D), lambda s, place, has: (place[2 * s + 1], 0, 0)),
            ]
            + [pair] * 3
            + [rows] * 2
            + [whole(rms.shape), whole(vec.shape)]
            + [whole(vec_master.shape)] * 3,
            out_specs=[rows, whole((rms.shape[0], 2))] + [pair] * 4 + [whole(vec_master.shape)] * 4,
        ),
        out_shape=[
            jax.ShapeDtypeStruct(d_res.shape, jnp.float32),
            jax.ShapeDtypeStruct((rms.shape[0], 2), jnp.float32),
        ]
        + [full] * 4
        + [vec_full] * 4,
        compiler_params=pltpu.CompilerParams(vmem_limit_bytes=60 * MIB),
        cost_estimate=pl.CostEstimate(
            flops=20 * slots * BLK * D, bytes_accessed=30 * slots * BLK * D, transcendentals=2 * slots * BLK * D
        ),
        name="adam_all",
    )(place, has, reduced, reduced, moment, second, master, d_res, part, rms, vec, vec_moment, vec_second, vec_master)


EARLY = 6
MIDDLE = 8
LATE = 10
FIRST = 10
LIST = EARLY + MIDDLE + LATE
HEAD_BLOCKS = 3 * D // BLK
MESH = pl.DeviceIdType.MESH


class Place:
    def __init__(self):
        dp = lax.axis_index("dp")
        self.z = lax.axis_index("seq")
        self.core = dp % 2
        x = (dp // 2) % 2
        y = dp // 4
        self.chip = dp // 2
        self.chip_x = 2 * y + 1 - x
        self.chip_y = 2 * (1 - y) + x
        self.chip_xy = 2 * (1 - y) + 1 - x
        self.to_core = {"dp": dp + 1 - 2 * self.core}
        self.to_x = {"dp": dp + 2 - 4 * x}
        self.to_y = {"dp": dp + 4 - 8 * y}
        z = self.z
        self.z_hops = (z + 1 - 2 * (z % 2), (z + 2) % 4, 3 - z)
        self.to_z = tuple({"seq": hop} for hop in self.z_hops)
        self.partners = (self.to_core, self.to_x, self.to_y) + self.to_z

    def meet(self):
        barrier = pltpu.get_barrier_semaphore()
        for partner in self.partners:
            pl.semaphore_signal(barrier, inc=1, device_id=partner, device_id_type=MESH)
        pl.semaphore_wait(barrier, len(self.partners))


class Sender:
    def __init__(self, send_sem, recv_sem):
        self.send_sem, self.recv_sem = send_sem, recv_sem

    def copy(self, k, src, dst, partner):
        return pltpu.make_async_remote_copy(
            src_ref=src,
            dst_ref=dst,
            send_sem=self.send_sem.at[k],
            recv_sem=self.recv_sem.at[k],
            device_id=partner,
            device_id_type=MESH,
        )


class Gather:
    def __init__(self, here, sender, first_sem, count, own, own_row, pool, row_of):
        self.here, self.sender, self.k, self.n = here, sender, first_sem, count
        self.own, self.own_row, self.pool, self.row_of = own, own_row, pool, row_of
        self.half = count * BLK // 2

    def link(self, name):
        here, half = self.here, self.half

        def own(part):
            return self.own.at[pl.ds(self.own_row + part * half, half)]

        def piece(chip, part):
            return self.pool.at[pl.ds(self.row_of(chip, here.core) + part * half, half)]

        def whole(chip):
            return self.pool.at[pl.ds(self.row_of(chip, here.core), 2 * half)]

        order = ("x0", "x1", "y1", "y0", "y_on", "x_on", "share_x", "share_y", "share_xy")
        src, dst, partner = {
            "x0": lambda: (own(0), piece(here.chip, 0), here.to_x),
            "x1": lambda: (own(1), piece(here.chip, 1), here.to_x),
            "y1": lambda: (own(1), piece(here.chip, 1), here.to_y),
            "y0": lambda: (own(0), piece(here.chip, 0), here.to_y),
            "y_on": lambda: (piece(here.chip_x, 0), piece(here.chip_x, 0), here.to_y),
            "x_on": lambda: (piece(here.chip_y, 1), piece(here.chip_y, 1), here.to_x),
            "share_x": lambda: (whole(here.chip_x), whole(here.chip_x), here.to_core),
            "share_y": lambda: (whole(here.chip_y), whole(here.chip_y), here.to_core),
            "share_xy": lambda: (whole(here.chip_xy), whole(here.chip_xy), here.to_core),
        }[name]()
        return self.sender.copy(self.k + order.index(name), src, dst, partner)

    def start(self):
        for name in ("x0", "y1", "x1", "y0"):
            self.link(name).start()

    def pass_on(self):
        self.link("x0").wait_recv()
        self.link("y_on").start()
        self.link("y1").wait_recv()
        self.link("x_on").start()

    def share_near(self):
        self.link("x1").wait_recv()
        self.link("share_x").start()
        self.link("y0").wait_recv()
        self.link("share_y").start()

    def sent(self):
        for name in ("x0", "y1", "x1", "y0", "y_on", "x_on"):
            self.link(name).wait_send()

    def share_far(self):
        self.link("y_on").wait_recv()
        self.link("x_on").wait_recv()
        self.link("share_xy").start()

    def finish(self):
        for name in ("share_x", "share_y", "share_xy"):
            self.link(name).wait_recv()

    def shared(self):
        for name in ("share_x", "share_y", "share_xy"):
            self.link(name).wait_send()


def front_kernel(
    place_ref, mine_ref, lengths_ref, vec_ref, master_in, tokens_in,
    pool, q_out, k_out, v_out, ctx_out, w_out, tok_out, ctx_split, lse_ref,
    stage, both, near, pack, w, tok, qs, ks, vs, cs,
    send_sem, recv_sem, load_sem,
):
    here = Place()
    z = here.z
    sender = Sender(send_sem, recv_sem)
    rows = SEQLEN
    own = tokens_in.shape[0] // 4
    part = tokens_in.shape[1]
    slots = master_in.shape[0]
    groups = 3
    group = slots // groups
    second = LIST - FIRST

    def local(src, dst, k):
        return pltpu.make_async_copy(src, dst, load_sem.at[k])

    loads = [
        local(master_in.at[pl.ds(g * group, group)], stage.at[pl.ds(g * group, group)], g) for g in range(groups)
    ]
    for load in loads:
        load.start()
    own_tokens = [
        local(tokens_in.at[own * z + s], tok.at[pl.ds(s * rows + part * z, part)], 3 + s) for s in range(own)
    ]
    for load in own_tokens:
        load.start()
    here.meet()
    swaps = [
        sender.copy(
            own * hop + s,
            tokens_in.at[own * here.z_hops[hop] + s],
            tok.at[pl.ds(s * rows + part * z, part)],
            here.to_z[hop],
        )
        for hop in range(3)
        for s in range(own)
    ]
    for swap in swaps:
        swap.start()
    trades = [
        sender.copy(
            6 + g,
            both.at[pl.ds(here.core * slots + g * group, group)],
            both.at[pl.ds(here.core * slots + g * group, group)],
            here.to_core,
        )
        for g in range(groups)
    ]
    for g in range(groups):
        loads[g].wait()

        def convert(i, _):
            both[here.core * slots + g * group + i] = stage[g * group + i].astype(jnp.bfloat16)
            return 0

        lax.fori_loop(0, group, convert, 0)
        trades[g].start()
    for trade in trades:
        trade.wait_recv()

    def fill_near(p, _):
        near[pl.ds((here.chip * FIRST + p) * BLK, BLK), :] = both[mine_ref[p]]
        return 0

    lax.fori_loop(0, FIRST, fill_near, 0)
    first = Gather(
        here, sender, 9, FIRST // 2, near, (here.chip * FIRST + here.core * (FIRST // 2)) * BLK, near,
        lambda chip, core: (chip * FIRST + core * (FIRST // 2)) * BLK,
    )
    then = Gather(
        here, sender, 18, second // 2, pack, here.core * (second // 2) * BLK, pool,
        lambda chip, core: (chip * LIST + FIRST + core * (second // 2)) * BLK,
    )
    first.start()

    def fill_pack(p, _):
        pack[pl.ds(p * BLK, BLK), :] = both[mine_ref[FIRST + p]]
        return 0

    lax.fori_loop(0, second, fill_pack, 0)
    own_second = local(pack, pool.at[pl.ds((here.chip * LIST + FIRST) * BLK, second * BLK)], 5)
    own_second.start()
    first.pass_on()
    first.share_near()
    first.sent()
    then.start()
    first.share_far()
    first.finish()

    def fill_w(b, _):
        at = place_ref[b]
        w[pl.ds(b * BLK, BLK), :] = near[pl.ds(((at // LIST) * FIRST + at % LIST) * BLK, BLK), :]
        return 0

    lax.fori_loop(0, HEAD_BLOCKS, fill_w, 0)
    keeps = [
        local(near.at[pl.ds(chip * FIRST * BLK, FIRST * BLK)], pool.at[pl.ds(chip * LIST * BLK, FIRST * BLK)], 6 + chip)
        for chip in range(4)
    ] + [local(w, w_out, 10)]
    for keep in keeps:
        keep.start()
    for load in own_tokens:
        load.wait()
    for swap in swaps:
        swap.wait_recv()
    keep_tok = local(tok, tok_out, 11)
    keep_tok.start()

    def send_ctx(s, hop):
        return sender.copy(
            27 + 3 * s + hop,
            cs.at[pl.ds(s * rows + part * here.z_hops[hop], part)],
            ctx_split.at[own * z + s],
            here.to_z[hop],
        )

    def keep_own(s):
        at = pl.ds(s * rows, rows)
        return [local(ref.at[at], out.at[at], 12 + k) for k, (ref, out) in enumerate(((qs, q_out), (ks, k_out), (vs, v_out), (cs, ctx_out)))] + [
            local(cs.at[pl.ds(s * rows + part * z, part)], ctx_split.at[own * z + s], 16)
        ]

    key = lax.broadcasted_iota(jnp.int32, (rows, 1), 0)

    def sequence(s, _):
        at = pl.ds(pl.multiple_of(s * rows, rows), rows)
        values = tok[at, :]
        qs[at, :] = ((mm(values, w[0:D, :]) + vec_ref[0:1, :]).astype(jnp.bfloat16) * 0.125).astype(jnp.bfloat16)
        ks[at, :] = mm(values, w[D : 2 * D, :]).astype(jnp.bfloat16)
        vs[at, :] = (mm(values, w[2 * D :, :]) + vec_ref[1:2, :]).astype(jnp.bfloat16)
        bias = jnp.where(key < lengths_ref[own * z + s], 0.0, MASKED)

        def pair(p, _):
            forward_pair(qs.at[at], ks.at[at], vs.at[at], cs.at[at], lse_ref, s, p, bias)
            return 0

        lax.fori_loop(0, PAIRS, pair, 0)
        for hop in range(3):
            send_ctx(s, hop).start()

        @pl.when(s > 0)
        def _():
            for keep in keep_own(s - 1):
                keep.wait()

        for keep in keep_own(s):
            keep.start()

        @pl.when(s == 0)
        def _():
            then.pass_on()

        return 0

    lax.fori_loop(0, own, sequence, 0)
    then.share_near()
    then.share_far()
    then.sent()
    then.finish()
    for keep in keep_own(own - 1) + keeps + [keep_tok, own_second]:
        keep.wait()
    for s in range(own):
        for hop in range(3):
            send_ctx(s, hop).wait_recv()
            send_ctx(s, hop).wait_send()
    for copy in swaps + trades:
        copy.wait_send()
    first.shared()
    then.shared()


def front(place, mine, lengths, vec, master, tokens):
    seqs, part, _ = tokens.shape
    total = seqs * part
    own = total // SEQLEN
    any_spec = pl.BlockSpec(memory_space=pl.ANY)
    vmem = pl.BlockSpec(memory_space=pltpu.VMEM)
    smem = pl.BlockSpec(memory_space=pltpu.SMEM)
    low = jnp.bfloat16
    slots = master.shape[0]
    flat = jax.ShapeDtypeStruct((total, D), low)
    return pl.pallas_call(
        front_kernel,
        in_specs=[smem] * 3 + [vmem] + [any_spec] * 2,
        out_specs=[any_spec] * 8 + [vmem],
        out_shape=[
            jax.ShapeDtypeStruct((4 * LIST * BLK, D), low),
            flat,
            flat,
            flat,
            flat,
            jax.ShapeDtypeStruct((3 * D, D), low),
            flat,
            jax.ShapeDtypeStruct(tokens.shape, low),
            jax.ShapeDtypeStruct((own, 16, SEQLEN), jnp.float32),
        ],
        scratch_shapes=[
            pltpu.VMEM(master.shape, jnp.float32),
            pltpu.VMEM((2 * slots, BLK, D), low),
            pltpu.VMEM((4 * FIRST * BLK, D), low),
            pltpu.VMEM(((LIST - FIRST) * BLK, D), low),
            pltpu.VMEM((3 * D, D), low),
        ]
        + [pltpu.VMEM((total, D), low)] * 5
        + [
            pltpu.SemaphoreType.DMA((33,)),
            pltpu.SemaphoreType.DMA((33,)),
            pltpu.SemaphoreType.DMA((17,)),
        ],
        compiler_params=pltpu.CompilerParams(
            vmem_limit_bytes=60 * MIB, collective_id=2, has_side_effects=True
        ),
        cost_estimate=pl.CostEstimate(
            flops=6 * total * D * D + 4 * total * SEQLEN * D,
            bytes_accessed=40 * total * D + 8 * slots * BLK * D,
            transcendentals=total * SEQLEN * H,
        ),
        name="front",
    )(place, mine, lengths, vec, master, tokens)


def add_rows(out_ref, out_row, terms, count, step=64):
    def body(i, _):
        value = None
        for ref, row in terms:
            part = ref[pl.ds(row + i * step, step), :].astype(jnp.float32)
            value = part if value is None else value + part
        out_ref[pl.ds(out_row + i * step, step), :] = value.astype(jnp.bfloat16)
        return 0

    lax.fori_loop(0, count // step, body, 0)


class Reduce:
    def __init__(self, here, sender, first_sem, count, first, column, blk_ref, grad, pack, buffers, red):
        self.here, self.sender, self.k = here, sender, first_sem
        self.n, self.first, self.blk, self.grad = count, first, blk_ref, grad
        self.acc, self.rx, self.ry, self.r2, self.z1, self.z2, self.fin = buffers
        self.red = red
        self.half = count * BLK // 2
        self.size = count * BLK
        self.cols = pl.ds(column, self.fin.shape[1])
        self.pack = pack.at[pl.ds(0, 4 * self.size), self.cols]

    def rows(self, ref, chip, half):
        return ref.at[pl.ds(chip * self.size + half * self.half, self.half)]

    def link(self, name):
        here, k, acc = self.here, self.k, self.acc
        keep = (here.z % 2) * self.half
        other = (1 - here.z % 2) * self.half
        mine = here.chip * self.size
        fin_keep = self.fin.at[pl.ds(keep, self.half)]
        order = ("core", "x_far", "x_near", "y_far", "y_near", "y_on", "x_on", "z_half", "z_far", "z_back", "share")
        src, dst, partner = {
            "core": lambda: (self.pack, acc, here.to_core),
            "x_far": lambda: (self.rows(acc, here.chip_xy, 0), self.rx.at[1], here.to_x),
            "x_near": lambda: (self.rows(acc, here.chip_x, 0), self.rx.at[0], here.to_x),
            "y_far": lambda: (self.rows(acc, here.chip_xy, 1), self.ry.at[1], here.to_y),
            "y_near": lambda: (self.rows(acc, here.chip_y, 1), self.ry.at[0], here.to_y),
            "y_on": lambda: (self.rows(acc, here.chip_y, 0), self.r2.at[0], here.to_y),
            "x_on": lambda: (self.rows(acc, here.chip_x, 1), self.r2.at[1], here.to_x),
            "z_half": lambda: (acc.at[pl.ds(mine + other, self.half)], self.z1, here.to_z[0]),
            "z_far": lambda: (acc.at[pl.ds(mine + keep, self.half)], self.z2, here.to_z[1]),
            "z_back": lambda: (fin_keep, fin_keep, here.to_z[0]),
            "share": lambda: (self.fin, self.result(), here.to_core),
        }[name]()
        return self.sender.copy(k + order.index(name), src, dst, partner)

    def result(self):
        return self.red.at[pl.ds((self.first + self.here.core * self.n) * BLK, self.size), self.cols]

    def start_core(self):
        here, n = self.here, self.n

        def body(t, _):
            entry = (t // n) * LIST + self.first + (1 - here.core) * n + t % n
            self.pack[pl.ds(t * BLK, BLK), :] = self.grad[self.blk[entry], :, self.cols]
            return 0

        lax.fori_loop(0, 4 * n, body, 0)
        self.link("core").start()

    def add_own(self, chip):
        here, n = self.here, self.n

        def body(i, _):
            entry = chip * LIST + self.first + here.core * n + i
            rows = pl.ds(chip * self.size + i * BLK, BLK)
            mine = self.grad[self.blk[entry], :, self.cols].astype(jnp.float32)
            self.acc[rows, :] = (self.acc[rows, :].astype(jnp.float32) + mine).astype(jnp.bfloat16)
            return 0

        lax.fori_loop(0, n, body, 0)

    def start_plane(self):
        here = self.here
        self.link("core").wait_recv()
        self.add_own(here.chip_xy)
        self.link("x_far").start()
        self.link("y_far").start()
        self.add_own(here.chip_x)
        self.add_own(here.chip_y)
        self.link("x_near").start()
        self.link("y_near").start()
        self.add_own(here.chip)

    def pass_plane(self):
        here = self.here
        self.link("x_far").wait_recv()
        at = here.chip_y * self.size
        add_rows(self.acc, at, ((self.acc, at), (self.rx.at[1], 0)), self.half)
        self.link("y_on").start()
        self.link("y_far").wait_recv()
        at = here.chip_x * self.size + self.half
        add_rows(self.acc, at, ((self.acc, at), (self.ry.at[1], 0)), self.half)
        self.link("x_on").start()

    def start_z(self):
        here = self.here
        mine = here.chip * self.size
        self.link("x_near").wait_recv()
        self.link("y_on").wait_recv()
        add_rows(self.acc, mine, ((self.acc, mine), (self.rx.at[0], 0), (self.r2.at[0], 0)), self.half)
        self.link("y_near").wait_recv()
        self.link("x_on").wait_recv()
        low = mine + self.half
        add_rows(self.acc, low, ((self.acc, low), (self.ry.at[0], 0), (self.r2.at[1], 0)), self.half)
        self.link("z_half").start()

    def far_z(self):
        here = self.here
        keep = here.chip * self.size + (here.z % 2) * self.half
        self.link("z_half").wait_recv()
        add_rows(self.acc, keep, ((self.acc, keep), (self.z1, 0)), self.half)
        self.link("z_far").start()

    def back_z(self):
        here = self.here
        keep = (here.z % 2) * self.half
        self.link("z_far").wait_recv()
        add_rows(self.fin, keep, ((self.acc, here.chip * self.size + keep), (self.z2, 0)), self.half)
        self.link("z_back").start()

    def share(self, local_sem):
        red = self.result()
        self.link("z_back").wait_recv()
        self.link("z_back").wait_send()
        self.link("share").start()
        pltpu.make_async_copy(self.fin, red, local_sem).start()

    def finish(self, local_sem):
        red = self.result()
        self.link("share").wait_recv()
        pltpu.make_async_copy(self.fin, red, local_sem).wait()
        for name in ("core", "x_far", "x_near", "y_far", "y_near", "y_on", "x_on", "z_half", "z_far", "share"):
            if name != "core" or self.first >= EARLY + MIDDLE:
                self.link(name).wait_send()


def back_pair(q_ref, k_ref, v_ref, ctx_ref, do_ref, lse_ref, seq, p, bias):
    rows = q_ref.shape[0]
    cols = pl.ds(pl.multiple_of(p * LANES, LANES), LANES)
    row8 = lax.broadcasted_iota(jnp.int32, (16, rows), 0)

    def extra_rows(lead, row):
        one, two, three = (part.astype(jnp.float32) for part in split3(row))
        return jnp.where(
            row8 == 0, lead, jnp.where(row8 == 1, one, jnp.where(row8 == 2, two, jnp.where(row8 == 3, three, 0.0)))
        )

    q2, k2, v2, do2 = q_ref[:, cols], k_ref[:, cols], v_ref[:, cols], do_ref[:, cols]
    q2t, k2t, do2t = q2.T, k2.T, do2.T
    prod = do2t.astype(jnp.float32) * ctx_ref[:, cols].T.astype(jnp.float32)
    dq_parts = []
    d_key = jnp.zeros((rows, LANES), jnp.float32)
    d_value = jnp.zeros((rows, LANES), jnp.float32)
    for half in range(2):
        head = slice(half * DH, half * DH + DH)
        inside, spare = spare_lanes(rows, half, bias)
        zero = jnp.zeros_like(k2)
        lse = lse_ref[seq, pl.ds(2 * p + half, 1), :]
        delta = jnp.sum(prod[head], axis=0, keepdims=True)
        scores = mm(jnp.where(inside, k2, spare), beside(q2t[head], extra_rows(1.0, -lse), half))
        probs = jnp.exp(scores)
        d_probs = mm(jnp.where(inside, v2, spare), beside(do2t[head], extra_rows(0.0, -delta), half))
        d_scores = (probs * d_probs).astype(jnp.bfloat16)
        d_value += mm(probs.astype(jnp.bfloat16), jnp.where(inside, do2, zero))
        d_key += mm(d_scores, jnp.where(inside, q2, zero))
        dq_parts.append(mm(k2t[head], d_scores))
    d_query = jnp.concatenate(dq_parts, axis=0).T * 0.125
    return cols, d_query.astype(jnp.bfloat16), d_key.astype(jnp.bfloat16), d_value.astype(jnp.bfloat16)


def tail_kernel(
    blk_ref, lengths_ref, vec_in, squares_in, lse_ref,
    dctx_in, ctx_split, dbranch, dinner, mid, act, dfeed, tok_in, q_in, k_in, v_in, ctx_in, w_in,
    red, ingrad, vec_out, rms_out,
    grad, pack, d3, att, tok, w, *rest,
):
    here = Place()
    z = here.z
    phase_buffers = [rest[7 * i : 7 * i + 7] for i in range(4)]
    vec_src, vec_land, rms_src, rms_land, send_sem, recv_sem, load_sem = rest[28:]
    sender = Sender(send_sem, recv_sem)
    rows = SEQLEN
    own = dctx_in.shape[0] // 4
    part = dctx_in.shape[1]
    total = own * rows
    wide = D // 2

    def local(src, dst, k):
        return pltpu.make_async_copy(src, dst, load_sem.at[k])

    first_loads = (
        local(ctx_split, att.at[2], 0),
        local(dinner.at[:, pl.ds(0, D)], att.at[3], 1),
        local(dbranch, d3.at[0], 2),
        local(mid, d3.at[1], 3),
        local(dfeed, d3.at[2], 4),
        local(q_in, att.at[0], 5),
        local(k_in, att.at[1], 6),
        local(tok_in, tok, 7),
        local(w_in, w, 10),
    )
    for load in first_loads:
        load.start()
    here.meet()

    def swap(half, s, hop):
        cols = pl.ds(half * wide, wide)
        return sender.copy(
            6 * half + 3 * s + hop,
            dctx_in.at[own * here.z_hops[hop] + s, :, cols],
            att.at[4, pl.ds(s * rows + part * z, part), cols],
            here.to_z[hop],
        )

    swaps = [[swap(half, s, hop) for s in range(own) for hop in range(3)] for half in range(2)]
    own_swaps = [local(dctx_in.at[own * z + s], att.at[4, pl.ds(s * rows + part * z, part)], 8 + s) for s in range(own)]
    for copy in swaps[0] + own_swaps:
        copy.start()
    for load in first_loads[2:5]:
        load.wait()

    early, middle = (
        Reduce(here, sender, 24 + 11 * i, count // 2, first, 0, blk_ref, grad, pack, phase_buffers[i], red)
        for i, (count, first) in enumerate(((EARLY, 0), (MIDDLE, EARLY)))
    )
    late = [
        Reduce(here, sender, 46 + 11 * i, LATE // 2, EARLY + MIDDLE, i * wide, blk_ref, grad, pack, phase_buffers[2 + i], red)
        for i in range(2)
    ]

    def grads(step, _):
        slot = 2 + step % 2
        held = att.at[slot]
        pltpu.make_async_copy(held, held, load_sem.at[step % 2]).wait()
        value = mm_tn(att[slot], d3[(step + 3) // 4])
        grad[pl.ds(HEAD_BLOCKS + step * (D // BLK), D // BLK)] = value.astype(jnp.bfloat16).reshape(D // BLK, BLK, D)

        @pl.when(step < CHUNKS - 1)
        def _():
            local(dinner.at[:, pl.ds((step + 1) * D, D)], held, step % 2).start()

        @pl.when((step >= CHUNKS - 1) & (step < 2 * CHUNKS - 1))
        def _():
            local(act.at[:, pl.ds((step - CHUNKS + 1) * D, D)], held, step % 2).start()

        @pl.when(step == CHUNKS)
        def _():
            early.start_core()

        @pl.when(step == CHUNKS + 2)
        def _():
            early.start_plane()

        @pl.when(step == CHUNKS + 3)
        def _():
            for copy in swaps[0]:
                copy.wait_send()
            for copy in swaps[1]:
                copy.start()

        return 0

    grad[0:HEAD_BLOCKS] = jnp.zeros((HEAD_BLOCKS, BLK, D), jnp.bfloat16)
    lax.fori_loop(0, 1 + 2 * CHUNKS, grads, 0)
    more_loads = (local(v_in, att.at[2], 0), local(ctx_in, att.at[3], 1))
    for load in more_loads:
        load.start()
    early.link("core").wait_send()
    middle.start_core()
    for load in first_loads[5:] + tuple(own_swaps) + more_loads:
        load.wait()
    for copy in swaps[0]:
        copy.wait_recv()

    key = lax.broadcasted_iota(jnp.int32, (rows, 1), 0)

    def head_grads(half):
        cols = pl.ds(half * wide, wide)
        for block, which in ((0, 1), (6, 2), (12, 0)):
            value = mm_tn(tok[...], d3[which, :, cols]).astype(jnp.bfloat16)
            grad[block : block + 6, :, cols] = value.reshape(D // BLK, BLK, wide)

    def send_ingrad(s, hop):
        return sender.copy(
            68 + 3 * s + hop,
            att.at[0, pl.ds(s * rows + part * here.z_hops[hop], part)],
            ingrad.at[own * z + s],
            here.to_z[hop],
        )

    def own_ingrad(s):
        return local(att.at[0, pl.ds(s * rows + part * z, part)], ingrad.at[own * z + s], 11 + s)

    def input_gradient(s):
        at = pl.ds(s * rows, rows)
        value = mm_nt(d3[1, at, :], w[0:D, :])
        value += mm_nt(d3[2, at, :], w[D : 2 * D, :])
        value += mm_nt(d3[0, at, :], w[2 * D :, :])
        att[0, at, :] = value.astype(jnp.bfloat16)
        for hop in range(3):
            send_ingrad(s, hop).start()
        own_ingrad(s).start()

    group = PAIRS // 2

    def pair_step(i, _):
        s = (i // group) % own
        p = (i // (own * group)) * group + i % group
        bias = jnp.where(key < lengths_ref[own * z + s], 0.0, MASKED)
        at = pl.ds(pl.multiple_of(s * rows, rows), rows)
        cols, d_query, d_key, d_value = back_pair(*(att.at[k, at] for k in range(5)), lse_ref, s, p, bias)
        d3[1, at, cols] = d_query
        d3[2, at, cols] = d_key
        d3[0, at, cols] = d_value

        @pl.when(i == 0)
        def _():
            early.pass_plane()

        @pl.when(i == 2)
        def _():
            middle.start_plane()

        @pl.when(i == 4)
        def _():
            early.start_z()

        @pl.when(i == 5)
        def _():
            head_grads(0)
            middle.link("core").wait_send()
            late[0].start_core()
            for copy in swaps[1]:
                copy.wait_recv()

        @pl.when(i == 6)
        def _():
            middle.pass_plane()
            early.far_z()

        @pl.when(i == 8)
        def _():
            late[0].start_plane()
            input_gradient(0)

        @pl.when(i == 11)
        def _():
            middle.start_z()
            early.back_z()

        return 0

    lax.fori_loop(0, own * PAIRS, pair_step, 0)

    head_grads(1)
    late[1].start_core()
    vec_src[0] = vec_in[...]
    vec_src[0, 0:1, :] = jnp.sum(d3[1].astype(jnp.float32), axis=0, keepdims=True)
    vec_src[0, 1:2, :] = jnp.sum(d3[0].astype(jnp.float32), axis=0, keepdims=True)
    for i in range(squares_in.shape[0]):
        sums = jnp.sum(squares_in[i], axis=-1, keepdims=True)
        rms_src[0, 8 * i : 8 * i + 8, :] = jnp.broadcast_to(sums, (8, LANES))
    ways = (here.to_z[0], here.to_z[1], here.to_core, here.to_x, here.to_y)
    vec_copies = [sender.copy(12 + w, vec_src.at[w], vec_land.at[w], way) for w, way in enumerate(ways)]
    rms_copies = [sender.copy(17 + w, rms_src.at[w], rms_land.at[w], ways[w]) for w in range(2)]

    def vec_step(w):
        if w > 0:
            vec_copies[w - 1].wait_recv()
            after = vec_src[w - 1] + vec_land[w - 1]
            if w < len(ways):
                vec_src[w] = after
            else:
                vec_out[...] = after
        if w < len(ways):
            vec_copies[w].start()
        if 0 < w <= 2:
            rms_copies[w - 1].wait_recv()
            after = rms_src[w - 1] + rms_land[w - 1]
            if w < 2:
                rms_src[w] = after
            else:
                lane = lax.broadcasted_iota(jnp.int32, (1, LANES), 1)
                tiles = squares_in.shape[0]
                each = dctx_in.shape[0] // tiles
                for n in range(dctx_in.shape[0]):
                    row = 8 * (n // each) + 2 * (n % each)
                    sums = jnp.where(lane == 0, after[row : row + 1], after[row + 1 : row + 2])
                    rms_out[n : n + 1, :] = jnp.sqrt(sums / (lengths_ref[n].astype(jnp.float32) * D))
        if w < 2:
            rms_copies[w].start()

    late[0].pass_plane()
    vec_step(0)
    late[1].start_plane()
    middle.far_z()
    input_gradient(1)
    vec_step(1)
    late[1].pass_plane()
    late[0].start_z()
    early.share(load_sem.at[13])
    vec_step(2)
    late[0].far_z()
    late[1].start_z()
    vec_step(3)
    late[1].far_z()
    middle.back_z()
    late[0].back_z()
    vec_step(4)
    middle.share(load_sem.at[14])
    late[0].share(load_sem.at[15])
    vec_step(5)
    late[1].back_z()
    late[1].share(load_sem.at[16])
    for i, phase in enumerate((early, middle, late[0], late[1])):
        phase.finish(load_sem.at[13 + i])
    for copy in swaps[1] + vec_copies + rms_copies:
        copy.wait_send()
    for s in range(own):
        own_ingrad(s).wait()
        for hop in range(3):
            send_ingrad(s, hop).wait_recv()
            send_ingrad(s, hop).wait_send()


def tail(blk, lengths, vec, squares, lse, d_ctx, ctx_split, d_branch, d_inner, mid, act, d_feed, tokens, q, k, v, ctx, w):
    total = tokens.shape[0]
    any_spec = pl.BlockSpec(memory_space=pl.ANY)
    vmem = pl.BlockSpec(memory_space=pltpu.VMEM)
    smem = pl.BlockSpec(memory_space=pltpu.SMEM)
    low = jnp.bfloat16
    sums = (8 * squares.shape[0], LANES)

    def phase(n, width):
        half = n * BLK // 2
        return [
            pltpu.VMEM((4 * n * BLK, width), low),
            pltpu.VMEM((2, half, width), low),
            pltpu.VMEM((2, half, width), low),
            pltpu.VMEM((2, half, width), low),
            pltpu.VMEM((half, width), low),
            pltpu.VMEM((half, width), low),
            pltpu.VMEM((n * BLK, width), low),
        ]

    return pl.pallas_call(
        tail_kernel,
        in_specs=[smem] * 2 + [vmem] * 3 + [any_spec] * 13,
        out_specs=[any_spec] * 2 + [vmem] * 2,
        out_shape=[
            jax.ShapeDtypeStruct((LIST * BLK, D), low),
            jax.ShapeDtypeStruct(d_ctx.shape, low),
            jax.ShapeDtypeStruct(vec.shape, jnp.float32),
            jax.ShapeDtypeStruct((d_ctx.shape[0], LANES), jnp.float32),
        ],
        scratch_shapes=[
            pltpu.VMEM((HEAD_BLOCKS + (D + 2 * FF) // BLK, BLK, D), low),
            pltpu.VMEM((2 * max(EARLY, MIDDLE, LATE) * BLK, D), low),
            pltpu.VMEM((3, total, D), low),
            pltpu.VMEM((5, total, D), low),
            pltpu.VMEM((total, D), low),
            pltpu.VMEM((3 * D, D), low),
        ]
        + phase(EARLY // 2, D)
        + phase(MIDDLE // 2, D)
        + phase(LATE // 2, D // 2)
        + phase(LATE // 2, D // 2)
        + [
            pltpu.VMEM((5,) + vec.shape, jnp.float32),
            pltpu.VMEM((5,) + vec.shape, jnp.float32),
            pltpu.VMEM((2,) + sums, jnp.float32),
            pltpu.VMEM((2,) + sums, jnp.float32),
            pltpu.SemaphoreType.DMA((74,)),
            pltpu.SemaphoreType.DMA((74,)),
            pltpu.SemaphoreType.DMA((17,)),
        ],
        compiler_params=pltpu.CompilerParams(
            vmem_limit_bytes=63 * MIB, collective_id=1, has_side_effects=True
        ),
        cost_estimate=pl.CostEstimate(
            flops=2 * total * D * (6 * D + 2 * FF) + 10 * total * SEQLEN * D,
            bytes_accessed=total * (24 * D + 4 * FF) + 8 * FF * D,
            transcendentals=total * SEQLEN * H,
        ),
        name="tail",
    )(blk, lengths, vec, squares, lse, d_ctx, ctx_split, d_branch, d_inner, mid, act, d_feed, tokens, q, k, v, ctx, w)


def tables_kernel(owner_ref, place_ref, mine_ref, block_ref, spot_ref, has_ref, fits_ref, *, slots):
    dp = lax.axis_index("dp")
    chip_slots = 2 * slots
    near_blocks = HEAD_BLOCKS + (D + FF) // BLK
    for ref in (mine_ref, block_ref, spot_ref, has_ref):
        for i in range(ref.shape[0]):
            ref[i] = 0

    def body(b, counts):
        listed, early, middle, late, bad = counts
        slot = owner_ref[b]
        chip = slot // chip_slots
        shift = 8 * chip
        one = jnp.left_shift(1, shift)

        def count(packed):
            return jnp.right_shift(packed, shift) & 255

        order = count(listed)
        n_early, n_middle, n_late = count(early), count(middle), count(late)
        body_block = b >= HEAD_BLOCKS
        in_early = body_block & (b < near_blocks) & (n_early < EARLY)
        in_middle = body_block & jnp.logical_not(in_early) & (n_middle < MIDDLE)
        in_late = jnp.logical_not(in_early | in_middle)
        spot = jnp.where(in_early, n_early, jnp.where(in_middle, EARLY + n_middle, EARLY + MIDDLE + n_late))
        wrong = (order >= LIST) | (spot >= LIST) | (jnp.logical_not(body_block) & (order >= FIRST))
        spot = jnp.minimum(spot, LIST - 1)
        place_ref[b] = chip * LIST + jnp.minimum(order, LIST - 1)
        block_ref[chip * LIST + spot] = b

        @pl.when(chip == dp // 2)
        def _():
            mine_ref[jnp.minimum(order, LIST - 1)] = slot - chip * chip_slots

            @pl.when(slot // slots == dp)
            def _():
                spot_ref[slot % slots] = spot
                has_ref[slot % slots] = 1

        return (
            listed + one,
            early + jnp.where(in_early, one, 0),
            middle + jnp.where(in_middle, one, 0),
            late + jnp.where(in_late, one, 0),
            bad | wrong.astype(jnp.int32),
        )

    zero = jnp.int32(0)
    counts = lax.fori_loop(0, owner_ref.shape[0], body, (zero,) * 5, unroll=4)
    fits_ref[0] = 1 - counts[4]


def tables(owner, slots):
    chips = lax.axis_size("dp") // 2
    smem = pl.BlockSpec(memory_space=pltpu.SMEM)
    sizes = (owner.shape[0], LIST, chips * LIST, slots, slots, 1)
    return pl.pallas_call(
        partial(tables_kernel, slots=slots),
        in_specs=[smem],
        out_specs=[smem] * len(sizes),
        out_shape=[jax.ShapeDtypeStruct((n,), jnp.int32) for n in sizes],
        name="tables",
    )(owner)


def general(tokens, cotangent, lengths, owner, master, vec_master):
    slot_local = master.shape[0]
    gathered = lax.all_gather(master.astype(jnp.bfloat16), "dp", axis=0, tiled=True)
    seq_place = lax.axis_index("seq")
    slot_total = slot_local * lax.axis_size("dp")
    tokens = to_whole(tokens, "seq")
    cotangent = to_whole(cotangent, "seq")
    seq_count, seq_len, width = tokens.shape
    token_count = seq_count * seq_len
    lengths = lax.dynamic_slice_in_dim(lengths, seq_place * seq_count, seq_count)
    q, k, v, ctx, lse, _ = attend(owner, lengths, tokens, gathered, vec_master)
    flat = tokens.reshape(token_count, D)
    _, mid, out, act, d_inner, d_feed, d_branch, d_res, d_ctx, vec_feed, squares = feed_both(
        owner, lengths, seq_len,
        flat, ctx, cotangent.reshape(token_count, D), gathered, vec_master,
    )
    held = feed_grads(owner, slot_total, ctx, d_branch, d_inner, mid, act, d_feed)
    ingrad, vec_attend, held = attend_back(
        owner, owner, lengths, tokens, q, k, v, ctx, d_ctx, lse, d_res, gathered, held
    )
    local_sums = jnp.sum(squares.reshape(seq_count, -1, 8, D)[:, :, :2], axis=(1, 3))
    own_rms = jnp.sqrt(local_sums / (lengths[:, None].astype(jnp.float32) * D))
    sublayer_rms = lax.all_gather(own_rms, "seq", axis=0, tiled=True)
    vec_local = jnp.concatenate([vec_attend[:2], vec_feed[2:12]], axis=0)
    vec_grad = lax.psum(vec_local, ("dp", "seq"))
    owned = lax.psum_scatter(held, "dp", scatter_dimension=0, tiled=True)
    reduced = lax.psum(owned, "seq")
    first_slot = lax.axis_index("dp") * slot_local
    slots = jnp.arange(slot_local, dtype=jnp.int32)
    has = jnp.any((first_slot + slots)[:, None] == owner[None, :], axis=1).astype(jnp.int32)
    whole = (seq_count, seq_len, D)
    return (
        to_split(out.reshape(whole), "seq"),
        jnp.zeros((token_count, D), jnp.float32),
        to_split(ingrad.reshape(whole), "seq").reshape(token_count, D),
        to_split(mid.reshape(whole), "seq").astype(jnp.float32),
        jnp.pad(sublayer_rms, ((0, 0), (0, LANES - 2))),
        jnp.pad(vec_grad, ((0, 4), (0, 0))),
        reduced,
        slots,
        has,
    )


def listed(tokens, cotangent, lengths, owner, master, vec_master, place, mine, block, spot, has):
    seqs, part, _ = tokens.shape
    total = seqs * part
    pool, q, k, v, ctx, w, whole, ctx_split, lse = front(
        place, mine, lengths, vec_master, master, tokens
    )
    ctx_split = ctx_split.reshape(total, D)
    wide_mid, mid, out, act, d_inner, d_feed, d_branch, d_res, d_ctx, vec_feed, squares = feed_both(
        place, lengths, part,
        tokens.reshape(total, D), ctx_split, cotangent.reshape(total, D), pool.reshape(-1, BLK, D), vec_master,
    )
    reduced, ingrad, vec_grad, rms = tail(
        block, lengths, vec_feed, squares, lse, d_ctx.reshape(seqs, part, D), ctx_split, d_branch, d_inner,
        mid, act, d_feed, whole, q, k, v, ctx, w,
    )
    return (
        out.reshape(tokens.shape),
        d_res,
        ingrad.reshape(total, D),
        wide_mid.reshape(tokens.shape),
        rms,
        vec_grad,
        reduced.reshape(LIST, BLK, D),
        spot,
        has,
    )


def per_device(
    tokens, cotangent, lengths, owner, master, moment, second, vec_master, vec_moment, vec_second
):
    slot_local = master.shape[0]
    given = (tokens, cotangent, lengths, owner, master, vec_master)
    if lax.axis_size("dp") == 8 and lax.axis_size("seq") == 4:
        place, mine, block, spot, has, fits = tables(owner, slot_local)

        def otherwise(*args):
            results = general(*args[:6])
            pad = ((0, LIST - slot_local), (0, 0), (0, 0))
            return results[:6] + (jnp.pad(results[6], pad),) + results[7:]

        results = lax.cond(fits[0] > 0, listed, otherwise, *given, place, mine, block, spot, has)
    else:
        results = general(*given)
    layer_out, d_res, ingrad, residual_mid, rms, vec_grad, reduced, spot, has = results
    updated = adam_all(
        spot, has, reduced, moment, second, master,
        d_res, ingrad, rms, vec_grad, vec_moment, vec_second, vec_master,
    )
    input_grad, sublayer_rms, slots, vectors = updated[0], updated[1], updated[2:6], updated[6:]
    return (layer_out, input_grad.reshape(tokens.shape), residual_mid, sublayer_rms, *slots, *vectors)


def solution(mesh):
    return jax.shard_map(
        per_device,
        mesh=mesh,
        in_specs=(
            P("dp", "seq", None),
            P("dp", "seq", None),
            P("dp"),
            P(),
            P("dp", None, None),
            P("dp", None, None),
            P("dp", None, None),
            P(),
            P(),
            P(),
        ),
        out_specs=(
            P("dp", "seq", None),
            P("dp", "seq", None),
            P("dp", "seq", None),
            P("dp", None),
            P("dp", None, None),
            P("dp", None, None),
            P("dp", None, None),
            P("dp", None, None),
            P(),
            P(),
            P(),
            P(),
        ),
        check_vma=False,
    )
```

```python
from functools import partial

import jax
import jax.numpy as jnp
from jax import lax
from jax.experimental import pallas as pl
from jax.experimental.pallas import tpu as pltpu
from jax.sharding import PartitionSpec as P

D = 768
H = 12
DH = 64
FF = 3072
BLK = 128
SEQLEN = 512
STEP = 5


first_decay = 0.5
second_decay = 0.5
matrix_rate = 0.02
vector_rate = 0.2
weight_decay = 0.01
adam_epsilon = 1e-08


def adam_step(gradient, moment, second, weight, rate):
    moment_new = first_decay * moment + (1.0 - first_decay) * gradient
    second_new = second_decay * second + (1.0 - second_decay) * gradient * gradient
    moment_hat = moment_new * (1.0 / (1.0 - first_decay**STEP))
    second_hat = second_new * (1.0 / (1.0 - second_decay**STEP))
    root = second_hat * lax.rsqrt(second_hat) + adam_epsilon
    inverse = pltpu.reciprocal(root, approx=True)
    inverse = inverse * (2.0 - root * inverse)
    weight_new = weight - rate * (moment_hat * inverse + weight_decay * weight)
    return (moment_new, second_new, weight_new)


def seq_swap(parts, axis):
    size = lax.axis_size(axis)
    me = lax.axis_index(axis)
    stacked = parts
    got = [None] * size
    mine = lax.dynamic_index_in_dim(stacked, me, 0, keepdims=False)
    out = [mine]
    for hop in range(1, size):
        there = jnp.bitwise_xor(me, hop)
        piece = lax.dynamic_index_in_dim(stacked, there, 0, keepdims=False)
        route = [(i, i ^ hop) for i in range(size)]
        out.append(lax.ppermute(piece, axis, route))
    return out


def from_hops(pieces, axis):
    size = lax.axis_size(axis)
    me = lax.axis_index(axis)
    stacked = jnp.stack(pieces, axis=0)
    order = jnp.bitwise_xor(jnp.arange(size, dtype=jnp.int32), me)
    return jnp.take(stacked, order, axis=0)


def to_whole(block, axis):
    size = lax.axis_size(axis)
    count, length, width = block.shape
    pieces = seq_swap(block.reshape(size, count // size, length, width), axis)
    stacked = from_hops(pieces, axis)
    return jnp.swapaxes(stacked, 0, 1).reshape(count // size, size * length, width)


def to_split(whole, axis):
    size = lax.axis_size(axis)
    own, full, width = whole.shape
    parts = jnp.swapaxes(whole.reshape(own, size, full // size, width), 0, 1)
    pieces = seq_swap(parts, axis)
    return from_hops(pieces, axis).reshape(size * own, full // size, width)


LANES = 128
PAIRS = D // LANES
CHUNKS = FF // D
MASKED = -1e30
NT = (((1,), (1,)), ((), ()))
TN = (((0,), (0,)), ((), ()))
MIB = 1 << 20


def mm(left, right):
    return jnp.dot(left, right, preferred_element_type=jnp.float32)


def mm_nt(left, right):
    return lax.dot_general(left, right, NT, preferred_element_type=jnp.float32)


def mm_tn(left, right):
    return lax.dot_general(left, right, TN, preferred_element_type=jnp.float32)


def load_blocks(pool_ref, place_ref, first, into_ref, sem):
    def start(i, _):
        pltpu.make_async_copy(
            pool_ref.at[place_ref[first + i]], into_ref.at[pl.ds(i * BLK, BLK)], sem
        ).start()
        return 0

    lax.fori_loop(0, into_ref.shape[0] // BLK, start, 0)


def wait_whole(ref, sem):
    pltpu.make_async_copy(ref, ref, sem).wait()


def spare_lanes(rows, half, bias_column):
    lane = lax.broadcasted_iota(jnp.int32, (rows, LANES), 1)
    first = DH * (1 - half)
    spare = jnp.where(lane == first, bias_column, jnp.where(lane < first + 4, 1.0, 0.0))
    inside = (lane >= DH * half) & (lane < DH * half + DH)
    return inside, spare.astype(jnp.bfloat16)


def split3(row):
    one = row.astype(jnp.bfloat16)
    rest = row - one.astype(jnp.float32)
    two = rest.astype(jnp.bfloat16)
    three = (rest - two.astype(jnp.float32)).astype(jnp.bfloat16)
    return one, two, three


def beside(head_rows, extra, half):
    columns = head_rows.shape[1]
    pad = jnp.zeros((DH - extra.shape[0], columns), jnp.bfloat16)
    parts = [extra.astype(jnp.bfloat16), pad]
    order = [head_rows] + parts if half == 0 else parts + [head_rows]
    return jnp.concatenate(order, axis=0)


def forward_pair(q_ref, k_ref, v_ref, ctx_ref, lse_ref, seq, p, bias):
    rows = q_ref.shape[0]
    cols = pl.ds(pl.multiple_of(p * LANES, LANES), LANES)
    row8 = lax.broadcasted_iota(jnp.int32, (16, rows), 0)
    q2t = q_ref[:, cols].T
    k2 = k_ref[:, cols]
    v2t = v_ref[:, cols].T
    outs = []
    for half in range(2):
        inside, spare = spare_lanes(rows, half, bias)
        k_aug = jnp.where(inside, k2, spare)
        head = slice(half * DH, half * DH + DH)
        q_aug = beside(q2t[head], jnp.where(row8 == 0, 1.0, 0.0), half)
        scores = mm(k_aug, q_aug)
        top = jnp.max(scores, axis=0, keepdims=True)
        expos = jnp.exp(scores - top).astype(jnp.bfloat16)
        v_aug = jnp.concatenate([v2t[head], jnp.ones((16, rows), jnp.bfloat16)], axis=0)
        both = mm(v_aug, expos)
        total = both[DH : DH + 1]
        outs.append(both[0:DH] / total)
        lse_ref[seq, pl.ds(2 * p + half, 1), :] = top + jnp.log(total)
    ctx_ref[:, cols] = jnp.concatenate(outs, axis=0).T.astype(jnp.bfloat16)


def attend_kernel(
    place_ref, lengths_ref, tokens_ref, pool_ref, vec_ref,
    q_ref, k_ref, v_ref, ctx_ref, lse_ref, w_scr,
    sem,
):
    seq = pl.program_id(0)
    rows = tokens_ref.shape[0]

    @pl.when(seq == 0)
    def _():
        load_blocks(pool_ref, place_ref, 0, w_scr, sem)
        wait_whole(w_scr, sem)

    tokens = tokens_ref[...]
    q_ref[...] = ((mm(tokens, w_scr[0:D, :]) + vec_ref[0:1, :]).astype(jnp.bfloat16) * 0.125).astype(jnp.bfloat16)
    k_ref[...] = mm(tokens, w_scr[D : 2 * D, :]).astype(jnp.bfloat16)
    v_ref[...] = (mm(tokens, w_scr[2 * D :, :]) + vec_ref[1:2, :]).astype(jnp.bfloat16)
    key = lax.broadcasted_iota(jnp.int32, (rows, 1), 0)
    bias = jnp.where(key < lengths_ref[seq], 0.0, MASKED)

    def pair(p, _):
        forward_pair(q_ref, k_ref, v_ref, ctx_ref, lse_ref, 0, p, bias)
        return 0

    lax.fori_loop(0, PAIRS, pair, 0)


def attend(place, lengths, tokens, pool, vec):
    seqs, rows, _ = tokens.shape
    flat = tokens.reshape(seqs * rows, D)
    row_spec = pl.BlockSpec((rows, D), lambda s, *_: (s, 0))
    any_spec = pl.BlockSpec(memory_space=pl.ANY)
    low = jax.ShapeDtypeStruct((seqs * rows, D), jnp.bfloat16)
    return pl.pallas_call(
        attend_kernel,
        grid_spec=pltpu.PrefetchScalarGridSpec(
            num_scalar_prefetch=2,
            grid=(seqs,),
            in_specs=[row_spec, any_spec, pl.BlockSpec(vec.shape, lambda s, *_: (0, 0))],
            out_specs=[row_spec] * 4
            + [
                pl.BlockSpec((1, 16, rows), lambda s, *_: (s, 0, 0)),
                pl.BlockSpec((3 * D, D), lambda s, *_: (0, 0)),
            ],
            scratch_shapes=[pltpu.SemaphoreType.DMA],
        ),
        out_shape=[low] * 4
        + [
            jax.ShapeDtypeStruct((seqs, 16, rows), jnp.float32),
            jax.ShapeDtypeStruct((3 * D, D), jnp.bfloat16),
        ],
        compiler_params=pltpu.CompilerParams(vmem_limit_bytes=48 * MIB),
        cost_estimate=pl.CostEstimate(
            flops=6 * seqs * rows * D * D + 4 * seqs * rows * rows * D,
            bytes_accessed=10 * seqs * rows * D + 6 * D * D,
            transcendentals=seqs * rows * rows * H,
        ),
        name="attend",
    )(place, lengths, flat, pool, vec)


def gelu_parts(x):
    z = jnp.abs(x) * 0.7071067811865476
    t_in = 1.0 + 0.3275911 * z
    t = pltpu.reciprocal(t_in, approx=True)
    t = t * (2.0 - t_in * t)
    e = jnp.exp(-0.5 * (x * x))
    poly = 1.061405429 * t - 1.453152027
    poly = poly * t + 1.421413741
    poly = poly * t - 0.284496736
    poly = poly * t + 0.254829592
    tail = (0.5 * t) * poly * e
    dist = jnp.where(x >= 0, 1.0 - tail, tail)
    return dist, x * e * 0.3989422804014327


def norm_stats(resid):
    center = resid - jnp.mean(resid, axis=-1, keepdims=True)
    scale = lax.rsqrt(jnp.mean(center * center, axis=-1, keepdims=True) + 1e-05)
    return center * scale, scale


def norm_back(d_out, gain, hat, scale):
    d_hat = d_out * gain
    mean_one = jnp.mean(d_hat, axis=-1, keepdims=True)
    mean_hat = jnp.mean(d_hat * hat, axis=-1, keepdims=True)
    return scale * (d_hat - mean_one - hat * mean_hat)


def feed_kernel(
    place_ref, lengths_ref, tokens_ref, ctx_ref, cot_ref, pool_ref, vec_ref,
    wide_mid_ref, mid_ref, out_ref, act_ref, dinner_ref, dfeed_ref, dbranch_ref, dres_ref, dctx_ref, grad_ref, sq_ref,
    w_out, w_up, w_down, slope_scr, sem, *, seq_rows,
):
    step = pl.program_id(0)
    rows = tokens_ref.shape[0]
    tiles = sq_ref.shape[0]
    first = 3 * D // BLK

    @pl.when(step == 0)
    def _():
        load_blocks(pool_ref, place_ref, first, w_out, sem.at[0])
        load_blocks(pool_ref, place_ref, first + D // BLK, w_up, sem.at[1])
        load_blocks(pool_ref, place_ref, first + (D + FF) // BLK, w_down, sem.at[2])
        wait_whole(w_out, sem.at[0])
        grad_ref[...] = jnp.zeros_like(grad_ref)

    def add_row(row, value):
        grad_ref[row : row + 1, :] += jnp.sum(value, axis=0, keepdims=True)

    segment = min(rows, seq_rows)
    row = lax.broadcasted_iota(jnp.int32, (rows, 1), 0)
    length = jnp.zeros((rows, 1), jnp.int32)
    for j in range(rows // segment):
        length = jnp.where(row // segment == j, lengths_ref[(step * rows + j * segment) // seq_rows], length)
    place_in = (step * rows + row) % seq_rows
    if seq_rows < SEQLEN:
        place_in += lax.axis_index("seq") * seq_rows
    valid = (place_in < length).astype(jnp.float32)

    def square_sums(which, value):
        square = value * value * valid
        for j in range(rows // segment):
            sq_ref[0, 2 * j + which : 2 * j + which + 1, :] = jnp.sum(
                square[j * segment : (j + 1) * segment], axis=0, keepdims=True
            )

    branch = mm(ctx_ref[...], w_out[...]) + vec_ref[2:3, :]
    square_sums(0, branch)
    hat1, scale1 = norm_stats(tokens_ref[...].astype(jnp.float32) + branch)
    middle = hat1 * vec_ref[4:5, :] + vec_ref[5:6, :]
    wide_mid_ref[...] = middle
    mid_ref[...] = middle.astype(jnp.bfloat16)
    mid_low = mid_ref[...]

    @pl.when(step == 0)
    def _():
        wait_whole(w_up, sem.at[1])

    feed = jnp.zeros((rows, D), jnp.float32) + vec_ref[3:4, :]
    parts = [slice(c * D, (c + 1) * D) for c in range(CHUNKS)]

    def up(c):
        return mm_nt(mid_low, w_up[parts[c], :])

    def bend(c, inner):
        inner = inner + vec_ref[8 + c : 9 + c, :]
        dist, bell = gelu_parts(inner)
        act = (inner * dist).astype(jnp.bfloat16)
        act_ref[:, parts[c]] = act
        slope_scr[:, parts[c]] = dist + bell
        return act

    inner = up(0)

    @pl.when(step == 0)
    def _():
        wait_whole(w_down, sem.at[2])

    for c in range(CHUNKS):
        after = up(c + 1) if c + 1 < CHUNKS else None
        act = bend(c, inner)
        feed += mm(act, w_down[parts[c], :])
        inner = after
    square_sums(1, feed)
    hat2, scale2 = norm_stats(middle + feed)
    gain2 = vec_ref[6:7, :]
    out_ref[...] = (hat2 * gain2 + vec_ref[7:8, :]).astype(jnp.bfloat16)
    upstream = cot_ref[...].astype(jnp.float32) * valid
    add_row(6, upstream * hat2)
    add_row(7, upstream)
    d_res2 = norm_back(upstream, gain2, hat2, scale2)
    d_feed = d_res2.astype(jnp.bfloat16)
    dfeed_ref[...] = d_feed
    add_row(3, d_feed.astype(jnp.float32))
    d_mid = d_res2
    d_act = mm_nt(d_feed, w_down[parts[0], :])
    for c in range(CHUNKS):
        after = mm_nt(d_feed, w_down[parts[c + 1], :]) if c + 1 < CHUNKS else None
        d_inner = (d_act * slope_scr[:, parts[c]]).astype(jnp.bfloat16)
        dinner_ref[:, parts[c]] = d_inner
        add_row(8 + c, d_inner.astype(jnp.float32))
        d_mid += mm(d_inner, w_up[parts[c], :])
        d_act = after
    add_row(4, d_mid * hat1)
    add_row(5, d_mid)
    d_res1 = norm_back(d_mid, vec_ref[4:5, :], hat1, scale1)
    dres_ref[...] = d_res1
    d_branch = d_res1.astype(jnp.bfloat16)
    dbranch_ref[...] = d_branch
    add_row(2, d_branch.astype(jnp.float32))
    dctx_ref[...] = mm_nt(d_branch, w_out[...]).astype(jnp.bfloat16)


def feed_both(place, lengths, seq_rows, tokens, ctx, cot, pool, vec, tile=512):
    total = tokens.shape[0]
    steps = total // tile
    row_spec = pl.BlockSpec((tile, D), lambda s, *_: (s, 0))
    wide_spec = pl.BlockSpec((tile, FF), lambda s, *_: (s, 0))
    any_spec = pl.BlockSpec(memory_space=pl.ANY)
    low = jax.ShapeDtypeStruct((total, D), jnp.bfloat16)
    wide = jax.ShapeDtypeStruct((total, FF), jnp.bfloat16)
    return pl.pallas_call(
        partial(feed_kernel, seq_rows=seq_rows),
        grid_spec=pltpu.PrefetchScalarGridSpec(
            num_scalar_prefetch=2,
            grid=(steps,),
            in_specs=[row_spec] * 3 + [any_spec, pl.BlockSpec(vec.shape, lambda s, *_: (0, 0))],
            out_specs=[row_spec, row_spec, row_spec, wide_spec, wide_spec, row_spec, row_spec, row_spec, row_spec,
                pl.BlockSpec((16, D), lambda s, *_: (0, 0)),
                pl.BlockSpec((1, 8, D), lambda s, *_: (s, 0, 0))],
            scratch_shapes=[
                pltpu.VMEM((D, D), jnp.bfloat16),
                pltpu.VMEM((FF, D), jnp.bfloat16),
                pltpu.VMEM((FF, D), jnp.bfloat16),
                pltpu.VMEM((tile, FF), jnp.float32),
                pltpu.SemaphoreType.DMA((3,)),
            ],
        ),
        out_shape=[jax.ShapeDtypeStruct((total, D), jnp.float32), low, low, wide, wide, low, low, jax.ShapeDtypeStruct((total, D), jnp.float32), low,
            jax.ShapeDtypeStruct((16, D), jnp.float32),
            jax.ShapeDtypeStruct((steps, 8, D), jnp.float32)],
        compiler_params=pltpu.CompilerParams(vmem_limit_bytes=62 * MIB),
        cost_estimate=pl.CostEstimate(
            flops=8 * total * D * FF + 4 * total * D * D,
            bytes_accessed=total * (16 * D + 4 * FF) + 12 * FF * D,
            transcendentals=total * FF,
        ),
        name="feed_both",
    )(place, lengths, tokens, ctx, cot, pool, vec)


def send_blocks(value, held, slot, first, place_ref, out_ref, sem):
    held[slot] = value.astype(jnp.bfloat16).reshape(D // BLK, BLK, D)
    for i in range(D // BLK):
        pltpu.make_async_copy(
            held.at[slot, i], out_ref.at[place_ref[first + i]], sem.at[slot]
        ).start()


def feed_grads_kernel(
    place_ref, ctx_ref, dbranch_ref, dinner_ref, mid_ref, act_ref, dfeed_ref, out_ref, held, sem
):
    step = pl.program_id(0)
    slot = lax.rem(step, 2)
    base = 3 * D // BLK

    @pl.when(step >= 2)
    def _():
        wait_whole(held.at[slot], sem.at[slot])

    first = base + step * (D // BLK)

    @pl.when(step == 0)
    def _():
        send_blocks(mm_tn(ctx_ref[...], dbranch_ref[...]), held, slot, first, place_ref, out_ref, sem)

    @pl.when((step >= 1) & (step <= CHUNKS))
    def _():
        send_blocks(mm_tn(dinner_ref[...], mid_ref[...]), held, slot, first, place_ref, out_ref, sem)

    @pl.when(step > CHUNKS)
    def _():
        send_blocks(mm_tn(act_ref[...], dfeed_ref[...]), held, slot, first, place_ref, out_ref, sem)

    @pl.when(step == 2 * CHUNKS)
    def _():
        wait_whole(held.at[slot], sem.at[slot])
        wait_whole(held.at[1 - slot], sem.at[1 - slot])


def feed_grads(place, places, ctx, d_branch, d_inner, mid, act, d_feed):
    total = ctx.shape[0]
    whole = pl.BlockSpec((total, D), lambda s, *_: (0, 0))
    return pl.pallas_call(
        feed_grads_kernel,
        grid_spec=pltpu.PrefetchScalarGridSpec(
            num_scalar_prefetch=1,
            grid=(1 + 2 * CHUNKS,),
            in_specs=[
                whole,
                whole,
                pl.BlockSpec((total, D), lambda s, *_: (0, jnp.clip(s - 1, 0, CHUNKS - 1))),
                whole,
                pl.BlockSpec((total, D), lambda s, *_: (0, jnp.clip(s - 1 - CHUNKS, 0, CHUNKS - 1))),
                whole,
            ],
            out_specs=pl.BlockSpec(memory_space=pl.ANY),
            scratch_shapes=[
                pltpu.VMEM((2, D // BLK, BLK, D), jnp.bfloat16),
                pltpu.SemaphoreType.DMA((2,)),
            ],
        ),
        out_shape=jax.ShapeDtypeStruct((places, BLK, D), jnp.bfloat16),
        compiler_params=pltpu.CompilerParams(vmem_limit_bytes=48 * MIB),
        cost_estimate=pl.CostEstimate(
            flops=4 * total * D * FF + 2 * total * D * D,
            bytes_accessed=total * (8 * D + 4 * FF) + 4 * FF * D,
            transcendentals=0,
        ),
        name="feed_grads",
    )(place, ctx, d_branch, d_inner, mid, act, d_feed)


def attend_back_kernel(
    place_w_ref, place_ref, lengths_ref, tokens_ref, q_ref, k_ref, v_ref, ctx_ref, dctx_ref, lse_ref, dres_ref, pool_ref, held_in,
    ingrad_ref, vec_ref, out_ref,
    w_scr, dq_scr, dk_scr, dv_scr, total_scr, held, sem, w_sem,
):
    seq = pl.program_id(0)
    last = pl.num_programs(0) - 1
    rows = tokens_ref.shape[0]

    @pl.when(seq == 0)
    def _():
        load_blocks(pool_ref, place_w_ref, 0, w_scr, w_sem)
        vec_ref[...] = jnp.zeros_like(vec_ref)

    key = lax.broadcasted_iota(jnp.int32, (rows, 1), 0)
    bias = jnp.where(key < lengths_ref[seq], 0.0, MASKED)

    def pair(p, _):
        cols, d_query, d_key, d_value = back_pair(q_ref, k_ref, v_ref, ctx_ref, dctx_ref, lse_ref, 0, p, bias)
        dq_scr[:, cols] = d_query
        dk_scr[:, cols] = d_key
        dv_scr[:, cols] = d_value
        return 0

    lax.fori_loop(0, PAIRS, pair, 0)

    @pl.when(seq == 0)
    def _():
        wait_whole(w_scr, w_sem)

    dq, dk, dv = dq_scr[...], dk_scr[...], dv_scr[...]
    vec_ref[0:1, :] += jnp.sum(dq.astype(jnp.float32), axis=0, keepdims=True)
    vec_ref[1:2, :] += jnp.sum(dv.astype(jnp.float32), axis=0, keepdims=True)
    ingrad = dres_ref[...] + mm_nt(dq, w_scr[0:D, :])
    ingrad += mm_nt(dk, w_scr[D : 2 * D, :])
    ingrad += mm_nt(dv, w_scr[2 * D :, :])
    ingrad_ref[...] = ingrad.astype(jnp.bfloat16)
    tokens = tokens_ref[...]
    for i, right in enumerate((dq, dk, dv)):
        part = slice(i * D, (i + 1) * D)

        @pl.when(seq == 0)
        def _():
            total_scr[part, :] = mm_tn(tokens, right)

        @pl.when(seq > 0)
        def _():
            total_scr[part, :] += mm_tn(tokens, right)

    @pl.when(seq == last)
    def _():
        for i in range(3):
            send_blocks(total_scr[i * D : (i + 1) * D, :], held, i, i * (D // BLK), place_ref, out_ref, sem)
        for i in range(3):
            wait_whole(held.at[i], sem.at[i])


def attend_back(place_w, place, lengths, tokens, q, k, v, ctx, d_ctx, lse, d_res, pool, held):
    seqs, rows, _ = tokens.shape
    flat = tokens.reshape(seqs * rows, D)
    row_spec = pl.BlockSpec((rows, D), lambda s, *_: (s, 0))
    any_spec = pl.BlockSpec(memory_space=pl.ANY)
    return pl.pallas_call(
        attend_back_kernel,
        grid_spec=pltpu.PrefetchScalarGridSpec(
            num_scalar_prefetch=3,
            grid=(seqs,),
            in_specs=[row_spec] * 6
            + [pl.BlockSpec((1, 16, rows), lambda s, *_: (s, 0, 0)), row_spec, any_spec, any_spec],
            out_specs=[row_spec, pl.BlockSpec((8, D), lambda s, *_: (0, 0)), any_spec],
            scratch_shapes=[
                pltpu.VMEM((3 * D, D), jnp.bfloat16),
                pltpu.VMEM((rows, D), jnp.bfloat16),
                pltpu.VMEM((rows, D), jnp.bfloat16),
                pltpu.VMEM((rows, D), jnp.bfloat16),
                pltpu.VMEM((3 * D, D), jnp.float32),
                pltpu.VMEM((3, D // BLK, BLK, D), jnp.bfloat16),
                pltpu.SemaphoreType.DMA((3,)),
                pltpu.SemaphoreType.DMA,
            ],
        ),
        out_shape=[
            jax.ShapeDtypeStruct((seqs * rows, D), jnp.bfloat16),
            jax.ShapeDtypeStruct((8, D), jnp.float32),
            jax.ShapeDtypeStruct(held.shape, held.dtype),
        ],
        input_output_aliases={12: 2},
        compiler_params=pltpu.CompilerParams(vmem_limit_bytes=62 * MIB),
        cost_estimate=pl.CostEstimate(
            flops=12 * seqs * rows * D * D + 10 * seqs * rows * rows * D,
            bytes_accessed=20 * seqs * rows * D + 12 * D * D,
            transcendentals=seqs * rows * rows * H,
        ),
        name="attend_back",
    )(place_w, place, lengths, flat, q, k, v, ctx, d_ctx, lse, d_res, pool, held)


def adam_kernel(
    place_ref, has_ref, grad_a, grad_b, moment_ref, second_ref, master_ref,
    dres_ref, part_ref, rms_ref, vec_ref, vec_moment_ref, vec_second_ref, vec_master_ref,
    ingrad_out, rms_out, grad_out, moment_out, second_out, master_out,
    vec_out, vec_moment_out, vec_second_out, vec_master_out,
):
    step = pl.program_id(0)
    for j, grad_in in enumerate((grad_a, grad_b)):
        got = grad_in[0].astype(jnp.float32)
        gradient = jnp.where(has_ref[2 * step + j] > 0, got, jnp.zeros_like(got))
        grad_out[j] = gradient
        moment_out[j], second_out[j], master_out[j] = adam_step(
            gradient, moment_ref[j], second_ref[j], master_ref[j], matrix_rate
        )
    ingrad_out[...] = dres_ref[...] + part_ref[...].astype(jnp.float32)

    @pl.when(step == 0)
    def _():
        rms_out[...] = rms_ref[:, 0:2]
        gradient = vec_ref[0 : vec_out.shape[0], :]
        vec_out[...] = gradient
        vec_moment_out[...], vec_second_out[...], vec_master_out[...] = adam_step(
            gradient, vec_moment_ref[...], vec_second_ref[...], vec_master_ref[...], vector_rate
        )


def adam_all(place, has, reduced, moment, second, master, d_res, part, rms, vec, vec_moment, vec_second, vec_master):
    slots = master.shape[0]
    steps = slots // 2
    total = d_res.shape[0]
    pieces = 1
    while 2 * pieces <= steps:
        pieces *= 2
    pair = pl.BlockSpec((2, BLK, D), lambda s, *_: (s, 0, 0))
    rows = pl.BlockSpec((total // pieces, D), lambda s, *_: (jnp.minimum(s, pieces - 1), 0))

    def whole(shape):
        return pl.BlockSpec(shape, lambda s, *_: (0, 0))

    full = jax.ShapeDtypeStruct(master.shape, jnp.float32)
    vec_full = jax.ShapeDtypeStruct(vec_master.shape, jnp.float32)
    return pl.pallas_call(
        adam_kernel,
        grid_spec=pltpu.PrefetchScalarGridSpec(
            num_scalar_prefetch=2,
            grid=(steps,),
            in_specs=[
                pl.BlockSpec((1, BLK, D), lambda s, place, has: (place[2 * s], 0, 0)),
                pl.BlockSpec((1, BLK, D), lambda s, place, has: (place[2 * s + 1], 0, 0)),
            ]
            + [pair] * 3
            + [rows] * 2
            + [whole(rms.shape), whole(vec.shape)]
            + [whole(vec_master.shape)] * 3,
            out_specs=[rows, whole((rms.shape[0], 2))] + [pair] * 4 + [whole(vec_master.shape)] * 4,
        ),
        out_shape=[
            jax.ShapeDtypeStruct(d_res.shape, jnp.float32),
            jax.ShapeDtypeStruct((rms.shape[0], 2), jnp.float32),
        ]
        + [full] * 4
        + [vec_full] * 4,
        compiler_params=pltpu.CompilerParams(vmem_limit_bytes=60 * MIB),
        cost_estimate=pl.CostEstimate(
            flops=20 * slots * BLK * D, bytes_accessed=30 * slots * BLK * D, transcendentals=2 * slots * BLK * D
        ),
        name="adam_all",
    )(place, has, reduced, reduced, moment, second, master, d_res, part, rms, vec, vec_moment, vec_second, vec_master)


EARLY = 6
MIDDLE = 8
LATE = 10
FIRST = 10
LIST = EARLY + MIDDLE + LATE
HEAD_BLOCKS = 3 * D // BLK
MESH = pl.DeviceIdType.MESH


class Place:
    def __init__(self):
        dp = lax.axis_index("dp")
        self.z = lax.axis_index("seq")
        self.core = dp % 2
        x = (dp // 2) % 2
        y = dp // 4
        self.chip = dp // 2
        self.chip_x = 2 * y + 1 - x
        self.chip_y = 2 * (1 - y) + x
        self.chip_xy = 2 * (1 - y) + 1 - x
        self.to_core = {"dp": dp + 1 - 2 * self.core}
        self.to_x = {"dp": dp + 2 - 4 * x}
        self.to_y = {"dp": dp + 4 - 8 * y}
        z = self.z
        self.z_hops = (z + 1 - 2 * (z % 2), (z + 2) % 4, 3 - z)
        self.to_z = tuple({"seq": hop} for hop in self.z_hops)
        self.partners = (self.to_core, self.to_x, self.to_y) + self.to_z

    def meet(self):
        barrier = pltpu.get_barrier_semaphore()
        for partner in self.partners:
            pl.semaphore_signal(barrier, inc=1, device_id=partner, device_id_type=MESH)
        pl.semaphore_wait(barrier, len(self.partners))


class Sender:
    def __init__(self, send_sem, recv_sem):
        self.send_sem, self.recv_sem = send_sem, recv_sem

    def copy(self, k, src, dst, partner):
        return pltpu.make_async_remote_copy(
            src_ref=src,
            dst_ref=dst,
            send_sem=self.send_sem.at[k],
            recv_sem=self.recv_sem.at[k],
            device_id=partner,
            device_id_type=MESH,
        )


class Gather:
    def __init__(self, here, sender, first_sem, count, own, own_row, pool, row_of):
        self.here, self.sender, self.k, self.n = here, sender, first_sem, count
        self.own, self.own_row, self.pool, self.row_of = own, own_row, pool, row_of
        self.half = count * BLK // 2

    def link(self, name):
        here, half = self.here, self.half

        def own(part):
            return self.own.at[pl.ds(self.own_row + part * half, half)]

        def piece(chip, part):
            return self.pool.at[pl.ds(self.row_of(chip, here.core) + part * half, half)]

        def whole(chip):
            return self.pool.at[pl.ds(self.row_of(chip, here.core), 2 * half)]

        order = ("x0", "x1", "y1", "y0", "y_on", "x_on", "share_x", "share_y", "share_xy", "share_me")
        src, dst, partner = {
            "x0": lambda: (own(0), piece(here.chip, 0), here.to_x),
            "x1": lambda: (own(1), piece(here.chip, 1), here.to_x),
            "y1": lambda: (own(1), piece(here.chip, 1), here.to_y),
            "y0": lambda: (own(0), piece(here.chip, 0), here.to_y),
            "y_on": lambda: (piece(here.chip_x, 0), piece(here.chip_x, 0), here.to_y),
            "x_on": lambda: (piece(here.chip_y, 1), piece(here.chip_y, 1), here.to_x),
            "share_x": lambda: (whole(here.chip_x), whole(here.chip_x), here.to_core),
            "share_y": lambda: (whole(here.chip_y), whole(here.chip_y), here.to_core),
            "share_xy": lambda: (whole(here.chip_xy), whole(here.chip_xy), here.to_core),
            "share_me": lambda: (
                self.own.at[pl.ds(self.own_row, 2 * half)], whole(here.chip), here.to_core
            ),
        }[name]()
        return self.sender.copy(self.k + order.index(name), src, dst, partner)

    def start(self):
        for name in ("x0", "y1", "x1", "y0", "share_me"):
            self.link(name).start()

    def pass_on(self):
        self.link("x0").wait_recv()
        self.link("y_on").start()
        self.link("y1").wait_recv()
        self.link("x_on").start()

    def share_near(self):
        self.link("x1").wait_recv()
        self.link("share_x").start()
        self.link("y0").wait_recv()
        self.link("share_y").start()

    def sent(self):
        for name in ("x0", "y1", "x1", "y0", "y_on", "x_on"):
            self.link(name).wait_send()

    def share_far(self):
        self.link("y_on").wait_recv()
        self.link("x_on").wait_recv()
        self.link("share_xy").start()

    def finish(self):
        for name in ("share_me", "share_x", "share_y", "share_xy"):
            self.link(name).wait_recv()

    def shared(self):
        for name in ("share_me", "share_x", "share_y", "share_xy"):
            self.link(name).wait_send()


def front_kernel(
    place_ref, mine_ref, lengths_ref, vec_ref, master_in, tokens_in,
    pool, q_out, k_out, v_out, ctx_out, w_out, tok_out, ctx_split, lse_ref,
    stage, give, take, near, pack, w, tok, qs, ks, vs, cs,
    send_sem, recv_sem, load_sem,
):
    here = Place()
    z = here.z
    sender = Sender(send_sem, recv_sem)
    rows = SEQLEN
    own = tokens_in.shape[0] // 4
    part = tokens_in.shape[1]
    slots = master_in.shape[0]
    second = LIST - FIRST

    def local(src, dst, k):
        return pltpu.make_async_copy(src, dst, load_sem.at[k])

    load_master = local(master_in, stage, 0)
    load_master.start()
    own_tokens = [
        local(tokens_in.at[own * z + s], tok.at[pl.ds(s * rows + part * z, part)], 3 + s) for s in range(own)
    ]
    for load in own_tokens:
        load.start()
    here.meet()
    swaps = [
        sender.copy(
            own * hop + s,
            tokens_in.at[own * here.z_hops[hop] + s],
            tok.at[pl.ds(s * rows + part * z, part)],
            here.to_z[hop],
        )
        for hop in range(3)
        for s in range(own)
    ]
    for swap in swaps:
        swap.start()
    parts = (FIRST // 2, second // 2)
    starts = (0, FIRST)
    trades = [
        sender.copy(
            6 + i,
            give.at[pl.ds(i * parts[0] * BLK, parts[i] * BLK)],
            take.at[pl.ds(i * parts[0] * BLK, parts[i] * BLK)],
            here.to_core,
        )
        for i in range(2)
    ]
    load_master.wait()

    def held(entry):
        return stage[jnp.clip(mine_ref[entry] - here.core * slots, 0, slots - 1)].astype(jnp.bfloat16)

    for i in range(2):

        def fill_give(p, _):
            give[pl.ds((i * parts[0] + p) * BLK, BLK), :] = held(starts[i] + (1 - here.core) * parts[i] + p)
            return 0

        lax.fori_loop(0, parts[i], fill_give, 0)
        trades[i].start()

    def own_block(i, p):
        entry = starts[i] + here.core * parts[i] + p
        traded = take[pl.ds((i * parts[0] + p) * BLK, BLK), :]
        return jnp.where(mine_ref[entry] // slots == here.core, held(entry), traded)

    trades[0].wait_recv()

    def fill_near(p, _):
        near[pl.ds((here.chip * FIRST + here.core * parts[0] + p) * BLK, BLK), :] = own_block(0, p)
        return 0

    lax.fori_loop(0, parts[0], fill_near, 0)
    first = Gather(
        here, sender, 8, FIRST // 2, near, (here.chip * FIRST + here.core * (FIRST // 2)) * BLK, near,
        lambda chip, core: (chip * FIRST + core * (FIRST // 2)) * BLK,
    )
    then = Gather(
        here, sender, 18, second // 2, pack, 0, pool,
        lambda chip, core: (chip * LIST + FIRST + core * (second // 2)) * BLK,
    )
    first.start()

    trades[1].wait_recv()

    def fill_pack(p, _):
        pack[pl.ds(p * BLK, BLK), :] = own_block(1, p)
        return 0

    lax.fori_loop(0, parts[1], fill_pack, 0)
    own_second = local(
        pack, pool.at[pl.ds((here.chip * LIST + FIRST + here.core * parts[1]) * BLK, parts[1] * BLK)], 5
    )
    own_second.start()
    first.pass_on()
    first.share_near()
    first.sent()
    then.start()
    first.share_far()
    first.finish()

    def fill_w(b, _):
        at = place_ref[b]
        w[pl.ds(b * BLK, BLK), :] = near[pl.ds(((at // LIST) * FIRST + at % LIST) * BLK, BLK), :]
        return 0

    lax.fori_loop(0, HEAD_BLOCKS, fill_w, 0)
    keeps = [
        local(near.at[pl.ds(chip * FIRST * BLK, FIRST * BLK)], pool.at[pl.ds(chip * LIST * BLK, FIRST * BLK)], 6 + chip)
        for chip in range(4)
    ] + [local(w, w_out, 10)]
    for keep in keeps:
        keep.start()
    for load in own_tokens:
        load.wait()
    for swap in swaps:
        swap.wait_recv()
    keep_tok = local(tok, tok_out, 11)
    keep_tok.start()

    def send_ctx(s, hop):
        return sender.copy(
            28 + 3 * s + hop,
            cs.at[pl.ds(s * rows + part * here.z_hops[hop], part)],
            ctx_split.at[own * z + s],
            here.to_z[hop],
        )

    def keep_own(s):
        at = pl.ds(s * rows, rows)
        return [local(ref.at[at], out.at[at], 12 + k) for k, (ref, out) in enumerate(((qs, q_out), (ks, k_out), (vs, v_out), (cs, ctx_out)))] + [
            local(cs.at[pl.ds(s * rows + part * z, part)], ctx_split.at[own * z + s], 16)
        ]

    key = lax.broadcasted_iota(jnp.int32, (rows, 1), 0)

    def sequence(s, _):
        at = pl.ds(pl.multiple_of(s * rows, rows), rows)
        values = tok[at, :]
        qs[at, :] = ((mm(values, w[0:D, :]) + vec_ref[0:1, :]).astype(jnp.bfloat16) * 0.125).astype(jnp.bfloat16)
        ks[at, :] = mm(values, w[D : 2 * D, :]).astype(jnp.bfloat16)
        vs[at, :] = (mm(values, w[2 * D :, :]) + vec_ref[1:2, :]).astype(jnp.bfloat16)
        bias = jnp.where(key < lengths_ref[own * z + s], 0.0, MASKED)

        def pair(p, _):
            forward_pair(qs.at[at], ks.at[at], vs.at[at], cs.at[at], lse_ref, s, p, bias)
            return 0

        lax.fori_loop(0, PAIRS, pair, 0)
        for hop in range(3):
            send_ctx(s, hop).start()

        @pl.when(s > 0)
        def _():
            for keep in keep_own(s - 1):
                keep.wait()

        for keep in keep_own(s):
            keep.start()

        @pl.when(s == 0)
        def _():
            then.pass_on()

        return 0

    lax.fori_loop(0, own, sequence, 0)
    then.share_near()
    then.share_far()
    then.sent()
    then.finish()
    for keep in keep_own(own - 1) + keeps + [keep_tok, own_second]:
        keep.wait()
    for s in range(own):
        for hop in range(3):
            send_ctx(s, hop).wait_recv()
            send_ctx(s, hop).wait_send()
    for copy in swaps + trades:
        copy.wait_send()
    first.shared()
    then.shared()


def front(place, mine, lengths, vec, master, tokens):
    seqs, part, _ = tokens.shape
    total = seqs * part
    own = total // SEQLEN
    any_spec = pl.BlockSpec(memory_space=pl.ANY)
    vmem = pl.BlockSpec(memory_space=pltpu.VMEM)
    smem = pl.BlockSpec(memory_space=pltpu.SMEM)
    low = jnp.bfloat16
    slots = master.shape[0]
    flat = jax.ShapeDtypeStruct((total, D), low)
    return pl.pallas_call(
        front_kernel,
        in_specs=[smem] * 3 + [vmem] + [any_spec] * 2,
        out_specs=[any_spec] * 8 + [vmem],
        out_shape=[
            jax.ShapeDtypeStruct((4 * LIST * BLK, D), low),
            flat,
            flat,
            flat,
            flat,
            jax.ShapeDtypeStruct((3 * D, D), low),
            flat,
            jax.ShapeDtypeStruct(tokens.shape, low),
            jax.ShapeDtypeStruct((own, 16, SEQLEN), jnp.float32),
        ],
        scratch_shapes=[
            pltpu.VMEM(master.shape, jnp.float32),
            pltpu.VMEM((LIST // 2 * BLK, D), low),
            pltpu.VMEM((LIST // 2 * BLK, D), low),
            pltpu.VMEM((4 * FIRST * BLK, D), low),
            pltpu.VMEM(((LIST - FIRST) // 2 * BLK, D), low),
            pltpu.VMEM((3 * D, D), low),
        ]
        + [pltpu.VMEM((total, D), low)] * 5
        + [
            pltpu.SemaphoreType.DMA((34,)),
            pltpu.SemaphoreType.DMA((34,)),
            pltpu.SemaphoreType.DMA((17,)),
        ],
        compiler_params=pltpu.CompilerParams(
            vmem_limit_bytes=60 * MIB, collective_id=2, has_side_effects=True
        ),
        cost_estimate=pl.CostEstimate(
            flops=6 * total * D * D + 4 * total * SEQLEN * D,
            bytes_accessed=40 * total * D + 8 * slots * BLK * D,
            transcendentals=total * SEQLEN * H,
        ),
        name="front",
    )(place, mine, lengths, vec, master, tokens)


def add_rows(out_ref, out_row, terms, count, step=32):
    def body(i, _):
        value = None
        for ref, row in terms:
            part = ref[pl.ds(pl.multiple_of(row + i * step, step), step), :]
            value = part if value is None else value + part
        out_ref[pl.ds(pl.multiple_of(out_row + i * step, step), step), :] = value
        return 0

    lax.fori_loop(0, count // step, body, 0, unroll=2)


class Reduce:
    def __init__(self, here, sender, first_sem, count, first, column, blk_ref, grad, pack, buffers, red):
        self.here, self.sender, self.k = here, sender, first_sem
        self.n, self.first, self.blk, self.grad = count, first, blk_ref, grad
        self.acc, self.rx, self.ry, self.r2, self.z1, self.z2, self.fin = buffers
        self.red = red
        self.half = count * BLK // 2
        self.size = count * BLK
        self.cols = pl.ds(column, self.fin.shape[1])
        self.pack = pack.at[pl.ds(0, 4 * self.size), self.cols]

    def rows(self, ref, chip, half):
        return ref.at[pl.ds(chip * self.size + half * self.half, self.half)]

    def link(self, name):
        here, k, acc = self.here, self.k, self.acc
        keep = (here.z % 2) * self.half
        other = (1 - here.z % 2) * self.half
        mine = here.chip * self.size
        fin_keep = self.fin.at[pl.ds(keep, self.half)]
        order = (
            "core_xy", "core_x", "core_y", "core_me", "x_far", "x_near", "y_far", "y_near",
            "y_on", "x_on", "z_half", "z_far", "z_back", "share",
        )

        def across(chip):
            rows = pl.ds(chip * self.size, self.size)
            return self.pack.at[rows], acc.at[rows], here.to_core

        src, dst, partner = {
            "core_xy": lambda: across(here.chip_xy),
            "core_x": lambda: across(here.chip_x),
            "core_y": lambda: across(here.chip_y),
            "core_me": lambda: across(here.chip),
            "x_far": lambda: (self.rows(acc, here.chip_xy, 0), self.rx.at[1], here.to_x),
            "x_near": lambda: (self.rows(acc, here.chip_x, 0), self.rx.at[0], here.to_x),
            "y_far": lambda: (self.rows(acc, here.chip_xy, 1), self.ry.at[1], here.to_y),
            "y_near": lambda: (self.rows(acc, here.chip_y, 1), self.ry.at[0], here.to_y),
            "y_on": lambda: (self.rows(acc, here.chip_y, 0), self.r2.at[0], here.to_y),
            "x_on": lambda: (self.rows(acc, here.chip_x, 1), self.r2.at[1], here.to_x),
            "z_half": lambda: (acc.at[pl.ds(mine + other, self.half)], self.z1, here.to_z[0]),
            "z_far": lambda: (acc.at[pl.ds(mine + keep, self.half)], self.z2, here.to_z[1]),
            "z_back": lambda: (fin_keep, fin_keep, here.to_z[0]),
            "share": lambda: (self.fin, self.result(), here.to_core),
        }[name]()
        return self.sender.copy(k + order.index(name), src, dst, partner)

    def result(self):
        return self.red.at[pl.ds((self.first + self.here.core * self.n) * BLK, self.size), self.cols]

    def start_core(self):
        here, n = self.here, self.n
        chips = (here.chip_xy, here.chip_x, here.chip_y, here.chip)
        for chip, name in zip(chips, ("core_xy", "core_x", "core_y", "core_me")):

            def body(i, _):
                block = self.blk[chip * LIST + self.first + (1 - here.core) * n + i]
                self.pack[pl.ds(chip * self.size + i * BLK, BLK), :] = self.grad[block, :, self.cols]
                return 0

            lax.fori_loop(0, n, body, 0)
            self.link(name).start()

    def sent_core(self):
        for name in ("core_xy", "core_x", "core_y", "core_me"):
            self.link(name).wait_send()

    def add_own(self, chip):
        here, n = self.here, self.n

        def body(i, _):
            entry = chip * LIST + self.first + here.core * n + i
            block = self.blk[entry]
            for piece in range(0, BLK, 32):
                rows = pl.ds(pl.multiple_of(chip * self.size + i * BLK, BLK) + piece, 32)
                self.acc[rows, :] = self.acc[rows, :] + self.grad[block, piece : piece + 32, self.cols]
            return 0

        lax.fori_loop(0, n, body, 0)

    def start_far(self):
        self.link("core_xy").wait_recv()
        self.add_own(self.here.chip_xy)
        self.link("x_far").start()
        self.link("y_far").start()

    def start_near(self):
        self.link("core_x").wait_recv()
        self.add_own(self.here.chip_x)
        self.link("x_near").start()
        self.link("core_y").wait_recv()
        self.add_own(self.here.chip_y)
        self.link("y_near").start()

    def pass_plane(self):
        here = self.here
        self.link("x_far").wait_recv()
        at = here.chip_y * self.size
        add_rows(self.acc, at, ((self.acc, at), (self.rx.at[1], 0)), self.half)
        self.link("y_on").start()
        self.link("y_far").wait_recv()
        at = here.chip_x * self.size + self.half
        add_rows(self.acc, at, ((self.acc, at), (self.ry.at[1], 0)), self.half)
        self.link("x_on").start()

    def start_z(self):
        here = self.here
        mine = here.chip * self.size
        self.link("core_me").wait_recv()
        self.add_own(here.chip)
        self.link("x_near").wait_recv()
        self.link("y_on").wait_recv()
        add_rows(self.acc, mine, ((self.acc, mine), (self.rx.at[0], 0), (self.r2.at[0], 0)), self.half)
        self.link("y_near").wait_recv()
        self.link("x_on").wait_recv()
        low = mine + self.half
        add_rows(self.acc, low, ((self.acc, low), (self.ry.at[0], 0), (self.r2.at[1], 0)), self.half)
        self.link("z_half").start()

    def far_z(self):
        here = self.here
        keep = here.chip * self.size + (here.z % 2) * self.half
        self.link("z_half").wait_recv()
        add_rows(self.acc, keep, ((self.acc, keep), (self.z1, 0)), self.half)
        self.link("z_far").start()

    def back_z(self):
        here = self.here
        keep = (here.z % 2) * self.half
        self.link("z_far").wait_recv()
        add_rows(self.fin, keep, ((self.acc, here.chip * self.size + keep), (self.z2, 0)), self.half)
        self.link("z_back").start()

    def share(self, local_sem):
        red = self.result()
        self.link("z_back").wait_recv()
        self.link("z_back").wait_send()
        self.link("share").start()
        pltpu.make_async_copy(self.fin, red, local_sem).start()

    def finish(self, local_sem):
        red = self.result()
        self.link("share").wait_recv()
        pltpu.make_async_copy(self.fin, red, local_sem).wait()
        for name in ("x_far", "x_near", "y_far", "y_near", "y_on", "x_on", "z_half", "z_far", "share"):
            self.link(name).wait_send()


def back_pair(q_ref, k_ref, v_ref, ctx_ref, do_ref, lse_ref, seq, p, bias):
    rows = q_ref.shape[0]
    cols = pl.ds(pl.multiple_of(p * LANES, LANES), LANES)
    row8 = lax.broadcasted_iota(jnp.int32, (16, rows), 0)

    def extra_rows(lead, row):
        one, two, three = (part.astype(jnp.float32) for part in split3(row))
        return jnp.where(
            row8 == 0, lead, jnp.where(row8 == 1, one, jnp.where(row8 == 2, two, jnp.where(row8 == 3, three, 0.0)))
        )

    q2, k2, v2, do2 = q_ref[:, cols], k_ref[:, cols], v_ref[:, cols], do_ref[:, cols]
    q2t, k2t, do2t = q2.T, k2.T, do2.T
    prod = do2t.astype(jnp.float32) * ctx_ref[:, cols].T.astype(jnp.float32)
    dq_parts = []
    d_key = jnp.zeros((rows, LANES), jnp.float32)
    d_value = jnp.zeros((rows, LANES), jnp.float32)
    for half in range(2):
        head = slice(half * DH, half * DH + DH)
        inside, spare = spare_lanes(rows, half, bias)
        zero = jnp.zeros_like(k2)
        lse = lse_ref[seq, pl.ds(2 * p + half, 1), :]
        delta = jnp.sum(prod[head], axis=0, keepdims=True)
        scores = mm(jnp.where(inside, k2, spare), beside(q2t[head], extra_rows(1.0, -lse), half))
        probs = jnp.exp(scores)
        d_probs = mm(jnp.where(inside, v2, spare), beside(do2t[head], extra_rows(0.0, -delta), half))
        d_scores = (probs * d_probs).astype(jnp.bfloat16)
        d_value += mm(probs.astype(jnp.bfloat16), jnp.where(inside, do2, zero))
        d_key += mm(d_scores, jnp.where(inside, q2, zero))
        dq_parts.append(mm(k2t[head], d_scores))
    d_query = jnp.concatenate(dq_parts, axis=0).T * 0.125
    return cols, d_query.astype(jnp.bfloat16), d_key.astype(jnp.bfloat16), d_value.astype(jnp.bfloat16)


def tail_kernel(
    blk_ref, lengths_ref, vec_in, squares_in, lse_ref,
    dctx_in, ctx_split, dbranch, dinner, mid, act, dfeed, tok_in, q_in, k_in, v_in, ctx_in, w_in,
    red, ingrad, vec_out, rms_out,
    grad, pack, d3, att, tok, w, *rest,
):
    here = Place()
    z = here.z
    phase_buffers = [rest[7 * i : 7 * i + 7] for i in range(4)]
    vec_src, vec_land, rms_src, rms_land, send_sem, recv_sem, load_sem = rest[28:]
    sender = Sender(send_sem, recv_sem)
    rows = SEQLEN
    own = dctx_in.shape[0] // 4
    part = dctx_in.shape[1]
    total = own * rows
    wide = D // 2

    def local(src, dst, k):
        return pltpu.make_async_copy(src, dst, load_sem.at[k])

    first_loads = (
        local(ctx_split, att.at[2], 0),
        local(dinner.at[:, pl.ds(0, D)], att.at[3], 1),
        local(dbranch, d3.at[0], 2),
        local(mid, d3.at[1], 3),
        local(dfeed, d3.at[2], 4),
        local(q_in, att.at[0], 5),
        local(k_in, att.at[1], 6),
        local(tok_in, tok, 7),
        local(w_in, w, 10),
    )
    for load in first_loads[:5]:
        load.start()
    here.meet()

    def swap(half, s, hop):
        cols = pl.ds(half * wide, wide)
        return sender.copy(
            6 * half + 3 * s + hop,
            dctx_in.at[own * here.z_hops[hop] + s, :, cols],
            att.at[4, pl.ds(s * rows + part * z, part), cols],
            here.to_z[hop],
        )

    swaps = [[swap(half, s, hop) for s in range(own) for hop in range(3)] for half in range(2)]
    own_swaps = [local(dctx_in.at[own * z + s], att.at[4, pl.ds(s * rows + part * z, part)], 8 + s) for s in range(own)]
    for copy in swaps[0] + own_swaps:
        copy.start()
    for load in first_loads[2:5]:
        load.wait()

    early, middle = (
        Reduce(here, sender, 24 + 14 * i, count // 2, first, 0, blk_ref, grad, pack, phase_buffers[i], red)
        for i, (count, first) in enumerate(((EARLY, 0), (MIDDLE, EARLY)))
    )
    late = [
        Reduce(here, sender, 52 + 14 * i, LATE // 2, EARLY + MIDDLE, i * wide, blk_ref, grad, pack, phase_buffers[2 + i], red)
        for i in range(2)
    ]

    def grads(step, _):
        slot = 2 + step % 2
        held = att.at[slot]
        pltpu.make_async_copy(held, held, load_sem.at[step % 2]).wait()
        value = mm_tn(att[slot], d3[(step + 3) // 4])
        grad[pl.ds(HEAD_BLOCKS + step * (D // BLK), D // BLK)] = value.astype(jnp.bfloat16).reshape(D // BLK, BLK, D)

        @pl.when(step < CHUNKS - 1)
        def _():
            local(dinner.at[:, pl.ds((step + 1) * D, D)], held, step % 2).start()

        @pl.when((step >= CHUNKS - 1) & (step < 2 * CHUNKS - 1))
        def _():
            local(act.at[:, pl.ds((step - CHUNKS + 1) * D, D)], held, step % 2).start()

        @pl.when(step == CHUNKS)
        def _():
            early.start_core()

        @pl.when(step == CHUNKS + 2)
        def _():
            early.start_far()

        @pl.when(step == CHUNKS + 3)
        def _():
            early.start_near()
            for copy in swaps[0]:
                copy.wait_send()
            for copy in swaps[1]:
                copy.start()

        return 0

    for load in first_loads[5:]:
        load.start()
    grad[0:HEAD_BLOCKS] = jnp.zeros((HEAD_BLOCKS, BLK, D), jnp.bfloat16)
    lax.fori_loop(0, 1 + 2 * CHUNKS, grads, 0)
    more_loads = (local(v_in, att.at[2], 0), local(ctx_in, att.at[3], 1))
    for load in more_loads:
        load.start()
    early.sent_core()
    middle.start_core()
    for load in first_loads[5:] + tuple(own_swaps) + more_loads:
        load.wait()
    for copy in swaps[0]:
        copy.wait_recv()

    key = lax.broadcasted_iota(jnp.int32, (rows, 1), 0)

    def head_grads(half):
        cols = pl.ds(half * wide, wide)
        for block, which in ((0, 1), (6, 2), (12, 0)):
            value = mm_tn(tok[...], d3[which, :, cols]).astype(jnp.bfloat16)
            grad[block : block + 6, :, cols] = value.reshape(D // BLK, BLK, wide)

    def send_ingrad(s, hop):
        return sender.copy(
            80 + 3 * s + hop,
            att.at[0, pl.ds(s * rows + part * here.z_hops[hop], part)],
            ingrad.at[own * z + s],
            here.to_z[hop],
        )

    def own_ingrad(s):
        return local(att.at[0, pl.ds(s * rows + part * z, part)], ingrad.at[own * z + s], 11 + s)

    def input_gradient(s):
        at = pl.ds(s * rows, rows)
        value = mm_nt(d3[1, at, :], w[0:D, :])
        value += mm_nt(d3[2, at, :], w[D : 2 * D, :])
        value += mm_nt(d3[0, at, :], w[2 * D :, :])
        att[0, at, :] = value.astype(jnp.bfloat16)
        for hop in range(3):
            send_ingrad(s, hop).start()
        own_ingrad(s).start()

    def second_half():
        for copy in swaps[1]:
            copy.wait_recv()

    group = PAIRS // 2

    def pair_step(i, _):
        s = (i // group) % own
        p = (i // (own * group)) * group + i % group
        bias = jnp.where(key < lengths_ref[own * z + s], 0.0, MASKED)
        at = pl.ds(pl.multiple_of(s * rows, rows), rows)
        cols, d_query, d_key, d_value = back_pair(*(att.at[k, at] for k in range(5)), lse_ref, s, p, bias)
        d3[1, at, cols] = d_query
        d3[2, at, cols] = d_key
        d3[0, at, cols] = d_value

        stages = {
            0: (early.pass_plane,),
            2: (middle.start_far,),
            3: (middle.start_near,),
            4: (early.start_z,),
            5: (lambda: head_grads(0), middle.sent_core, late[0].start_core, second_half),
            6: (early.far_z,),
            7: (middle.pass_plane,),
            8: (late[0].start_far, lambda: input_gradient(0)),
            9: (late[0].start_near,),
            10: (early.back_z,),
            11: (middle.start_z,),
        }
        for at_step, calls in stages.items():

            @pl.when(i == at_step)
            def _():
                for call in calls:
                    call()

        return 0

    lax.fori_loop(0, own * PAIRS, pair_step, 0)

    head_grads(1)
    late[1].start_core()
    vec_src[0] = vec_in[...]
    vec_src[0, 0:1, :] = jnp.sum(d3[1].astype(jnp.float32), axis=0, keepdims=True)
    vec_src[0, 1:2, :] = jnp.sum(d3[0].astype(jnp.float32), axis=0, keepdims=True)
    for i in range(squares_in.shape[0]):
        sums = jnp.sum(squares_in[i], axis=-1, keepdims=True)
        rms_src[0, 8 * i : 8 * i + 8, :] = jnp.broadcast_to(sums, (8, LANES))
    ways = (here.to_z[0], here.to_z[1], here.to_core, here.to_x, here.to_y)
    vec_copies = [sender.copy(12 + w, vec_src.at[w], vec_land.at[w], way) for w, way in enumerate(ways)]
    rms_copies = [sender.copy(17 + w, rms_src.at[w], rms_land.at[w], ways[w]) for w in range(2)]

    def vec_step(w):
        if w > 0:
            vec_copies[w - 1].wait_recv()
            after = vec_src[w - 1] + vec_land[w - 1]
            if w < len(ways):
                vec_src[w] = after
            else:
                vec_out[...] = after
        if w < len(ways):
            vec_copies[w].start()
        if 0 < w <= 2:
            rms_copies[w - 1].wait_recv()
            after = rms_src[w - 1] + rms_land[w - 1]
            if w < 2:
                rms_src[w] = after
            else:
                lane = lax.broadcasted_iota(jnp.int32, (1, LANES), 1)
                tiles = squares_in.shape[0]
                each = dctx_in.shape[0] // tiles
                for n in range(dctx_in.shape[0]):
                    row = 8 * (n // each) + 2 * (n % each)
                    sums = jnp.where(lane == 0, after[row : row + 1], after[row + 1 : row + 2])
                    rms_out[n : n + 1, :] = jnp.sqrt(sums / (lengths_ref[n].astype(jnp.float32) * D))
        if w < 2:
            rms_copies[w].start()

    late[0].pass_plane()
    vec_step(0)
    late[1].start_far()
    middle.far_z()
    late[1].start_near()
    input_gradient(1)
    vec_step(1)
    late[1].pass_plane()
    late[0].start_z()
    early.share(load_sem.at[13])
    vec_step(2)
    late[0].far_z()
    late[1].start_z()
    vec_step(3)
    late[1].far_z()
    middle.back_z()
    late[0].back_z()
    vec_step(4)
    middle.share(load_sem.at[14])
    late[0].share(load_sem.at[15])
    vec_step(5)
    late[1].back_z()
    late[1].share(load_sem.at[16])
    for phase in late:
        phase.sent_core()
    for i, phase in enumerate((early, middle, late[0], late[1])):
        phase.finish(load_sem.at[13 + i])
    for copy in swaps[1] + vec_copies + rms_copies:
        copy.wait_send()
    for s in range(own):
        own_ingrad(s).wait()
        for hop in range(3):
            send_ingrad(s, hop).wait_recv()
            send_ingrad(s, hop).wait_send()


def tail(blk, lengths, vec, squares, lse, d_ctx, ctx_split, d_branch, d_inner, mid, act, d_feed, tokens, q, k, v, ctx, w):
    total = tokens.shape[0]
    any_spec = pl.BlockSpec(memory_space=pl.ANY)
    vmem = pl.BlockSpec(memory_space=pltpu.VMEM)
    smem = pl.BlockSpec(memory_space=pltpu.SMEM)
    low = jnp.bfloat16
    sums = (8 * squares.shape[0], LANES)

    def phase(n, width):
        half = n * BLK // 2
        return [
            pltpu.VMEM((4 * n * BLK, width), low),
            pltpu.VMEM((2, half, width), low),
            pltpu.VMEM((2, half, width), low),
            pltpu.VMEM((2, half, width), low),
            pltpu.VMEM((half, width), low),
            pltpu.VMEM((half, width), low),
            pltpu.VMEM((n * BLK, width), low),
        ]

    return pl.pallas_call(
        tail_kernel,
        in_specs=[smem] * 2 + [vmem] * 3 + [any_spec] * 13,
        out_specs=[any_spec] * 2 + [vmem] * 2,
        out_shape=[
            jax.ShapeDtypeStruct((LIST * BLK, D), low),
            jax.ShapeDtypeStruct(d_ctx.shape, low),
            jax.ShapeDtypeStruct(vec.shape, jnp.float32),
            jax.ShapeDtypeStruct((d_ctx.shape[0], LANES), jnp.float32),
        ],
        scratch_shapes=[
            pltpu.VMEM((HEAD_BLOCKS + (D + 2 * FF) // BLK, BLK, D), low),
            pltpu.VMEM((2 * max(EARLY, MIDDLE, LATE) * BLK, D), low),
            pltpu.VMEM((3, total, D), low),
            pltpu.VMEM((5, total, D), low),
            pltpu.VMEM((total, D), low),
            pltpu.VMEM((3 * D, D), low),
        ]
        + phase(EARLY // 2, D)
        + phase(MIDDLE // 2, D)
        + phase(LATE // 2, D // 2)
        + phase(LATE // 2, D // 2)
        + [
            pltpu.VMEM((5,) + vec.shape, jnp.float32),
            pltpu.VMEM((5,) + vec.shape, jnp.float32),
            pltpu.VMEM((2,) + sums, jnp.float32),
            pltpu.VMEM((2,) + sums, jnp.float32),
            pltpu.SemaphoreType.DMA((86,)),
            pltpu.SemaphoreType.DMA((86,)),
            pltpu.SemaphoreType.DMA((17,)),
        ],
        compiler_params=pltpu.CompilerParams(
            vmem_limit_bytes=63 * MIB, collective_id=1, has_side_effects=True
        ),
        cost_estimate=pl.CostEstimate(
            flops=2 * total * D * (6 * D + 2 * FF) + 10 * total * SEQLEN * D,
            bytes_accessed=total * (24 * D + 4 * FF) + 8 * FF * D,
            transcendentals=total * SEQLEN * H,
        ),
        name="tail",
    )(blk, lengths, vec, squares, lse, d_ctx, ctx_split, d_branch, d_inner, mid, act, d_feed, tokens, q, k, v, ctx, w)


def tables_kernel(owner_ref, place_ref, mine_ref, block_ref, spot_ref, has_ref, fits_ref, *, slots):
    dp = lax.axis_index("dp")
    chip_slots = 2 * slots
    near_blocks = HEAD_BLOCKS + (D + FF) // BLK
    for ref in (mine_ref, block_ref, spot_ref, has_ref):
        for i in range(ref.shape[0]):
            ref[i] = 0

    def body(b, counts):
        listed, early, middle, late, bad = counts
        slot = owner_ref[b]
        chip = slot // chip_slots
        shift = 8 * chip
        one = jnp.left_shift(1, shift)

        def count(packed):
            return jnp.right_shift(packed, shift) & 255

        order = count(listed)
        n_early, n_middle, n_late = count(early), count(middle), count(late)
        body_block = b >= HEAD_BLOCKS
        in_early = body_block & (b < near_blocks) & (n_early < EARLY)
        in_middle = body_block & jnp.logical_not(in_early) & (n_middle < MIDDLE)
        in_late = jnp.logical_not(in_early | in_middle)
        spot = jnp.where(in_early, n_early, jnp.where(in_middle, EARLY + n_middle, EARLY + MIDDLE + n_late))
        wrong = (order >= LIST) | (spot >= LIST) | (jnp.logical_not(body_block) & (order >= FIRST))
        spot = jnp.minimum(spot, LIST - 1)
        place_ref[b] = chip * LIST + jnp.minimum(order, LIST - 1)
        block_ref[chip * LIST + spot] = b

        @pl.when(chip == dp // 2)
        def _():
            mine_ref[jnp.minimum(order, LIST - 1)] = slot - chip * chip_slots

            @pl.when(slot // slots == dp)
            def _():
                spot_ref[slot % slots] = spot
                has_ref[slot % slots] = 1

        return (
            listed + one,
            early + jnp.where(in_early, one, 0),
            middle + jnp.where(in_middle, one, 0),
            late + jnp.where(in_late, one, 0),
            bad | wrong.astype(jnp.int32),
        )

    zero = jnp.int32(0)
    counts = lax.fori_loop(0, owner_ref.shape[0], body, (zero,) * 5, unroll=4)
    fits_ref[0] = 1 - counts[4]


def tables(owner, slots):
    chips = lax.axis_size("dp") // 2
    smem = pl.BlockSpec(memory_space=pltpu.SMEM)
    sizes = (owner.shape[0], LIST, chips * LIST, slots, slots, 1)
    return pl.pallas_call(
        partial(tables_kernel, slots=slots),
        in_specs=[smem],
        out_specs=[smem] * len(sizes),
        out_shape=[jax.ShapeDtypeStruct((n,), jnp.int32) for n in sizes],
        name="tables",
    )(owner)


def general(tokens, cotangent, lengths, owner, master, vec_master):
    slot_local = master.shape[0]
    gathered = lax.all_gather(master.astype(jnp.bfloat16), "dp", axis=0, tiled=True)
    seq_place = lax.axis_index("seq")
    slot_total = slot_local * lax.axis_size("dp")
    tokens = to_whole(tokens, "seq")
    cotangent = to_whole(cotangent, "seq")
    seq_count, seq_len, width = tokens.shape
    token_count = seq_count * seq_len
    lengths = lax.dynamic_slice_in_dim(lengths, seq_place * seq_count, seq_count)
    q, k, v, ctx, lse, _ = attend(owner, lengths, tokens, gathered, vec_master)
    flat = tokens.reshape(token_count, D)
    _, mid, out, act, d_inner, d_feed, d_branch, d_res, d_ctx, vec_feed, squares = feed_both(
        owner, lengths, seq_len,
        flat, ctx, cotangent.reshape(token_count, D), gathered, vec_master,
    )
    held = feed_grads(owner, slot_total, ctx, d_branch, d_inner, mid, act, d_feed)
    ingrad, vec_attend, held = attend_back(
        owner, owner, lengths, tokens, q, k, v, ctx, d_ctx, lse, d_res, gathered, held
    )
    local_sums = jnp.sum(squares.reshape(seq_count, -1, 8, D)[:, :, :2], axis=(1, 3))
    own_rms = jnp.sqrt(local_sums / (lengths[:, None].astype(jnp.float32) * D))
    sublayer_rms = lax.all_gather(own_rms, "seq", axis=0, tiled=True)
    vec_local = jnp.concatenate([vec_attend[:2], vec_feed[2:12]], axis=0)
    vec_grad = lax.psum(vec_local, ("dp", "seq"))
    owned = lax.psum_scatter(held, "dp", scatter_dimension=0, tiled=True)
    reduced = lax.psum(owned, "seq")
    first_slot = lax.axis_index("dp") * slot_local
    slots = jnp.arange(slot_local, dtype=jnp.int32)
    has = jnp.any((first_slot + slots)[:, None] == owner[None, :], axis=1).astype(jnp.int32)
    whole = (seq_count, seq_len, D)
    return (
        to_split(out.reshape(whole), "seq"),
        jnp.zeros((token_count, D), jnp.float32),
        to_split(ingrad.reshape(whole), "seq").reshape(token_count, D),
        to_split(mid.reshape(whole), "seq").astype(jnp.float32),
        jnp.pad(sublayer_rms, ((0, 0), (0, LANES - 2))),
        jnp.pad(vec_grad, ((0, 4), (0, 0))),
        reduced,
        slots,
        has,
    )


def listed(tokens, cotangent, lengths, owner, master, vec_master, place, mine, block, spot, has):
    seqs, part, _ = tokens.shape
    total = seqs * part
    pool, q, k, v, ctx, w, whole, ctx_split, lse = front(
        place, mine, lengths, vec_master, master, tokens
    )
    ctx_split = ctx_split.reshape(total, D)
    wide_mid, mid, out, act, d_inner, d_feed, d_branch, d_res, d_ctx, vec_feed, squares = feed_both(
        place, lengths, part,
        tokens.reshape(total, D), ctx_split, cotangent.reshape(total, D), pool.reshape(-1, BLK, D), vec_master,
    )
    reduced, ingrad, vec_grad, rms = tail(
        block, lengths, vec_feed, squares, lse, d_ctx.reshape(seqs, part, D), ctx_split, d_branch, d_inner,
        mid, act, d_feed, whole, q, k, v, ctx, w,
    )
    return (
        out.reshape(tokens.shape),
        d_res,
        ingrad.reshape(total, D),
        wide_mid.reshape(tokens.shape),
        rms,
        vec_grad,
        reduced.reshape(LIST, BLK, D),
        spot,
        has,
    )


def per_device(
    tokens, cotangent, lengths, owner, master, moment, second, vec_master, vec_moment, vec_second
):
    slot_local = master.shape[0]
    given = (tokens, cotangent, lengths, owner, master, vec_master)
    if lax.axis_size("dp") == 8 and lax.axis_size("seq") == 4:
        place, mine, block, spot, has, fits = tables(owner, slot_local)

        def otherwise(*args):
            results = general(*args[:6])
            pad = ((0, LIST - slot_local), (0, 0), (0, 0))
            return results[:6] + (jnp.pad(results[6], pad),) + results[7:]

        results = lax.cond(fits[0] > 0, listed, otherwise, *given, place, mine, block, spot, has)
    else:
        results = general(*given)
    layer_out, d_res, ingrad, residual_mid, rms, vec_grad, reduced, spot, has = results
    updated = adam_all(
        spot, has, reduced, moment, second, master,
        d_res, ingrad, rms, vec_grad, vec_moment, vec_second, vec_master,
    )
    input_grad, sublayer_rms, slots, vectors = updated[0], updated[1], updated[2:6], updated[6:]
    return (layer_out, input_grad.reshape(tokens.shape), residual_mid, sublayer_rms, *slots, *vectors)


def solution(mesh):
    return jax.shard_map(
        per_device,
        mesh=mesh,
        in_specs=(
            P("dp", "seq", None),
            P("dp", "seq", None),
            P("dp"),
            P(),
            P("dp", None, None),
            P("dp", None, None),
            P("dp", None, None),
            P(),
            P(),
            P(),
        ),
        out_specs=(
            P("dp", "seq", None),
            P("dp", "seq", None),
            P("dp", "seq", None),
            P("dp", None),
            P("dp", None, None),
            P("dp", None, None),
            P("dp", None, None),
            P("dp", None, None),
            P(),
            P(),
            P(),
            P(),
        ),
        check_vma=False,
    )
```

```python
from functools import partial

import jax
import jax.numpy as jnp
from jax import lax
from jax.experimental import pallas as pl
from jax.experimental.pallas import tpu as pltpu
from jax.sharding import PartitionSpec as P

D = 768
H = 12
DH = 64
FF = 3072
BLK = 128
SEQLEN = 512
STEP = 5


first_decay = 0.5
second_decay = 0.5
matrix_rate = 0.02
vector_rate = 0.2
weight_decay = 0.01
adam_epsilon = 1e-08


def adam_step(gradient, moment, second, weight, rate):
    moment_new = first_decay * moment + (1.0 - first_decay) * gradient
    second_new = second_decay * second + (1.0 - second_decay) * gradient * gradient
    moment_hat = moment_new * (1.0 / (1.0 - first_decay**STEP))
    second_hat = second_new * (1.0 / (1.0 - second_decay**STEP))
    root = second_hat * lax.rsqrt(second_hat) + adam_epsilon
    inverse = pltpu.reciprocal(root, approx=True)
    inverse = inverse * (2.0 - root * inverse)
    weight_new = weight - rate * (moment_hat * inverse + weight_decay * weight)
    return (moment_new, second_new, weight_new)


def seq_swap(parts, axis):
    size = lax.axis_size(axis)
    me = lax.axis_index(axis)
    stacked = parts
    got = [None] * size
    mine = lax.dynamic_index_in_dim(stacked, me, 0, keepdims=False)
    out = [mine]
    for hop in range(1, size):
        there = jnp.bitwise_xor(me, hop)
        piece = lax.dynamic_index_in_dim(stacked, there, 0, keepdims=False)
        route = [(i, i ^ hop) for i in range(size)]
        out.append(lax.ppermute(piece, axis, route))
    return out


def from_hops(pieces, axis):
    size = lax.axis_size(axis)
    me = lax.axis_index(axis)
    stacked = jnp.stack(pieces, axis=0)
    order = jnp.bitwise_xor(jnp.arange(size, dtype=jnp.int32), me)
    return jnp.take(stacked, order, axis=0)


def to_whole(block, axis):
    size = lax.axis_size(axis)
    count, length, width = block.shape
    pieces = seq_swap(block.reshape(size, count // size, length, width), axis)
    stacked = from_hops(pieces, axis)
    return jnp.swapaxes(stacked, 0, 1).reshape(count // size, size * length, width)


def to_split(whole, axis):
    size = lax.axis_size(axis)
    own, full, width = whole.shape
    parts = jnp.swapaxes(whole.reshape(own, size, full // size, width), 0, 1)
    pieces = seq_swap(parts, axis)
    return from_hops(pieces, axis).reshape(size * own, full // size, width)


LANES = 128
PAIRS = D // LANES
CHUNKS = FF // D
MASKED = -1e30
NT = (((1,), (1,)), ((), ()))
TN = (((0,), (0,)), ((), ()))
MIB = 1 << 20


def mm(left, right):
    return jnp.dot(left, right, preferred_element_type=jnp.float32)


def mm_nt(left, right):
    return lax.dot_general(left, right, NT, preferred_element_type=jnp.float32)


def mm_tn(left, right):
    return lax.dot_general(left, right, TN, preferred_element_type=jnp.float32)


def load_blocks(pool_ref, place_ref, first, into_ref, sem):
    def start(i, _):
        pltpu.make_async_copy(
            pool_ref.at[place_ref[first + i]], into_ref.at[pl.ds(i * BLK, BLK)], sem
        ).start()
        return 0

    lax.fori_loop(0, into_ref.shape[0] // BLK, start, 0)


def wait_whole(ref, sem):
    pltpu.make_async_copy(ref, ref, sem).wait()


def spare_lanes(rows, half, bias_column):
    lane = lax.broadcasted_iota(jnp.int32, (rows, LANES), 1)
    first = DH * (1 - half)
    spare = jnp.where(lane == first, bias_column, jnp.where(lane < first + 4, 1.0, 0.0))
    inside = (lane >= DH * half) & (lane < DH * half + DH)
    return inside, spare.astype(jnp.bfloat16)


def split3(row):
    one = row.astype(jnp.bfloat16)
    rest = row - one.astype(jnp.float32)
    two = rest.astype(jnp.bfloat16)
    three = (rest - two.astype(jnp.float32)).astype(jnp.bfloat16)
    return one, two, three


def beside(head_rows, extra, half):
    columns = head_rows.shape[1]
    pad = jnp.zeros((DH - extra.shape[0], columns), jnp.bfloat16)
    parts = [extra.astype(jnp.bfloat16), pad]
    order = [head_rows] + parts if half == 0 else parts + [head_rows]
    return jnp.concatenate(order, axis=0)


def forward_pair(q_ref, k_ref, v_ref, ctx_ref, lse_ref, seq, p, bias):
    rows = q_ref.shape[0]
    cols = pl.ds(pl.multiple_of(p * LANES, LANES), LANES)
    row8 = lax.broadcasted_iota(jnp.int32, (16, rows), 0)
    q2t = q_ref[:, cols].T
    k2 = k_ref[:, cols]
    v2t = v_ref[:, cols].T
    outs = []
    for half in range(2):
        inside, spare = spare_lanes(rows, half, bias)
        k_aug = jnp.where(inside, k2, spare)
        head = slice(half * DH, half * DH + DH)
        q_aug = beside(q2t[head], jnp.where(row8 == 0, 1.0, 0.0), half)
        scores = mm(k_aug, q_aug)
        top = jnp.max(scores, axis=0, keepdims=True)
        expos = jnp.exp(scores - top).astype(jnp.bfloat16)
        v_aug = jnp.concatenate([v2t[head], jnp.ones((16, rows), jnp.bfloat16)], axis=0)
        both = mm(v_aug, expos)
        total = both[DH : DH + 1]
        outs.append(both[0:DH] / total)
        lse_ref[seq, pl.ds(2 * p + half, 1), :] = top + jnp.log(total)
    ctx_ref[:, cols] = jnp.concatenate(outs, axis=0).T.astype(jnp.bfloat16)


def attend_kernel(
    place_ref, lengths_ref, tokens_ref, pool_ref, vec_ref,
    q_ref, k_ref, v_ref, ctx_ref, lse_ref, w_scr,
    sem,
):
    seq = pl.program_id(0)
    rows = tokens_ref.shape[0]

    @pl.when(seq == 0)
    def _():
        load_blocks(pool_ref, place_ref, 0, w_scr, sem)
        wait_whole(w_scr, sem)

    tokens = tokens_ref[...]
    q_ref[...] = ((mm(tokens, w_scr[0:D, :]) + vec_ref[0:1, :]).astype(jnp.bfloat16) * 0.125).astype(jnp.bfloat16)
    k_ref[...] = mm(tokens, w_scr[D : 2 * D, :]).astype(jnp.bfloat16)
    v_ref[...] = (mm(tokens, w_scr[2 * D :, :]) + vec_ref[1:2, :]).astype(jnp.bfloat16)
    key = lax.broadcasted_iota(jnp.int32, (rows, 1), 0)
    bias = jnp.where(key < lengths_ref[seq], 0.0, MASKED)

    def pair(p, _):
        forward_pair(q_ref, k_ref, v_ref, ctx_ref, lse_ref, 0, p, bias)
        return 0

    lax.fori_loop(0, PAIRS, pair, 0)


def attend(place, lengths, tokens, pool, vec):
    seqs, rows, _ = tokens.shape
    flat = tokens.reshape(seqs * rows, D)
    row_spec = pl.BlockSpec((rows, D), lambda s, *_: (s, 0))
    any_spec = pl.BlockSpec(memory_space=pl.ANY)
    low = jax.ShapeDtypeStruct((seqs * rows, D), jnp.bfloat16)
    return pl.pallas_call(
        attend_kernel,
        grid_spec=pltpu.PrefetchScalarGridSpec(
            num_scalar_prefetch=2,
            grid=(seqs,),
            in_specs=[row_spec, any_spec, pl.BlockSpec(vec.shape, lambda s, *_: (0, 0))],
            out_specs=[row_spec] * 4
            + [
                pl.BlockSpec((1, 16, rows), lambda s, *_: (s, 0, 0)),
                pl.BlockSpec((3 * D, D), lambda s, *_: (0, 0)),
            ],
            scratch_shapes=[pltpu.SemaphoreType.DMA],
        ),
        out_shape=[low] * 4
        + [
            jax.ShapeDtypeStruct((seqs, 16, rows), jnp.float32),
            jax.ShapeDtypeStruct((3 * D, D), jnp.bfloat16),
        ],
        compiler_params=pltpu.CompilerParams(vmem_limit_bytes=48 * MIB),
        cost_estimate=pl.CostEstimate(
            flops=6 * seqs * rows * D * D + 4 * seqs * rows * rows * D,
            bytes_accessed=10 * seqs * rows * D + 6 * D * D,
            transcendentals=seqs * rows * rows * H,
        ),
        name="attend",
    )(place, lengths, flat, pool, vec)


def gelu_parts(x):
    t_in = 1.0 + (0.3275911 * 0.7071067811865476) * jnp.abs(x)
    t = pltpu.reciprocal(t_in, approx=True)
    t = t * (2.0 - t_in * t)
    e = jnp.exp2((-0.5 * 1.4426950408889634) * (x * x))
    poly = (0.5 * 1.061405429) * t - (0.5 * 1.453152027)
    poly = poly * t + (0.5 * 1.421413741)
    poly = poly * t - (0.5 * 0.284496736)
    poly = poly * t + (0.5 * 0.254829592)
    tail = (poly * t) * e
    dist = jnp.where(x >= 0, 1.0 - tail, tail)
    return dist, x * (e * 0.3989422804014327)


def norm_stats(resid):
    center = resid - jnp.mean(resid, axis=-1, keepdims=True)
    scale = lax.rsqrt(jnp.mean(center * center, axis=-1, keepdims=True) + 1e-05)
    return center * scale, scale


def norm_back(d_out, gain, hat, scale):
    d_hat = d_out * gain
    mean_one = jnp.mean(d_hat, axis=-1, keepdims=True)
    mean_hat = jnp.mean(d_hat * hat, axis=-1, keepdims=True)
    return scale * (d_hat - mean_one - hat * mean_hat)


def feed_kernel(
    place_ref, lengths_ref, tokens_ref, ctx_ref, cot_ref, pool_ref, vec_ref,
    wide_mid_ref, mid_ref, out_ref, act_ref, dinner_ref, dfeed_ref, dbranch_ref, dres_ref, dctx_ref, grad_ref, sq_ref,
    w_out, w_up, w_down, slope_scr, sem, *, seq_rows,
):
    step = pl.program_id(0)
    rows = tokens_ref.shape[0]
    tiles = sq_ref.shape[0]
    first = 3 * D // BLK

    @pl.when(step == 0)
    def _():
        load_blocks(pool_ref, place_ref, first, w_out, sem.at[0])
        load_blocks(pool_ref, place_ref, first + D // BLK, w_up, sem.at[1])
        load_blocks(pool_ref, place_ref, first + (D + FF) // BLK, w_down, sem.at[2])
        wait_whole(w_out, sem.at[0])
        grad_ref[...] = jnp.zeros_like(grad_ref)

    def add_row(row, value):
        grad_ref[row : row + 1, :] += jnp.sum(value, axis=0, keepdims=True)

    segment = min(rows, seq_rows)
    row = lax.broadcasted_iota(jnp.int32, (rows, 1), 0)
    length = jnp.zeros((rows, 1), jnp.int32)
    for j in range(rows // segment):
        length = jnp.where(row // segment == j, lengths_ref[(step * rows + j * segment) // seq_rows], length)
    place_in = (step * rows + row) % seq_rows
    if seq_rows < SEQLEN:
        place_in += lax.axis_index("seq") * seq_rows
    valid = (place_in < length).astype(jnp.float32)

    def square_sums(which, value):
        square = value * value * valid
        for j in range(rows // segment):
            sq_ref[0, 2 * j + which : 2 * j + which + 1, :] = jnp.sum(
                square[j * segment : (j + 1) * segment], axis=0, keepdims=True
            )

    branch = mm(ctx_ref[...], w_out[...]) + vec_ref[2:3, :]
    square_sums(0, branch)
    hat1, scale1 = norm_stats(tokens_ref[...].astype(jnp.float32) + branch)
    middle = hat1 * vec_ref[4:5, :] + vec_ref[5:6, :]
    wide_mid_ref[...] = middle
    mid_ref[...] = middle.astype(jnp.bfloat16)
    mid_low = mid_ref[...]

    @pl.when(step == 0)
    def _():
        wait_whole(w_up, sem.at[1])

    width = D // 2
    count = FF // width
    parts = [slice(c * width, (c + 1) * width) for c in range(count)]

    def vec_part(c):
        return (slice(8 + c // 2, 9 + c // 2), slice((c % 2) * width, (c % 2 + 1) * width))

    def up(c):
        return mm_nt(mid_low, w_up[parts[c], :])

    def bend(c, inner):
        inner = inner + vec_ref[vec_part(c)]
        dist, bell = gelu_parts(inner)
        act = (inner * dist).astype(jnp.bfloat16)
        act_ref[:, parts[c]] = act
        slope_scr[:, parts[c]] = dist + bell

    for c in range(count):
        bend(c, up(c))

    @pl.when(step == 0)
    def _():
        wait_whole(w_down, sem.at[2])

    feed = mm(act_ref[...], w_down[...]) + vec_ref[3:4, :]
    square_sums(1, feed)
    hat2, scale2 = norm_stats(middle + feed)
    gain2 = vec_ref[6:7, :]
    out_ref[...] = (hat2 * gain2 + vec_ref[7:8, :]).astype(jnp.bfloat16)
    upstream = cot_ref[...].astype(jnp.float32) * valid
    add_row(6, upstream * hat2)
    add_row(7, upstream)
    d_res2 = norm_back(upstream, gain2, hat2, scale2)
    d_feed = d_res2.astype(jnp.bfloat16)
    dfeed_ref[...] = d_feed
    add_row(3, d_feed.astype(jnp.float32))
    d_mid = d_res2
    for c in range(count):
        d_inner = (mm_nt(d_feed, w_down[parts[c], :]) * slope_scr[:, parts[c]]).astype(jnp.bfloat16)
        dinner_ref[:, parts[c]] = d_inner
        grad_ref[vec_part(c)] += jnp.sum(d_inner.astype(jnp.float32), axis=0, keepdims=True)
    d_mid = d_res2 + mm(dinner_ref[...], w_up[...])
    add_row(4, d_mid * hat1)
    add_row(5, d_mid)
    d_res1 = norm_back(d_mid, vec_ref[4:5, :], hat1, scale1)
    dres_ref[...] = d_res1
    d_branch = d_res1.astype(jnp.bfloat16)
    dbranch_ref[...] = d_branch
    add_row(2, d_branch.astype(jnp.float32))
    dctx_ref[...] = mm_nt(d_branch, w_out[...]).astype(jnp.bfloat16)


def feed_both(place, lengths, seq_rows, tokens, ctx, cot, pool, vec, tile=256):
    total = tokens.shape[0]
    steps = total // tile
    row_spec = pl.BlockSpec((tile, D), lambda s, *_: (s, 0))
    wide_spec = pl.BlockSpec((tile, FF), lambda s, *_: (s, 0))
    any_spec = pl.BlockSpec(memory_space=pl.ANY)
    low = jax.ShapeDtypeStruct((total, D), jnp.bfloat16)
    wide = jax.ShapeDtypeStruct((total, FF), jnp.bfloat16)
    return pl.pallas_call(
        partial(feed_kernel, seq_rows=seq_rows),
        grid_spec=pltpu.PrefetchScalarGridSpec(
            num_scalar_prefetch=2,
            grid=(steps,),
            in_specs=[row_spec] * 3 + [any_spec, pl.BlockSpec(vec.shape, lambda s, *_: (0, 0))],
            out_specs=[row_spec, row_spec, row_spec, wide_spec, wide_spec, row_spec, row_spec, row_spec, row_spec,
                pl.BlockSpec((16, D), lambda s, *_: (0, 0)),
                pl.BlockSpec((1, 8, D), lambda s, *_: (s, 0, 0))],
            scratch_shapes=[
                pltpu.VMEM((D, D), jnp.bfloat16),
                pltpu.VMEM((FF, D), jnp.bfloat16),
                pltpu.VMEM((FF, D), jnp.bfloat16),
                pltpu.VMEM((tile, FF), jnp.float32),
                pltpu.SemaphoreType.DMA((3,)),
            ],
        ),
        out_shape=[jax.ShapeDtypeStruct((total, D), jnp.float32), low, low, wide, wide, low, low, jax.ShapeDtypeStruct((total, D), jnp.float32), low,
            jax.ShapeDtypeStruct((16, D), jnp.float32),
            jax.ShapeDtypeStruct((steps, 8, D), jnp.float32)],
        compiler_params=pltpu.CompilerParams(vmem_limit_bytes=62 * MIB),
        cost_estimate=pl.CostEstimate(
            flops=8 * total * D * FF + 4 * total * D * D,
            bytes_accessed=total * (16 * D + 4 * FF) + 12 * FF * D,
            transcendentals=total * FF,
        ),
        name="feed_both",
    )(place, lengths, tokens, ctx, cot, pool, vec)


def send_blocks(value, held, slot, first, place_ref, out_ref, sem):
    held[slot] = value.astype(jnp.bfloat16).reshape(D // BLK, BLK, D)
    for i in range(D // BLK):
        pltpu.make_async_copy(
            held.at[slot, i], out_ref.at[place_ref[first + i]], sem.at[slot]
        ).start()


def feed_grads_kernel(
    place_ref, ctx_ref, dbranch_ref, dinner_ref, mid_ref, act_ref, dfeed_ref, out_ref, held, sem
):
    step = pl.program_id(0)
    slot = lax.rem(step, 2)
    base = 3 * D // BLK

    @pl.when(step >= 2)
    def _():
        wait_whole(held.at[slot], sem.at[slot])

    first = base + step * (D // BLK)

    @pl.when(step == 0)
    def _():
        send_blocks(mm_tn(ctx_ref[...], dbranch_ref[...]), held, slot, first, place_ref, out_ref, sem)

    @pl.when((step >= 1) & (step <= CHUNKS))
    def _():
        send_blocks(mm_tn(dinner_ref[...], mid_ref[...]), held, slot, first, place_ref, out_ref, sem)

    @pl.when(step > CHUNKS)
    def _():
        send_blocks(mm_tn(act_ref[...], dfeed_ref[...]), held, slot, first, place_ref, out_ref, sem)

    @pl.when(step == 2 * CHUNKS)
    def _():
        wait_whole(held.at[slot], sem.at[slot])
        wait_whole(held.at[1 - slot], sem.at[1 - slot])


def feed_grads(place, places, ctx, d_branch, d_inner, mid, act, d_feed):
    total = ctx.shape[0]
    whole = pl.BlockSpec((total, D), lambda s, *_: (0, 0))
    return pl.pallas_call(
        feed_grads_kernel,
        grid_spec=pltpu.PrefetchScalarGridSpec(
            num_scalar_prefetch=1,
            grid=(1 + 2 * CHUNKS,),
            in_specs=[
                whole,
                whole,
                pl.BlockSpec((total, D), lambda s, *_: (0, jnp.clip(s - 1, 0, CHUNKS - 1))),
                whole,
                pl.BlockSpec((total, D), lambda s, *_: (0, jnp.clip(s - 1 - CHUNKS, 0, CHUNKS - 1))),
                whole,
            ],
            out_specs=pl.BlockSpec(memory_space=pl.ANY),
            scratch_shapes=[
                pltpu.VMEM((2, D // BLK, BLK, D), jnp.bfloat16),
                pltpu.SemaphoreType.DMA((2,)),
            ],
        ),
        out_shape=jax.ShapeDtypeStruct((places, BLK, D), jnp.bfloat16),
        compiler_params=pltpu.CompilerParams(vmem_limit_bytes=48 * MIB),
        cost_estimate=pl.CostEstimate(
            flops=4 * total * D * FF + 2 * total * D * D,
            bytes_accessed=total * (8 * D + 4 * FF) + 4 * FF * D,
            transcendentals=0,
        ),
        name="feed_grads",
    )(place, ctx, d_branch, d_inner, mid, act, d_feed)


def attend_back_kernel(
    place_w_ref, place_ref, lengths_ref, tokens_ref, q_ref, k_ref, v_ref, ctx_ref, dctx_ref, lse_ref, dres_ref, pool_ref, held_in,
    ingrad_ref, vec_ref, out_ref,
    w_scr, dq_scr, dk_scr, dv_scr, total_scr, held, sem, w_sem,
):
    seq = pl.program_id(0)
    last = pl.num_programs(0) - 1
    rows = tokens_ref.shape[0]

    @pl.when(seq == 0)
    def _():
        load_blocks(pool_ref, place_w_ref, 0, w_scr, w_sem)
        vec_ref[...] = jnp.zeros_like(vec_ref)

    key = lax.broadcasted_iota(jnp.int32, (rows, 1), 0)
    bias = jnp.where(key < lengths_ref[seq], 0.0, MASKED)

    def pair(p, _):
        cols, d_query, d_key, d_value = back_pair(q_ref, k_ref, v_ref, ctx_ref, dctx_ref, lse_ref, 0, p, bias)
        dq_scr[:, cols] = d_query
        dk_scr[:, cols] = d_key
        dv_scr[:, cols] = d_value
        return 0

    lax.fori_loop(0, PAIRS, pair, 0)

    @pl.when(seq == 0)
    def _():
        wait_whole(w_scr, w_sem)

    dq, dk, dv = dq_scr[...], dk_scr[...], dv_scr[...]
    vec_ref[0:1, :] += jnp.sum(dq.astype(jnp.float32), axis=0, keepdims=True)
    vec_ref[1:2, :] += jnp.sum(dv.astype(jnp.float32), axis=0, keepdims=True)
    ingrad = dres_ref[...] + mm_nt(dq, w_scr[0:D, :])
    ingrad += mm_nt(dk, w_scr[D : 2 * D, :])
    ingrad += mm_nt(dv, w_scr[2 * D :, :])
    ingrad_ref[...] = ingrad.astype(jnp.bfloat16)
    tokens = tokens_ref[...]
    for i, right in enumerate((dq, dk, dv)):
        part = slice(i * D, (i + 1) * D)

        @pl.when(seq == 0)
        def _():
            total_scr[part, :] = mm_tn(tokens, right)

        @pl.when(seq > 0)
        def _():
            total_scr[part, :] += mm_tn(tokens, right)

    @pl.when(seq == last)
    def _():
        for i in range(3):
            send_blocks(total_scr[i * D : (i + 1) * D, :], held, i, i * (D // BLK), place_ref, out_ref, sem)
        for i in range(3):
            wait_whole(held.at[i], sem.at[i])


def attend_back(place_w, place, lengths, tokens, q, k, v, ctx, d_ctx, lse, d_res, pool, held):
    seqs, rows, _ = tokens.shape
    flat = tokens.reshape(seqs * rows, D)
    row_spec = pl.BlockSpec((rows, D), lambda s, *_: (s, 0))
    any_spec = pl.BlockSpec(memory_space=pl.ANY)
    return pl.pallas_call(
        attend_back_kernel,
        grid_spec=pltpu.PrefetchScalarGridSpec(
            num_scalar_prefetch=3,
            grid=(seqs,),
            in_specs=[row_spec] * 6
            + [pl.BlockSpec((1, 16, rows), lambda s, *_: (s, 0, 0)), row_spec, any_spec, any_spec],
            out_specs=[row_spec, pl.BlockSpec((8, D), lambda s, *_: (0, 0)), any_spec],
            scratch_shapes=[
                pltpu.VMEM((3 * D, D), jnp.bfloat16),
                pltpu.VMEM((rows, D), jnp.bfloat16),
                pltpu.VMEM((rows, D), jnp.bfloat16),
                pltpu.VMEM((rows, D), jnp.bfloat16),
                pltpu.VMEM((3 * D, D), jnp.float32),
                pltpu.VMEM((3, D // BLK, BLK, D), jnp.bfloat16),
                pltpu.SemaphoreType.DMA((3,)),
                pltpu.SemaphoreType.DMA,
            ],
        ),
        out_shape=[
            jax.ShapeDtypeStruct((seqs * rows, D), jnp.bfloat16),
            jax.ShapeDtypeStruct((8, D), jnp.float32),
            jax.ShapeDtypeStruct(held.shape, held.dtype),
        ],
        input_output_aliases={12: 2},
        compiler_params=pltpu.CompilerParams(vmem_limit_bytes=62 * MIB),
        cost_estimate=pl.CostEstimate(
            flops=12 * seqs * rows * D * D + 10 * seqs * rows * rows * D,
            bytes_accessed=20 * seqs * rows * D + 12 * D * D,
            transcendentals=seqs * rows * rows * H,
        ),
        name="attend_back",
    )(place_w, place, lengths, flat, q, k, v, ctx, d_ctx, lse, d_res, pool, held)


def adam_kernel(
    place_ref, has_ref, *refs, per
):
    moment_ref, second_ref, master_ref, dres_ref, part_ref, rms_ref, vec_ref = refs[per : per + 7]
    vec_moment_ref, vec_second_ref, vec_master_ref = refs[per + 7 : per + 10]
    ingrad_out, rms_out, grad_out, moment_out, second_out, master_out = refs[per + 10 : per + 16]
    vec_out, vec_moment_out, vec_second_out, vec_master_out = refs[per + 16 :]
    step = pl.program_id(0)
    for j, grad_in in enumerate(refs[:per]):
        got = grad_in[0].astype(jnp.float32)
        gradient = jnp.where(has_ref[per * step + j] > 0, got, jnp.zeros_like(got))
        grad_out[j] = gradient
        moment_out[j], second_out[j], master_out[j] = adam_step(
            gradient, moment_ref[j], second_ref[j], master_ref[j], matrix_rate
        )
    ingrad_out[...] = dres_ref[...] + part_ref[...].astype(jnp.float32)

    @pl.when(step == 0)
    def _():
        rms_out[...] = rms_ref[:, 0:2]
        gradient = vec_ref[0 : vec_out.shape[0], :]
        vec_out[...] = gradient
        vec_moment_out[...], vec_second_out[...], vec_master_out[...] = adam_step(
            gradient, vec_moment_ref[...], vec_second_ref[...], vec_master_ref[...], vector_rate
        )


def adam_all(place, has, reduced, moment, second, master, d_res, part, rms, vec, vec_moment, vec_second, vec_master):
    slots = master.shape[0]
    per = 3 if slots % 3 == 0 else 2
    steps = slots // per
    total = d_res.shape[0]
    pieces = 1
    while 2 * pieces <= steps:
        pieces *= 2
    some = pl.BlockSpec((per, BLK, D), lambda s, *_: (s, 0, 0))
    rows = pl.BlockSpec((total // pieces, D), lambda s, *_: (jnp.minimum(s, pieces - 1), 0))

    def whole(shape):
        return pl.BlockSpec(shape, lambda s, *_: (0, 0))

    full = jax.ShapeDtypeStruct(master.shape, jnp.float32)
    vec_full = jax.ShapeDtypeStruct(vec_master.shape, jnp.float32)
    return pl.pallas_call(
        partial(adam_kernel, per=per),
        grid_spec=pltpu.PrefetchScalarGridSpec(
            num_scalar_prefetch=2,
            grid=(steps,),
            in_specs=[
                pl.BlockSpec((1, BLK, D), partial(lambda j, s, place, has: (place[per * s + j], 0, 0), j))
                for j in range(per)
            ]
            + [some] * 3
            + [rows] * 2
            + [whole(rms.shape), whole(vec.shape)]
            + [whole(vec_master.shape)] * 3,
            out_specs=[rows, whole((rms.shape[0], 2))] + [some] * 4 + [whole(vec_master.shape)] * 4,
        ),
        out_shape=[
            jax.ShapeDtypeStruct(d_res.shape, jnp.float32),
            jax.ShapeDtypeStruct((rms.shape[0], 2), jnp.float32),
        ]
        + [full] * 4
        + [vec_full] * 4,
        compiler_params=pltpu.CompilerParams(vmem_limit_bytes=60 * MIB),
        cost_estimate=pl.CostEstimate(
            flops=20 * slots * BLK * D, bytes_accessed=30 * slots * BLK * D, transcendentals=2 * slots * BLK * D
        ),
        name="adam_all",
    )(place, has, *(reduced,) * per, moment, second, master, d_res, part, rms, vec, vec_moment, vec_second, vec_master)


EARLY = 6
MIDDLE = 8
LATE = 10
FIRST = 10
LIST = EARLY + MIDDLE + LATE
HEAD_BLOCKS = 3 * D // BLK
MESH = pl.DeviceIdType.MESH


class Place:
    def __init__(self):
        dp = lax.axis_index("dp")
        self.z = lax.axis_index("seq")
        self.core = dp % 2
        x = (dp // 2) % 2
        y = dp // 4
        self.chip = dp // 2
        self.chip_x = 2 * y + 1 - x
        self.chip_y = 2 * (1 - y) + x
        self.chip_xy = 2 * (1 - y) + 1 - x
        self.to_core = {"dp": dp + 1 - 2 * self.core}
        self.to_x = {"dp": dp + 2 - 4 * x}
        self.to_y = {"dp": dp + 4 - 8 * y}
        z = self.z
        self.z_hops = (z + 1 - 2 * (z % 2), (z + 2) % 4, 3 - z)
        self.to_z = tuple({"seq": hop} for hop in self.z_hops)
        self.partners = (self.to_core, self.to_x, self.to_y) + self.to_z

    def meet(self):
        barrier = pltpu.get_barrier_semaphore()
        for partner in self.partners:
            pl.semaphore_signal(barrier, inc=1, device_id=partner, device_id_type=MESH)
        pl.semaphore_wait(barrier, len(self.partners))


class Sender:
    def __init__(self, send_sem, recv_sem):
        self.send_sem, self.recv_sem = send_sem, recv_sem

    def copy(self, k, src, dst, partner):
        return pltpu.make_async_remote_copy(
            src_ref=src,
            dst_ref=dst,
            send_sem=self.send_sem.at[k],
            recv_sem=self.recv_sem.at[k],
            device_id=partner,
            device_id_type=MESH,
        )


class Gather:
    def __init__(self, here, sender, first_sem, count, own, own_row, pool, row_of):
        self.here, self.sender, self.k, self.n = here, sender, first_sem, count
        self.own, self.own_row, self.pool, self.row_of = own, own_row, pool, row_of
        self.half = count * BLK // 2

    def link(self, name):
        here, half = self.here, self.half

        def own(part):
            return self.own.at[pl.ds(self.own_row + part * half, half)]

        def piece(chip, part):
            return self.pool.at[pl.ds(self.row_of(chip, here.core) + part * half, half)]

        def whole(chip):
            return self.pool.at[pl.ds(self.row_of(chip, here.core), 2 * half)]

        order = ("x0", "x1", "y1", "y0", "y_on", "x_on", "share_x", "share_y", "share_xy", "share_me")
        src, dst, partner = {
            "x0": lambda: (own(0), piece(here.chip, 0), here.to_x),
            "x1": lambda: (own(1), piece(here.chip, 1), here.to_x),
            "y1": lambda: (own(1), piece(here.chip, 1), here.to_y),
            "y0": lambda: (own(0), piece(here.chip, 0), here.to_y),
            "y_on": lambda: (piece(here.chip_x, 0), piece(here.chip_x, 0), here.to_y),
            "x_on": lambda: (piece(here.chip_y, 1), piece(here.chip_y, 1), here.to_x),
            "share_x": lambda: (whole(here.chip_x), whole(here.chip_x), here.to_core),
            "share_y": lambda: (whole(here.chip_y), whole(here.chip_y), here.to_core),
            "share_xy": lambda: (whole(here.chip_xy), whole(here.chip_xy), here.to_core),
            "share_me": lambda: (
                self.own.at[pl.ds(self.own_row, 2 * half)], whole(here.chip), here.to_core
            ),
        }[name]()
        return self.sender.copy(self.k + order.index(name), src, dst, partner)

    def start(self):
        for name in ("x0", "y1", "x1", "y0", "share_me"):
            self.link(name).start()

    def pass_on(self):
        self.link("x0").wait_recv()
        self.link("y_on").start()
        self.link("y1").wait_recv()
        self.link("x_on").start()

    def share_near(self):
        self.link("x1").wait_recv()
        self.link("share_x").start()
        self.link("y0").wait_recv()
        self.link("share_y").start()

    def sent(self):
        for name in ("x0", "y1", "x1", "y0", "y_on", "x_on"):
            self.link(name).wait_send()

    def share_far(self):
        self.link("y_on").wait_recv()
        self.link("x_on").wait_recv()
        self.link("share_xy").start()

    def finish(self):
        for name in ("share_me", "share_x", "share_y", "share_xy"):
            self.link(name).wait_recv()

    def shared(self):
        for name in ("share_me", "share_x", "share_y", "share_xy"):
            self.link(name).wait_send()


def front_kernel(
    place_ref, mine_ref, lengths_ref, vec_ref, master_in, tokens_in,
    pool, q_out, k_out, v_out, ctx_out, w_out, tok_out, ctx_split, lse_ref,
    stage, give, take, near, pack, w, tok, qs, ks, vs, cs,
    send_sem, recv_sem, load_sem,
):
    here = Place()
    z = here.z
    sender = Sender(send_sem, recv_sem)
    rows = SEQLEN
    own = tokens_in.shape[0] // 4
    part = tokens_in.shape[1]
    slots = master_in.shape[0]
    second = LIST - FIRST

    def local(src, dst, k):
        return pltpu.make_async_copy(src, dst, load_sem.at[k])

    load_master = local(master_in, stage, 0)
    load_master.start()
    own_tokens = [
        local(tokens_in.at[own * z + s], tok.at[pl.ds(s * rows + part * z, part)], 3 + s) for s in range(own)
    ]
    for load in own_tokens:
        load.start()
    here.meet()
    swaps = [
        sender.copy(
            own * hop + s,
            tokens_in.at[own * here.z_hops[hop] + s],
            tok.at[pl.ds(s * rows + part * z, part)],
            here.to_z[hop],
        )
        for hop in range(3)
        for s in range(own)
    ]
    for swap in swaps:
        swap.start()
    parts = (FIRST // 2, second // 2)
    starts = (0, FIRST)
    trades = [
        sender.copy(
            6 + i,
            give.at[pl.ds(i * parts[0] * BLK, parts[i] * BLK)],
            take.at[pl.ds(i * parts[0] * BLK, parts[i] * BLK)],
            here.to_core,
        )
        for i in range(2)
    ]
    load_master.wait()

    def held(entry):
        return stage[jnp.clip(mine_ref[entry] - here.core * slots, 0, slots - 1)].astype(jnp.bfloat16)

    for i in range(2):

        def fill_give(p, _):
            give[pl.ds((i * parts[0] + p) * BLK, BLK), :] = held(starts[i] + (1 - here.core) * parts[i] + p)
            return 0

        lax.fori_loop(0, parts[i], fill_give, 0)
        trades[i].start()

    def own_block(i, p):
        entry = starts[i] + here.core * parts[i] + p
        traded = take[pl.ds((i * parts[0] + p) * BLK, BLK), :]
        return jnp.where(mine_ref[entry] // slots == here.core, held(entry), traded)

    trades[0].wait_recv()

    def fill_near(p, _):
        near[pl.ds((here.chip * FIRST + here.core * parts[0] + p) * BLK, BLK), :] = own_block(0, p)
        return 0

    lax.fori_loop(0, parts[0], fill_near, 0)
    first = Gather(
        here, sender, 8, FIRST // 2, near, (here.chip * FIRST + here.core * (FIRST // 2)) * BLK, near,
        lambda chip, core: (chip * FIRST + core * (FIRST // 2)) * BLK,
    )
    then = Gather(
        here, sender, 18, second // 2, pack, 0, pool,
        lambda chip, core: (chip * LIST + FIRST + core * (second // 2)) * BLK,
    )
    first.start()

    trades[1].wait_recv()

    def fill_pack(p, _):
        pack[pl.ds(p * BLK, BLK), :] = own_block(1, p)
        return 0

    lax.fori_loop(0, parts[1], fill_pack, 0)
    own_second = local(
        pack, pool.at[pl.ds((here.chip * LIST + FIRST + here.core * parts[1]) * BLK, parts[1] * BLK)], 5
    )
    own_second.start()
    first.pass_on()
    first.share_near()
    first.sent()
    then.start()
    first.share_far()
    first.finish()

    def fill_w(b, _):
        at = place_ref[b]
        w[pl.ds(b * BLK, BLK), :] = near[pl.ds(((at // LIST) * FIRST + at % LIST) * BLK, BLK), :]
        return 0

    lax.fori_loop(0, HEAD_BLOCKS, fill_w, 0)
    keeps = [
        local(near.at[pl.ds(chip * FIRST * BLK, FIRST * BLK)], pool.at[pl.ds(chip * LIST * BLK, FIRST * BLK)], 6 + chip)
        for chip in range(4)
    ] + [local(w, w_out, 10)]
    for keep in keeps:
        keep.start()
    for load in own_tokens:
        load.wait()
    for swap in swaps:
        swap.wait_recv()
    keep_tok = local(tok, tok_out, 11)
    keep_tok.start()

    def send_ctx(s, hop):
        return sender.copy(
            28 + 3 * s + hop,
            cs.at[pl.ds(s * rows + part * here.z_hops[hop], part)],
            ctx_split.at[own * z + s],
            here.to_z[hop],
        )

    def keep_own(s):
        at = pl.ds(s * rows, rows)
        return [local(ref.at[at], out.at[at], 12 + k) for k, (ref, out) in enumerate(((qs, q_out), (ks, k_out), (vs, v_out), (cs, ctx_out)))] + [
            local(cs.at[pl.ds(s * rows + part * z, part)], ctx_split.at[own * z + s], 16)
        ]

    key = lax.broadcasted_iota(jnp.int32, (rows, 1), 0)

    def sequence(s, _):
        at = pl.ds(pl.multiple_of(s * rows, rows), rows)
        values = tok[at, :]
        qs[at, :] = ((mm(values, w[0:D, :]) + vec_ref[0:1, :]).astype(jnp.bfloat16) * 0.125).astype(jnp.bfloat16)
        ks[at, :] = mm(values, w[D : 2 * D, :]).astype(jnp.bfloat16)
        vs[at, :] = (mm(values, w[2 * D :, :]) + vec_ref[1:2, :]).astype(jnp.bfloat16)
        bias = jnp.where(key < lengths_ref[own * z + s], 0.0, MASKED)

        def pair(p, _):
            forward_pair(qs.at[at], ks.at[at], vs.at[at], cs.at[at], lse_ref, s, p, bias)
            return 0

        lax.fori_loop(0, PAIRS, pair, 0)
        for hop in range(3):
            send_ctx(s, hop).start()

        @pl.when(s > 0)
        def _():
            for keep in keep_own(s - 1):
                keep.wait()

        for keep in keep_own(s):
            keep.start()

        @pl.when(s == 0)
        def _():
            then.pass_on()

        return 0

    lax.fori_loop(0, own, sequence, 0)
    then.share_near()
    then.share_far()
    then.sent()
    then.finish()
    for keep in keep_own(own - 1) + keeps + [keep_tok, own_second]:
        keep.wait()
    for s in range(own):
        for hop in range(3):
            send_ctx(s, hop).wait_recv()
            send_ctx(s, hop).wait_send()
    for copy in swaps + trades:
        copy.wait_send()
    first.shared()
    then.shared()


def front(place, mine, lengths, vec, master, tokens):
    seqs, part, _ = tokens.shape
    total = seqs * part
    own = total // SEQLEN
    any_spec = pl.BlockSpec(memory_space=pl.ANY)
    vmem = pl.BlockSpec(memory_space=pltpu.VMEM)
    smem = pl.BlockSpec(memory_space=pltpu.SMEM)
    low = jnp.bfloat16
    slots = master.shape[0]
    flat = jax.ShapeDtypeStruct((total, D), low)
    return pl.pallas_call(
        front_kernel,
        in_specs=[smem] * 3 + [vmem] + [any_spec] * 2,
        out_specs=[any_spec] * 8 + [vmem],
        out_shape=[
            jax.ShapeDtypeStruct((4 * LIST * BLK, D), low),
            flat,
            flat,
            flat,
            flat,
            jax.ShapeDtypeStruct((3 * D, D), low),
            flat,
            jax.ShapeDtypeStruct(tokens.shape, low),
            jax.ShapeDtypeStruct((own, 16, SEQLEN), jnp.float32),
        ],
        scratch_shapes=[
            pltpu.VMEM(master.shape, jnp.float32),
            pltpu.VMEM((LIST // 2 * BLK, D), low),
            pltpu.VMEM((LIST // 2 * BLK, D), low),
            pltpu.VMEM((4 * FIRST * BLK, D), low),
            pltpu.VMEM(((LIST - FIRST) // 2 * BLK, D), low),
            pltpu.VMEM((3 * D, D), low),
        ]
        + [pltpu.VMEM((total, D), low)] * 5
        + [
            pltpu.SemaphoreType.DMA((34,)),
            pltpu.SemaphoreType.DMA((34,)),
            pltpu.SemaphoreType.DMA((17,)),
        ],
        compiler_params=pltpu.CompilerParams(
            vmem_limit_bytes=60 * MIB, collective_id=2, has_side_effects=True
        ),
        cost_estimate=pl.CostEstimate(
            flops=6 * total * D * D + 4 * total * SEQLEN * D,
            bytes_accessed=40 * total * D + 8 * slots * BLK * D,
            transcendentals=total * SEQLEN * H,
        ),
        name="front",
    )(place, mine, lengths, vec, master, tokens)


def add_rows(out_ref, out_row, terms, count, step=32):
    def body(i, _):
        value = None
        for ref, row in terms:
            part = ref[pl.ds(pl.multiple_of(row + i * step, step), step), :]
            value = part if value is None else value + part
        out_ref[pl.ds(pl.multiple_of(out_row + i * step, step), step), :] = value
        return 0

    lax.fori_loop(0, count // step, body, 0, unroll=2)


class Reduce:
    def __init__(self, here, sender, first_sem, count, first, column, blk_ref, grad, pack, buffers, red):
        self.here, self.sender, self.k = here, sender, first_sem
        self.n, self.first, self.blk, self.grad = count, first, blk_ref, grad
        self.acc, self.rx, self.ry, self.r2, self.z1, self.z2, self.fin = buffers
        self.red = red
        self.half = count * BLK // 2
        self.size = count * BLK
        self.cols = pl.ds(column, self.fin.shape[1])
        self.pack = pack.at[pl.ds(0, 4 * self.size), self.cols]

    def rows(self, ref, chip, half):
        return ref.at[pl.ds(chip * self.size + half * self.half, self.half)]

    def link(self, name):
        here, k, acc = self.here, self.k, self.acc
        keep = (here.z % 2) * self.half
        other = (1 - here.z % 2) * self.half
        mine = here.chip * self.size
        fin_keep = self.fin.at[pl.ds(keep, self.half)]
        order = (
            "core_xy", "core_x", "core_y", "core_me", "x_far", "x_near", "y_far", "y_near",
            "y_on", "x_on", "z_half", "z_far", "z_back", "share",
        )

        def across(chip):
            rows = pl.ds(chip * self.size, self.size)
            return self.pack.at[rows], acc.at[rows], here.to_core

        src, dst, partner = {
            "core_xy": lambda: across(here.chip_xy),
            "core_x": lambda: across(here.chip_x),
            "core_y": lambda: across(here.chip_y),
            "core_me": lambda: across(here.chip),
            "x_far": lambda: (self.rows(acc, here.chip_xy, 0), self.rx.at[1], here.to_x),
            "x_near": lambda: (self.rows(acc, here.chip_x, 0), self.rx.at[0], here.to_x),
            "y_far": lambda: (self.rows(acc, here.chip_xy, 1), self.ry.at[1], here.to_y),
            "y_near": lambda: (self.rows(acc, here.chip_y, 1), self.ry.at[0], here.to_y),
            "y_on": lambda: (self.rows(acc, here.chip_y, 0), self.r2.at[0], here.to_y),
            "x_on": lambda: (self.rows(acc, here.chip_x, 1), self.r2.at[1], here.to_x),
            "z_half": lambda: (acc.at[pl.ds(mine + other, self.half)], self.z1, here.to_z[0]),
            "z_far": lambda: (acc.at[pl.ds(mine + keep, self.half)], self.z2, here.to_z[1]),
            "z_back": lambda: (fin_keep, fin_keep, here.to_z[0]),
            "share": lambda: (self.fin, self.result(), here.to_core),
        }[name]()
        return self.sender.copy(k + order.index(name), src, dst, partner)

    def result(self):
        return self.red.at[pl.ds((self.first + self.here.core * self.n) * BLK, self.size), self.cols]

    def start_core(self):
        here, n = self.here, self.n
        chips = (here.chip_xy, here.chip_x, here.chip_y, here.chip)
        for chip, name in zip(chips, ("core_xy", "core_x", "core_y", "core_me")):

            def body(i, _):
                block = self.blk[chip * LIST + self.first + (1 - here.core) * n + i]
                self.pack[pl.ds(chip * self.size + i * BLK, BLK), :] = self.grad[block, :, self.cols]
                return 0

            lax.fori_loop(0, n, body, 0)
            self.link(name).start()

    def sent_core(self):
        for name in ("core_xy", "core_x", "core_y", "core_me"):
            self.link(name).wait_send()

    def add_own(self, chip):
        here, n = self.here, self.n

        def body(i, _):
            entry = chip * LIST + self.first + here.core * n + i
            block = self.blk[entry]
            for piece in range(0, BLK, 32):
                rows = pl.ds(pl.multiple_of(chip * self.size + i * BLK, BLK) + piece, 32)
                self.acc[rows, :] = self.acc[rows, :] + self.grad[block, piece : piece + 32, self.cols]
            return 0

        lax.fori_loop(0, n, body, 0)

    def start_far(self):
        self.link("core_xy").wait_recv()
        self.add_own(self.here.chip_xy)
        self.link("x_far").start()
        self.link("y_far").start()

    def start_near(self):
        self.link("core_x").wait_recv()
        self.add_own(self.here.chip_x)
        self.link("x_near").start()
        self.link("core_y").wait_recv()
        self.add_own(self.here.chip_y)
        self.link("y_near").start()

    def pass_plane(self):
        here = self.here
        self.link("x_far").wait_recv()
        at = here.chip_y * self.size
        add_rows(self.acc, at, ((self.acc, at), (self.rx.at[1], 0)), self.half)
        self.link("y_on").start()
        self.link("y_far").wait_recv()
        at = here.chip_x * self.size + self.half
        add_rows(self.acc, at, ((self.acc, at), (self.ry.at[1], 0)), self.half)
        self.link("x_on").start()

    def start_z(self):
        here = self.here
        mine = here.chip * self.size
        self.link("core_me").wait_recv()
        self.add_own(here.chip)
        self.link("x_near").wait_recv()
        self.link("y_on").wait_recv()
        add_rows(self.acc, mine, ((self.acc, mine), (self.rx.at[0], 0), (self.r2.at[0], 0)), self.half)
        self.link("y_near").wait_recv()
        self.link("x_on").wait_recv()
        low = mine + self.half
        add_rows(self.acc, low, ((self.acc, low), (self.ry.at[0], 0), (self.r2.at[1], 0)), self.half)
        self.link("z_half").start()

    def far_z(self):
        here = self.here
        keep = here.chip * self.size + (here.z % 2) * self.half
        self.link("z_half").wait_recv()
        add_rows(self.acc, keep, ((self.acc, keep), (self.z1, 0)), self.half)
        self.link("z_far").start()

    def back_z(self):
        here = self.here
        keep = (here.z % 2) * self.half
        self.link("z_far").wait_recv()
        add_rows(self.fin, keep, ((self.acc, here.chip * self.size + keep), (self.z2, 0)), self.half)
        self.link("z_back").start()

    def share(self, local_sem):
        red = self.result()
        self.link("z_back").wait_recv()
        self.link("z_back").wait_send()
        self.link("share").start()
        pltpu.make_async_copy(self.fin, red, local_sem).start()

    def finish(self, local_sem):
        red = self.result()
        self.link("share").wait_recv()
        pltpu.make_async_copy(self.fin, red, local_sem).wait()
        for name in ("x_far", "x_near", "y_far", "y_near", "y_on", "x_on", "z_half", "z_far", "share"):
            self.link(name).wait_send()


def back_pair(q_ref, k_ref, v_ref, ctx_ref, do_ref, lse_ref, seq, p, bias):
    rows = q_ref.shape[0]
    cols = pl.ds(pl.multiple_of(p * LANES, LANES), LANES)
    row8 = lax.broadcasted_iota(jnp.int32, (16, rows), 0)

    def extra_rows(lead, row):
        one, two, three = (part.astype(jnp.float32) for part in split3(row))
        return jnp.where(
            row8 == 0, lead, jnp.where(row8 == 1, one, jnp.where(row8 == 2, two, jnp.where(row8 == 3, three, 0.0)))
        )

    q2, k2, v2, do2 = q_ref[:, cols], k_ref[:, cols], v_ref[:, cols], do_ref[:, cols]
    q2t, k2t, do2t = q2.T, k2.T, do2.T
    prod = do2t.astype(jnp.float32) * ctx_ref[:, cols].T.astype(jnp.float32)
    dq_parts = []
    d_key = jnp.zeros((rows, LANES), jnp.float32)
    d_value = jnp.zeros((rows, LANES), jnp.float32)
    for half in range(2):
        head = slice(half * DH, half * DH + DH)
        inside, spare = spare_lanes(rows, half, bias)
        zero = jnp.zeros_like(k2)
        lse = lse_ref[seq, pl.ds(2 * p + half, 1), :]
        delta = jnp.sum(prod[head], axis=0, keepdims=True)
        scores = mm(jnp.where(inside, k2, spare), beside(q2t[head], extra_rows(1.0, -lse), half))
        probs = jnp.exp(scores)
        d_probs = mm(jnp.where(inside, v2, spare), beside(do2t[head], extra_rows(0.0, -delta), half))
        d_scores = (probs * d_probs).astype(jnp.bfloat16)
        d_value += mm(probs.astype(jnp.bfloat16), jnp.where(inside, do2, zero))
        d_key += mm(d_scores, jnp.where(inside, q2, zero))
        dq_parts.append(mm(k2t[head], d_scores))
    d_query = jnp.concatenate(dq_parts, axis=0).T * 0.125
    return cols, d_query.astype(jnp.bfloat16), d_key.astype(jnp.bfloat16), d_value.astype(jnp.bfloat16)


def tail_kernel(
    blk_ref, lengths_ref, vec_in, squares_in, lse_ref,
    dctx_in, ctx_split, dbranch, dinner, mid, act, dfeed, tok_in, q_in, k_in, v_in, ctx_in, w_in,
    red, ingrad, vec_out, rms_out,
    grad, pack, d3, att, tok, w, *rest,
):
    here = Place()
    z = here.z
    phase_buffers = [rest[7 * i : 7 * i + 7] for i in range(4)]
    vec_src, vec_land, rms_src, rms_land, send_sem, recv_sem, load_sem = rest[28:]
    sender = Sender(send_sem, recv_sem)
    rows = SEQLEN
    own = dctx_in.shape[0] // 4
    part = dctx_in.shape[1]
    total = own * rows
    wide = D // 2

    def local(src, dst, k):
        return pltpu.make_async_copy(src, dst, load_sem.at[k])

    first_loads = (
        local(ctx_split, att.at[2], 0),
        local(dinner.at[:, pl.ds(0, D)], att.at[3], 1),
        local(dbranch, d3.at[0], 2),
        local(mid, d3.at[1], 3),
        local(dfeed, d3.at[2], 4),
        local(q_in, att.at[0], 5),
        local(k_in, att.at[1], 6),
        local(tok_in, tok, 7),
        local(w_in, w, 10),
    )
    for load in first_loads[:5]:
        load.start()
    here.meet()

    def swap(half, s, hop):
        cols = pl.ds(half * wide, wide)
        return sender.copy(
            6 * half + 3 * s + hop,
            dctx_in.at[own * here.z_hops[hop] + s, :, cols],
            att.at[4, pl.ds(s * rows + part * z, part), cols],
            here.to_z[hop],
        )

    swaps = [[swap(half, s, hop) for s in range(own) for hop in range(3)] for half in range(2)]
    own_swaps = [local(dctx_in.at[own * z + s], att.at[4, pl.ds(s * rows + part * z, part)], 8 + s) for s in range(own)]
    for copy in swaps[0] + own_swaps:
        copy.start()
    for load in first_loads[2:5]:
        load.wait()

    early, middle = (
        Reduce(here, sender, 24 + 14 * i, count // 2, first, 0, blk_ref, grad, pack, phase_buffers[i], red)
        for i, (count, first) in enumerate(((EARLY, 0), (MIDDLE, EARLY)))
    )
    late = [
        Reduce(here, sender, 52 + 14 * i, LATE // 2, EARLY + MIDDLE, i * wide, blk_ref, grad, pack, phase_buffers[2 + i], red)
        for i in range(2)
    ]

    def grads(step, _):
        slot = 2 + step % 2
        held = att.at[slot]
        pltpu.make_async_copy(held, held, load_sem.at[step % 2]).wait()
        value = mm_tn(att[slot], d3[(step + 3) // 4])
        grad[pl.ds(HEAD_BLOCKS + step * (D // BLK), D // BLK)] = value.astype(jnp.bfloat16).reshape(D // BLK, BLK, D)

        @pl.when(step < CHUNKS - 1)
        def _():
            local(dinner.at[:, pl.ds((step + 1) * D, D)], held, step % 2).start()

        @pl.when((step >= CHUNKS - 1) & (step < 2 * CHUNKS - 1))
        def _():
            local(act.at[:, pl.ds((step - CHUNKS + 1) * D, D)], held, step % 2).start()

        @pl.when(step == CHUNKS)
        def _():
            early.start_core()

        @pl.when(step == CHUNKS + 1)
        def _():
            for copy in swaps[0]:
                copy.wait_send()
            for copy in swaps[1]:
                copy.start()

        @pl.when(step == CHUNKS + 2)
        def _():
            early.start_far()

        @pl.when(step == CHUNKS + 3)
        def _():
            early.start_near()

        return 0

    for load in first_loads[5:]:
        load.start()
    grad[0:HEAD_BLOCKS] = jnp.zeros((HEAD_BLOCKS, BLK, D), jnp.bfloat16)
    lax.fori_loop(0, 1 + 2 * CHUNKS, grads, 0)
    more_loads = (local(v_in, att.at[2], 0), local(ctx_in, att.at[3], 1))
    for load in more_loads:
        load.start()
    early.sent_core()
    middle.start_core()
    for load in first_loads[5:] + tuple(own_swaps) + more_loads:
        load.wait()
    for copy in swaps[0]:
        copy.wait_recv()

    key = lax.broadcasted_iota(jnp.int32, (rows, 1), 0)

    def head_grads(half):
        cols = pl.ds(half * wide, wide)
        for block, which in ((0, 1), (6, 2), (12, 0)):
            value = mm_tn(tok[...], d3[which, :, cols]).astype(jnp.bfloat16)
            grad[block : block + 6, :, cols] = value.reshape(D // BLK, BLK, wide)

    def send_ingrad(s, hop):
        return sender.copy(
            80 + 3 * s + hop,
            att.at[0, pl.ds(s * rows + part * here.z_hops[hop], part)],
            ingrad.at[own * z + s],
            here.to_z[hop],
        )

    def own_ingrad(s):
        return local(att.at[0, pl.ds(s * rows + part * z, part)], ingrad.at[own * z + s], 11 + s)

    def input_gradient(s):
        at = pl.ds(s * rows, rows)
        value = mm_nt(d3[1, at, :], w[0:D, :])
        value += mm_nt(d3[2, at, :], w[D : 2 * D, :])
        value += mm_nt(d3[0, at, :], w[2 * D :, :])
        att[0, at, :] = value.astype(jnp.bfloat16)
        for hop in range(3):
            send_ingrad(s, hop).start()
        own_ingrad(s).start()

    def second_half():
        for copy in swaps[1]:
            copy.wait_recv()

    group = PAIRS // 2

    def pair_step(i, _):
        s = (i // group) % own
        p = (i // (own * group)) * group + i % group
        bias = jnp.where(key < lengths_ref[own * z + s], 0.0, MASKED)
        at = pl.ds(pl.multiple_of(s * rows, rows), rows)
        cols, d_query, d_key, d_value = back_pair(*(att.at[k, at] for k in range(5)), lse_ref, s, p, bias)
        d3[1, at, cols] = d_query
        d3[2, at, cols] = d_key
        d3[0, at, cols] = d_value

        stages = {
            0: (early.pass_plane,),
            2: (middle.start_far,),
            4: (early.start_z, middle.start_near),
            5: (lambda: head_grads(0), second_half),
            6: (early.far_z, middle.pass_plane),
            8: (lambda: input_gradient(0),),
            9: (middle.sent_core, late[0].start_core, middle.start_z, late[0].start_far),
            10: (late[0].start_near,),
            11: (late[0].pass_plane,),
        }
        for at_step, calls in stages.items():

            @pl.when(i == at_step)
            def _():
                for call in calls:
                    call()

        return 0

    lax.fori_loop(0, own * PAIRS, pair_step, 0)

    head_grads(1)
    late[1].start_core()
    vec_src[0] = vec_in[...]
    vec_src[0, 0:1, :] = jnp.sum(d3[1].astype(jnp.float32), axis=0, keepdims=True)
    vec_src[0, 1:2, :] = jnp.sum(d3[0].astype(jnp.float32), axis=0, keepdims=True)
    for i in range(squares_in.shape[0]):
        sums = jnp.sum(squares_in[i], axis=-1, keepdims=True)
        rms_src[0, 8 * i : 8 * i + 8, :] = jnp.broadcast_to(sums, (8, LANES))
    ways = (here.to_z[0], here.to_z[1], here.to_core, here.to_x, here.to_y)
    vec_copies = [sender.copy(12 + w, vec_src.at[w], vec_land.at[w], way) for w, way in enumerate(ways)]
    rms_copies = [sender.copy(17 + w, rms_src.at[w], rms_land.at[w], ways[w]) for w in range(2)]

    def vec_step(w):
        if w > 0:
            vec_copies[w - 1].wait_recv()
            after = vec_src[w - 1] + vec_land[w - 1]
            if w < len(ways):
                vec_src[w] = after
            else:
                vec_out[...] = after
        if w < len(ways):
            vec_copies[w].start()
        if 0 < w <= 2:
            rms_copies[w - 1].wait_recv()
            after = rms_src[w - 1] + rms_land[w - 1]
            if w < 2:
                rms_src[w] = after
            else:
                lane = lax.broadcasted_iota(jnp.int32, (1, LANES), 1)
                tiles = squares_in.shape[0]
                each = dctx_in.shape[0] // tiles
                for n in range(dctx_in.shape[0]):
                    row = 8 * (n // each) + 2 * (n % each)
                    sums = jnp.where(lane == 0, after[row : row + 1], after[row + 1 : row + 2])
                    rms_out[n : n + 1, :] = jnp.sqrt(sums / (lengths_ref[n].astype(jnp.float32) * D))
        if w < 2:
            rms_copies[w].start()

    vec_step(0)
    late[1].start_far()
    early.back_z()
    middle.far_z()
    vec_step(1)
    late[0].start_z()
    late[1].start_near()
    late[1].pass_plane()
    vec_step(2)
    late[1].start_z()
    early.share(load_sem.at[13])
    vec_step(3)
    late[0].far_z()
    middle.back_z()
    vec_step(4)
    late[1].far_z()
    input_gradient(1)
    vec_step(5)
    late[0].back_z()
    late[1].back_z()
    late[0].share(load_sem.at[15])
    middle.share(load_sem.at[14])
    late[1].share(load_sem.at[16])
    for phase in late:
        phase.sent_core()
    for i, phase in enumerate((early, middle, late[0], late[1])):
        phase.finish(load_sem.at[13 + i])
    for copy in swaps[1] + vec_copies + rms_copies:
        copy.wait_send()
    for s in range(own):
        own_ingrad(s).wait()
        for hop in range(3):
            send_ingrad(s, hop).wait_recv()
            send_ingrad(s, hop).wait_send()


def tail(blk, lengths, vec, squares, lse, d_ctx, ctx_split, d_branch, d_inner, mid, act, d_feed, tokens, q, k, v, ctx, w):
    total = tokens.shape[0]
    any_spec = pl.BlockSpec(memory_space=pl.ANY)
    vmem = pl.BlockSpec(memory_space=pltpu.VMEM)
    smem = pl.BlockSpec(memory_space=pltpu.SMEM)
    low = jnp.bfloat16
    sums = (8 * squares.shape[0], LANES)

    def phase(n, width):
        half = n * BLK // 2
        return [
            pltpu.VMEM((4 * n * BLK, width), low),
            pltpu.VMEM((2, half, width), low),
            pltpu.VMEM((2, half, width), low),
            pltpu.VMEM((2, half, width), low),
            pltpu.VMEM((half, width), low),
            pltpu.VMEM((half, width), low),
            pltpu.VMEM((n * BLK, width), low),
        ]

    return pl.pallas_call(
        tail_kernel,
        in_specs=[smem] * 2 + [vmem] * 3 + [any_spec] * 13,
        out_specs=[any_spec] * 2 + [vmem] * 2,
        out_shape=[
            jax.ShapeDtypeStruct((LIST * BLK, D), low),
            jax.ShapeDtypeStruct(d_ctx.shape, low),
            jax.ShapeDtypeStruct(vec.shape, jnp.float32),
            jax.ShapeDtypeStruct((d_ctx.shape[0], LANES), jnp.float32),
        ],
        scratch_shapes=[
            pltpu.VMEM((HEAD_BLOCKS + (D + 2 * FF) // BLK, BLK, D), low),
            pltpu.VMEM((2 * max(EARLY, MIDDLE, LATE) * BLK, D), low),
            pltpu.VMEM((3, total, D), low),
            pltpu.VMEM((5, total, D), low),
            pltpu.VMEM((total, D), low),
            pltpu.VMEM((3 * D, D), low),
        ]
        + phase(EARLY // 2, D)
        + phase(MIDDLE // 2, D)
        + phase(LATE // 2, D // 2)
        + phase(LATE // 2, D // 2)
        + [
            pltpu.VMEM((5,) + vec.shape, jnp.float32),
            pltpu.VMEM((5,) + vec.shape, jnp.float32),
            pltpu.VMEM((2,) + sums, jnp.float32),
            pltpu.VMEM((2,) + sums, jnp.float32),
            pltpu.SemaphoreType.DMA((86,)),
            pltpu.SemaphoreType.DMA((86,)),
            pltpu.SemaphoreType.DMA((17,)),
        ],
        compiler_params=pltpu.CompilerParams(
            vmem_limit_bytes=63 * MIB, collective_id=1, has_side_effects=True
        ),
        cost_estimate=pl.CostEstimate(
            flops=2 * total * D * (6 * D + 2 * FF) + 10 * total * SEQLEN * D,
            bytes_accessed=total * (24 * D + 4 * FF) + 8 * FF * D,
            transcendentals=total * SEQLEN * H,
        ),
        name="tail",
    )(blk, lengths, vec, squares, lse, d_ctx, ctx_split, d_branch, d_inner, mid, act, d_feed, tokens, q, k, v, ctx, w)


def tables_kernel(owner_ref, place_ref, mine_ref, block_ref, spot_ref, has_ref, fits_ref, *, slots):
    dp = lax.axis_index("dp")
    chip_slots = 2 * slots
    near_blocks = HEAD_BLOCKS + (D + FF) // BLK
    for ref in (mine_ref, block_ref, spot_ref, has_ref):
        for i in range(ref.shape[0]):
            ref[i] = 0

    def body(b, counts):
        listed, early, middle, late, bad = counts
        slot = owner_ref[b]
        chip = slot // chip_slots
        shift = 8 * chip
        one = jnp.left_shift(1, shift)

        def count(packed):
            return jnp.right_shift(packed, shift) & 255

        order = count(listed)
        n_early, n_middle, n_late = count(early), count(middle), count(late)
        body_block = b >= HEAD_BLOCKS
        in_early = body_block & (b < near_blocks) & (n_early < EARLY)
        in_middle = body_block & jnp.logical_not(in_early) & (n_middle < MIDDLE)
        in_late = jnp.logical_not(in_early | in_middle)
        spot = jnp.where(in_early, n_early, jnp.where(in_middle, EARLY + n_middle, EARLY + MIDDLE + n_late))
        wrong = (order >= LIST) | (spot >= LIST) | (jnp.logical_not(body_block) & (order >= FIRST))
        spot = jnp.minimum(spot, LIST - 1)
        place_ref[b] = chip * LIST + jnp.minimum(order, LIST - 1)
        block_ref[chip * LIST + spot] = b

        @pl.when(chip == dp // 2)
        def _():
            mine_ref[jnp.minimum(order, LIST - 1)] = slot - chip * chip_slots

            @pl.when(slot // slots == dp)
            def _():
                spot_ref[slot % slots] = spot
                has_ref[slot % slots] = 1

        return (
            listed + one,
            early + jnp.where(in_early, one, 0),
            middle + jnp.where(in_middle, one, 0),
            late + jnp.where(in_late, one, 0),
            bad | wrong.astype(jnp.int32),
        )

    zero = jnp.int32(0)
    counts = lax.fori_loop(0, owner_ref.shape[0], body, (zero,) * 5, unroll=4)
    fits_ref[0] = 1 - counts[4]


def tables(owner, slots):
    chips = lax.axis_size("dp") // 2
    smem = pl.BlockSpec(memory_space=pltpu.SMEM)
    sizes = (owner.shape[0], LIST, chips * LIST, slots, slots, 1)
    return pl.pallas_call(
        partial(tables_kernel, slots=slots),
        in_specs=[smem],
        out_specs=[smem] * len(sizes),
        out_shape=[jax.ShapeDtypeStruct((n,), jnp.int32) for n in sizes],
        name="tables",
    )(owner)


def general(tokens, cotangent, lengths, owner, master, vec_master):
    slot_local = master.shape[0]
    gathered = lax.all_gather(master.astype(jnp.bfloat16), "dp", axis=0, tiled=True)
    seq_place = lax.axis_index("seq")
    slot_total = slot_local * lax.axis_size("dp")
    tokens = to_whole(tokens, "seq")
    cotangent = to_whole(cotangent, "seq")
    seq_count, seq_len, width = tokens.shape
    token_count = seq_count * seq_len
    lengths = lax.dynamic_slice_in_dim(lengths, seq_place * seq_count, seq_count)
    q, k, v, ctx, lse, _ = attend(owner, lengths, tokens, gathered, vec_master)
    flat = tokens.reshape(token_count, D)
    _, mid, out, act, d_inner, d_feed, d_branch, d_res, d_ctx, vec_feed, squares = feed_both(
        owner, lengths, seq_len,
        flat, ctx, cotangent.reshape(token_count, D), gathered, vec_master,
    )
    held = feed_grads(owner, slot_total, ctx, d_branch, d_inner, mid, act, d_feed)
    ingrad, vec_attend, held = attend_back(
        owner, owner, lengths, tokens, q, k, v, ctx, d_ctx, lse, d_res, gathered, held
    )
    local_sums = jnp.sum(squares.reshape(seq_count, -1, 8, D)[:, :, :2], axis=(1, 3))
    own_rms = jnp.sqrt(local_sums / (lengths[:, None].astype(jnp.float32) * D))
    sublayer_rms = lax.all_gather(own_rms, "seq", axis=0, tiled=True)
    vec_local = jnp.concatenate([vec_attend[:2], vec_feed[2:12]], axis=0)
    vec_grad = lax.psum(vec_local, ("dp", "seq"))
    owned = lax.psum_scatter(held, "dp", scatter_dimension=0, tiled=True)
    reduced = lax.psum(owned, "seq")
    first_slot = lax.axis_index("dp") * slot_local
    slots = jnp.arange(slot_local, dtype=jnp.int32)
    has = jnp.any((first_slot + slots)[:, None] == owner[None, :], axis=1).astype(jnp.int32)
    whole = (seq_count, seq_len, D)
    return (
        to_split(out.reshape(whole), "seq"),
        jnp.zeros((token_count, D), jnp.float32),
        to_split(ingrad.reshape(whole), "seq").reshape(token_count, D),
        to_split(mid.reshape(whole), "seq").astype(jnp.float32),
        jnp.pad(sublayer_rms, ((0, 0), (0, LANES - 2))),
        jnp.pad(vec_grad, ((0, 4), (0, 0))),
        reduced,
        slots,
        has,
    )


def listed(tokens, cotangent, lengths, owner, master, vec_master, place, mine, block, spot, has):
    seqs, part, _ = tokens.shape
    total = seqs * part
    pool, q, k, v, ctx, w, whole, ctx_split, lse = front(
        place, mine, lengths, vec_master, master, tokens
    )
    ctx_split = ctx_split.reshape(total, D)
    wide_mid, mid, out, act, d_inner, d_feed, d_branch, d_res, d_ctx, vec_feed, squares = feed_both(
        place, lengths, part,
        tokens.reshape(total, D), ctx_split, cotangent.reshape(total, D), pool.reshape(-1, BLK, D), vec_master,
    )
    reduced, ingrad, vec_grad, rms = tail(
        block, lengths, vec_feed, squares, lse, d_ctx.reshape(seqs, part, D), ctx_split, d_branch, d_inner,
        mid, act, d_feed, whole, q, k, v, ctx, w,
    )
    return (
        out.reshape(tokens.shape),
        d_res,
        ingrad.reshape(total, D),
        wide_mid.reshape(tokens.shape),
        rms,
        vec_grad,
        reduced.reshape(LIST, BLK, D),
        spot,
        has,
    )


def per_device(
    tokens, cotangent, lengths, owner, master, moment, second, vec_master, vec_moment, vec_second
):
    slot_local = master.shape[0]
    given = (tokens, cotangent, lengths, owner, master, vec_master)
    if lax.axis_size("dp") == 8 and lax.axis_size("seq") == 4:
        place, mine, block, spot, has, fits = tables(owner, slot_local)

        def otherwise(*args):
            results = general(*args[:6])
            pad = ((0, LIST - slot_local), (0, 0), (0, 0))
            return results[:6] + (jnp.pad(results[6], pad),) + results[7:]

        results = lax.cond(fits[0] > 0, listed, otherwise, *given, place, mine, block, spot, has)
    else:
        results = general(*given)
    layer_out, d_res, ingrad, residual_mid, rms, vec_grad, reduced, spot, has = results
    updated = adam_all(
        spot, has, reduced, moment, second, master,
        d_res, ingrad, rms, vec_grad, vec_moment, vec_second, vec_master,
    )
    input_grad, sublayer_rms, slots, vectors = updated[0], updated[1], updated[2:6], updated[6:]
    return (layer_out, input_grad.reshape(tokens.shape), residual_mid, sublayer_rms, *slots, *vectors)


def solution(mesh):
    return jax.shard_map(
        per_device,
        mesh=mesh,
        in_specs=(
            P("dp", "seq", None),
            P("dp", "seq", None),
            P("dp"),
            P(),
            P("dp", None, None),
            P("dp", None, None),
            P("dp", None, None),
            P(),
            P(),
            P(),
        ),
        out_specs=(
            P("dp", "seq", None),
            P("dp", "seq", None),
            P("dp", "seq", None),
            P("dp", None),
            P("dp", None, None),
            P("dp", None, None),
            P("dp", None, None),
            P("dp", None, None),
            P(),
            P(),
            P(),
            P(),
        ),
        check_vma=False,
    )
```

```python
from functools import partial

import jax
import jax.numpy as jnp
from jax import lax
from jax.experimental import pallas as pl
from jax.experimental.pallas import tpu as pltpu
from jax.sharding import PartitionSpec as P

D = 768
H = 12
DH = 64
FF = 3072
BLK = 128
SEQLEN = 512
STEP = 5


first_decay = 0.5
second_decay = 0.5
matrix_rate = 0.02
vector_rate = 0.2
weight_decay = 0.01
adam_epsilon = 1e-08


def adam_step(gradient, moment, second, weight, rate):
    moment_new = first_decay * moment + (1.0 - first_decay) * gradient
    second_new = second_decay * second + (1.0 - second_decay) * gradient * gradient
    moment_hat = moment_new * (1.0 / (1.0 - first_decay**STEP))
    second_hat = second_new * (1.0 / (1.0 - second_decay**STEP))
    root = second_hat * lax.rsqrt(second_hat) + adam_epsilon
    inverse = pltpu.reciprocal(root, approx=True)
    inverse = inverse * (2.0 - root * inverse)
    weight_new = weight - rate * (moment_hat * inverse + weight_decay * weight)
    return (moment_new, second_new, weight_new)


def seq_swap(parts, axis):
    size = lax.axis_size(axis)
    me = lax.axis_index(axis)
    stacked = parts
    got = [None] * size
    mine = lax.dynamic_index_in_dim(stacked, me, 0, keepdims=False)
    out = [mine]
    for hop in range(1, size):
        there = jnp.bitwise_xor(me, hop)
        piece = lax.dynamic_index_in_dim(stacked, there, 0, keepdims=False)
        route = [(i, i ^ hop) for i in range(size)]
        out.append(lax.ppermute(piece, axis, route))
    return out


def from_hops(pieces, axis):
    size = lax.axis_size(axis)
    me = lax.axis_index(axis)
    stacked = jnp.stack(pieces, axis=0)
    order = jnp.bitwise_xor(jnp.arange(size, dtype=jnp.int32), me)
    return jnp.take(stacked, order, axis=0)


def to_whole(block, axis):
    size = lax.axis_size(axis)
    count, length, width = block.shape
    pieces = seq_swap(block.reshape(size, count // size, length, width), axis)
    stacked = from_hops(pieces, axis)
    return jnp.swapaxes(stacked, 0, 1).reshape(count // size, size * length, width)


def to_split(whole, axis):
    size = lax.axis_size(axis)
    own, full, width = whole.shape
    parts = jnp.swapaxes(whole.reshape(own, size, full // size, width), 0, 1)
    pieces = seq_swap(parts, axis)
    return from_hops(pieces, axis).reshape(size * own, full // size, width)


LANES = 128
PAIRS = D // LANES
CHUNKS = FF // D
MASKED = -1e30
NT = (((1,), (1,)), ((), ()))
TN = (((0,), (0,)), ((), ()))
MIB = 1 << 20


def mm(left, right):
    return jnp.dot(left, right, preferred_element_type=jnp.float32)


def mm_nt(left, right):
    return lax.dot_general(left, right, NT, preferred_element_type=jnp.float32)


def mm_tn(left, right):
    return lax.dot_general(left, right, TN, preferred_element_type=jnp.float32)


def load_blocks(pool_ref, place_ref, first, into_ref, sem):
    def start(i, _):
        pltpu.make_async_copy(
            pool_ref.at[place_ref[first + i]], into_ref.at[pl.ds(i * BLK, BLK)], sem
        ).start()
        return 0

    lax.fori_loop(0, into_ref.shape[0] // BLK, start, 0)


def wait_whole(ref, sem):
    pltpu.make_async_copy(ref, ref, sem).wait()


def spare_lanes(rows, half, bias_column):
    lane = lax.broadcasted_iota(jnp.int32, (rows, LANES), 1)
    first = DH * (1 - half)
    spare = jnp.where(lane == first, bias_column, jnp.where(lane < first + 4, 1.0, 0.0))
    inside = (lane >= DH * half) & (lane < DH * half + DH)
    return inside, spare.astype(jnp.bfloat16)


def split3(row):
    one = row.astype(jnp.bfloat16)
    rest = row - one.astype(jnp.float32)
    two = rest.astype(jnp.bfloat16)
    three = (rest - two.astype(jnp.float32)).astype(jnp.bfloat16)
    return one, two, three


def beside(head_rows, extra, half):
    columns = head_rows.shape[1]
    pad = jnp.zeros((DH - extra.shape[0], columns), jnp.bfloat16)
    parts = [extra.astype(jnp.bfloat16), pad]
    order = [head_rows] + parts if half == 0 else parts + [head_rows]
    return jnp.concatenate(order, axis=0)


def forward_pair(q_ref, k_ref, v_ref, ctx_ref, lse_ref, seq, p, bias):
    rows = q_ref.shape[0]
    cols = pl.ds(pl.multiple_of(p * LANES, LANES), LANES)
    row8 = lax.broadcasted_iota(jnp.int32, (16, rows), 0)
    q2t = q_ref[:, cols].T
    k2 = k_ref[:, cols]
    v2t = v_ref[:, cols].T
    outs = []
    for half in range(2):
        inside, spare = spare_lanes(rows, half, bias)
        k_aug = jnp.where(inside, k2, spare)
        head = slice(half * DH, half * DH + DH)
        q_aug = beside(q2t[head], jnp.where(row8 == 0, 1.0, 0.0), half)
        scores = mm(k_aug, q_aug)
        top = jnp.max(scores, axis=0, keepdims=True)
        expos = jnp.exp(scores - top).astype(jnp.bfloat16)
        v_aug = jnp.concatenate([v2t[head], jnp.ones((16, rows), jnp.bfloat16)], axis=0)
        both = mm(v_aug, expos)
        total = both[DH : DH + 1]
        outs.append(both[0:DH] / total)
        lse_ref[seq, pl.ds(2 * p + half, 1), :] = top + jnp.log(total)
    ctx_ref[:, cols] = jnp.concatenate(outs, axis=0).T.astype(jnp.bfloat16)


def attend_kernel(
    place_ref, lengths_ref, tokens_ref, pool_ref, vec_ref,
    q_ref, k_ref, v_ref, ctx_ref, lse_ref, w_scr,
    sem,
):
    seq = pl.program_id(0)
    rows = tokens_ref.shape[0]

    @pl.when(seq == 0)
    def _():
        load_blocks(pool_ref, place_ref, 0, w_scr, sem)
        wait_whole(w_scr, sem)

    tokens = tokens_ref[...]
    q_ref[...] = ((mm(tokens, w_scr[0:D, :]) + vec_ref[0:1, :]).astype(jnp.bfloat16) * 0.125).astype(jnp.bfloat16)
    k_ref[...] = mm(tokens, w_scr[D : 2 * D, :]).astype(jnp.bfloat16)
    v_ref[...] = (mm(tokens, w_scr[2 * D :, :]) + vec_ref[1:2, :]).astype(jnp.bfloat16)
    key = lax.broadcasted_iota(jnp.int32, (rows, 1), 0)
    bias = jnp.where(key < lengths_ref[seq], 0.0, MASKED)

    def pair(p, _):
        forward_pair(q_ref, k_ref, v_ref, ctx_ref, lse_ref, 0, p, bias)
        return 0

    lax.fori_loop(0, PAIRS, pair, 0)


def attend(place, lengths, tokens, pool, vec):
    seqs, rows, _ = tokens.shape
    flat = tokens.reshape(seqs * rows, D)
    row_spec = pl.BlockSpec((rows, D), lambda s, *_: (s, 0))
    any_spec = pl.BlockSpec(memory_space=pl.ANY)
    low = jax.ShapeDtypeStruct((seqs * rows, D), jnp.bfloat16)
    return pl.pallas_call(
        attend_kernel,
        grid_spec=pltpu.PrefetchScalarGridSpec(
            num_scalar_prefetch=2,
            grid=(seqs,),
            in_specs=[row_spec, any_spec, pl.BlockSpec(vec.shape, lambda s, *_: (0, 0))],
            out_specs=[row_spec] * 4
            + [
                pl.BlockSpec((1, 16, rows), lambda s, *_: (s, 0, 0)),
                pl.BlockSpec((3 * D, D), lambda s, *_: (0, 0)),
            ],
            scratch_shapes=[pltpu.SemaphoreType.DMA],
        ),
        out_shape=[low] * 4
        + [
            jax.ShapeDtypeStruct((seqs, 16, rows), jnp.float32),
            jax.ShapeDtypeStruct((3 * D, D), jnp.bfloat16),
        ],
        compiler_params=pltpu.CompilerParams(vmem_limit_bytes=48 * MIB),
        cost_estimate=pl.CostEstimate(
            flops=6 * seqs * rows * D * D + 4 * seqs * rows * rows * D,
            bytes_accessed=10 * seqs * rows * D + 6 * D * D,
            transcendentals=seqs * rows * rows * H,
        ),
        name="attend",
    )(place, lengths, flat, pool, vec)


def gelu_parts(x):
    t_in = 1.0 + (0.3275911 * 0.7071067811865476) * jnp.abs(x)
    t = pltpu.reciprocal(t_in, approx=True)
    t = t * (2.0 - t_in * t)
    e = jnp.exp2((-0.5 * 1.4426950408889634) * (x * x))
    poly = (0.5 * 1.061405429) * t - (0.5 * 1.453152027)
    poly = poly * t + (0.5 * 1.421413741)
    poly = poly * t - (0.5 * 0.284496736)
    poly = poly * t + (0.5 * 0.254829592)
    tail = (poly * t) * e
    dist = jnp.where(x >= 0, 1.0 - tail, tail)
    return dist, x * (e * 0.3989422804014327)


def norm_stats(resid):
    center = resid - jnp.mean(resid, axis=-1, keepdims=True)
    scale = lax.rsqrt(jnp.mean(center * center, axis=-1, keepdims=True) + 1e-05)
    return center * scale, scale


def norm_back(d_out, gain, hat, scale):
    d_hat = d_out * gain
    mean_one = jnp.mean(d_hat, axis=-1, keepdims=True)
    mean_hat = jnp.mean(d_hat * hat, axis=-1, keepdims=True)
    return scale * (d_hat - mean_one - hat * mean_hat)


def feed_kernel(
    place_ref, lengths_ref, tokens_ref, ctx_ref, cot_ref, pool_ref, vec_ref,
    wide_mid_ref, mid_ref, out_ref, act_ref, dinner_ref, dfeed_ref, dbranch_ref, dctx_ref, grad_ref, sq_ref,
    w_out, w_up, w_down, slope_scr, sem, *, seq_rows,
):
    step = pl.program_id(0)
    rows = tokens_ref.shape[0]
    tiles = sq_ref.shape[0]
    first = 3 * D // BLK

    @pl.when(step == 0)
    def _():
        load_blocks(pool_ref, place_ref, first, w_out, sem.at[0])
        load_blocks(pool_ref, place_ref, first + D // BLK, w_up, sem.at[1])
        load_blocks(pool_ref, place_ref, first + (D + FF) // BLK, w_down, sem.at[2])
        wait_whole(w_out, sem.at[0])
        grad_ref[...] = jnp.zeros_like(grad_ref)

    def add_row(row, value):
        grad_ref[row : row + 1, :] += jnp.sum(value, axis=0, keepdims=True)

    segment = min(rows, seq_rows)
    row = lax.broadcasted_iota(jnp.int32, (rows, 1), 0)
    length = jnp.zeros((rows, 1), jnp.int32)
    for j in range(rows // segment):
        length = jnp.where(row // segment == j, lengths_ref[(step * rows + j * segment) // seq_rows], length)
    place_in = (step * rows + row) % seq_rows
    if seq_rows < SEQLEN:
        place_in += lax.axis_index("seq") * seq_rows
    valid = (place_in < length).astype(jnp.float32)

    def square_sums(which, value):
        square = value * value * valid
        for j in range(rows // segment):
            sq_ref[0, 2 * j + which : 2 * j + which + 1, :] = jnp.sum(
                square[j * segment : (j + 1) * segment], axis=0, keepdims=True
            )

    branch = mm(ctx_ref[...], w_out[...]) + vec_ref[2:3, :]
    square_sums(0, branch)
    hat1, scale1 = norm_stats(tokens_ref[...].astype(jnp.float32) + branch)
    middle = hat1 * vec_ref[4:5, :] + vec_ref[5:6, :]
    wide_mid_ref[...] = middle
    mid_ref[...] = middle.astype(jnp.bfloat16)
    mid_low = mid_ref[...]

    @pl.when(step == 0)
    def _():
        wait_whole(w_up, sem.at[1])

    parts = [slice(c * D, (c + 1) * D) for c in range(CHUNKS)]

    @pl.when(step == 0)
    def _():
        wait_whole(w_down, sem.at[2])

    feed = jnp.zeros((rows, D), jnp.float32) + vec_ref[3:4, :]
    for c in range(CHUNKS):
        inner = mm_nt(mid_low, w_up[parts[c], :]) + vec_ref[8 + c : 9 + c, :]
        dist, bell = gelu_parts(inner)
        act = (inner * dist).astype(jnp.bfloat16)
        act_ref[:, parts[c]] = act
        slope_scr[:, parts[c]] = dist + bell
        feed += mm(act, w_down[parts[c], :])
    square_sums(1, feed)
    hat2, scale2 = norm_stats(middle + feed)
    gain2 = vec_ref[6:7, :]
    out_ref[...] = (hat2 * gain2 + vec_ref[7:8, :]).astype(jnp.bfloat16)
    upstream = cot_ref[...].astype(jnp.float32) * valid
    add_row(6, upstream * hat2)
    add_row(7, upstream)
    d_res2 = norm_back(upstream, gain2, hat2, scale2)
    d_feed = d_res2.astype(jnp.bfloat16)
    dfeed_ref[...] = d_feed
    add_row(3, d_feed.astype(jnp.float32))
    d_mid = d_res2
    for c in range(CHUNKS):
        d_inner = (mm_nt(d_feed, w_down[parts[c], :]) * slope_scr[:, parts[c]]).astype(jnp.bfloat16)
        dinner_ref[:, parts[c]] = d_inner
        add_row(8 + c, d_inner.astype(jnp.float32))
        d_mid += mm(d_inner, w_up[parts[c], :])
    add_row(4, d_mid * hat1)
    add_row(5, d_mid)
    d_res1 = norm_back(d_mid, vec_ref[4:5, :], hat1, scale1)
    d_branch = d_res1.astype(jnp.bfloat16)
    dbranch_ref[...] = d_branch
    add_row(2, d_branch.astype(jnp.float32))
    dctx_ref[...] = mm_nt(d_branch, w_out[...]).astype(jnp.bfloat16)


def feed_both(place, lengths, seq_rows, tokens, ctx, cot, pool, vec, tile=256):
    total = tokens.shape[0]
    steps = total // tile
    row_spec = pl.BlockSpec((tile, D), lambda s, *_: (s, 0))
    wide_spec = pl.BlockSpec((tile, FF), lambda s, *_: (s, 0))
    any_spec = pl.BlockSpec(memory_space=pl.ANY)
    low = jax.ShapeDtypeStruct((total, D), jnp.bfloat16)
    wide = jax.ShapeDtypeStruct((total, FF), jnp.bfloat16)
    return pl.pallas_call(
        partial(feed_kernel, seq_rows=seq_rows),
        grid_spec=pltpu.PrefetchScalarGridSpec(
            num_scalar_prefetch=2,
            grid=(steps,),
            in_specs=[row_spec] * 3 + [any_spec, pl.BlockSpec(vec.shape, lambda s, *_: (0, 0))],
            out_specs=[row_spec, row_spec, row_spec, wide_spec, wide_spec, row_spec, row_spec, row_spec,
                pl.BlockSpec((16, D), lambda s, *_: (0, 0)),
                pl.BlockSpec((1, 8, D), lambda s, *_: (s, 0, 0))],
            scratch_shapes=[
                pltpu.VMEM((D, D), jnp.bfloat16),
                pltpu.VMEM((FF, D), jnp.bfloat16),
                pltpu.VMEM((FF, D), jnp.bfloat16),
                pltpu.VMEM((tile, FF), jnp.float32),
                pltpu.SemaphoreType.DMA((3,)),
            ],
        ),
        out_shape=[jax.ShapeDtypeStruct((total, D), jnp.float32), low, low, wide, wide, low, low, low,
            jax.ShapeDtypeStruct((16, D), jnp.float32),
            jax.ShapeDtypeStruct((steps, 8, D), jnp.float32)],
        compiler_params=pltpu.CompilerParams(vmem_limit_bytes=62 * MIB),
        cost_estimate=pl.CostEstimate(
            flops=8 * total * D * FF + 4 * total * D * D,
            bytes_accessed=total * (16 * D + 4 * FF) + 12 * FF * D,
            transcendentals=total * FF,
        ),
        name="feed_both",
    )(place, lengths, tokens, ctx, cot, pool, vec)


def send_blocks(value, held, slot, first, place_ref, out_ref, sem):
    held[slot] = value.astype(jnp.bfloat16).reshape(D // BLK, BLK, D)
    for i in range(D // BLK):
        pltpu.make_async_copy(
            held.at[slot, i], out_ref.at[place_ref[first + i]], sem.at[slot]
        ).start()


def feed_grads_kernel(
    place_ref, ctx_ref, dbranch_ref, dinner_ref, mid_ref, act_ref, dfeed_ref, out_ref, held, sem
):
    step = pl.program_id(0)
    slot = lax.rem(step, 2)
    base = 3 * D // BLK

    @pl.when(step >= 2)
    def _():
        wait_whole(held.at[slot], sem.at[slot])

    first = base + step * (D // BLK)

    @pl.when(step == 0)
    def _():
        send_blocks(mm_tn(ctx_ref[...], dbranch_ref[...]), held, slot, first, place_ref, out_ref, sem)

    @pl.when((step >= 1) & (step <= CHUNKS))
    def _():
        send_blocks(mm_tn(dinner_ref[...], mid_ref[...]), held, slot, first, place_ref, out_ref, sem)

    @pl.when(step > CHUNKS)
    def _():
        send_blocks(mm_tn(act_ref[...], dfeed_ref[...]), held, slot, first, place_ref, out_ref, sem)

    @pl.when(step == 2 * CHUNKS)
    def _():
        wait_whole(held.at[slot], sem.at[slot])
        wait_whole(held.at[1 - slot], sem.at[1 - slot])


def feed_grads(place, places, ctx, d_branch, d_inner, mid, act, d_feed):
    total = ctx.shape[0]
    whole = pl.BlockSpec((total, D), lambda s, *_: (0, 0))
    return pl.pallas_call(
        feed_grads_kernel,
        grid_spec=pltpu.PrefetchScalarGridSpec(
            num_scalar_prefetch=1,
            grid=(1 + 2 * CHUNKS,),
            in_specs=[
                whole,
                whole,
                pl.BlockSpec((total, D), lambda s, *_: (0, jnp.clip(s - 1, 0, CHUNKS - 1))),
                whole,
                pl.BlockSpec((total, D), lambda s, *_: (0, jnp.clip(s - 1 - CHUNKS, 0, CHUNKS - 1))),
                whole,
            ],
            out_specs=pl.BlockSpec(memory_space=pl.ANY),
            scratch_shapes=[
                pltpu.VMEM((2, D // BLK, BLK, D), jnp.bfloat16),
                pltpu.SemaphoreType.DMA((2,)),
            ],
        ),
        out_shape=jax.ShapeDtypeStruct((places, BLK, D), jnp.bfloat16),
        compiler_params=pltpu.CompilerParams(vmem_limit_bytes=48 * MIB),
        cost_estimate=pl.CostEstimate(
            flops=4 * total * D * FF + 2 * total * D * D,
            bytes_accessed=total * (8 * D + 4 * FF) + 4 * FF * D,
            transcendentals=0,
        ),
        name="feed_grads",
    )(place, ctx, d_branch, d_inner, mid, act, d_feed)


def attend_back_kernel(
    place_w_ref, place_ref, lengths_ref, tokens_ref, q_ref, k_ref, v_ref, ctx_ref, dctx_ref, lse_ref, dres_ref, pool_ref, held_in,
    ingrad_ref, vec_ref, out_ref,
    w_scr, dq_scr, dk_scr, dv_scr, total_scr, held, sem, w_sem,
):
    seq = pl.program_id(0)
    last = pl.num_programs(0) - 1
    rows = tokens_ref.shape[0]

    @pl.when(seq == 0)
    def _():
        load_blocks(pool_ref, place_w_ref, 0, w_scr, w_sem)
        vec_ref[...] = jnp.zeros_like(vec_ref)

    key = lax.broadcasted_iota(jnp.int32, (rows, 1), 0)
    bias = jnp.where(key < lengths_ref[seq], 0.0, MASKED)

    def pair(p, _):
        cols, d_query, d_key, d_value = back_pair(q_ref, k_ref, v_ref, ctx_ref, dctx_ref, lse_ref, 0, p, bias)
        dq_scr[:, cols] = d_query
        dk_scr[:, cols] = d_key
        dv_scr[:, cols] = d_value
        return 0

    lax.fori_loop(0, PAIRS, pair, 0)

    @pl.when(seq == 0)
    def _():
        wait_whole(w_scr, w_sem)

    dq, dk, dv = dq_scr[...], dk_scr[...], dv_scr[...]
    vec_ref[0:1, :] += jnp.sum(dq.astype(jnp.float32), axis=0, keepdims=True)
    vec_ref[1:2, :] += jnp.sum(dv.astype(jnp.float32), axis=0, keepdims=True)
    ingrad = dres_ref[...].astype(jnp.float32) + mm_nt(dq, w_scr[0:D, :])
    ingrad += mm_nt(dk, w_scr[D : 2 * D, :])
    ingrad += mm_nt(dv, w_scr[2 * D :, :])
    ingrad_ref[...] = ingrad.astype(jnp.bfloat16)
    tokens = tokens_ref[...]
    for i, right in enumerate((dq, dk, dv)):
        part = slice(i * D, (i + 1) * D)

        @pl.when(seq == 0)
        def _():
            total_scr[part, :] = mm_tn(tokens, right)

        @pl.when(seq > 0)
        def _():
            total_scr[part, :] += mm_tn(tokens, right)

    @pl.when(seq == last)
    def _():
        for i in range(3):
            send_blocks(total_scr[i * D : (i + 1) * D, :], held, i, i * (D // BLK), place_ref, out_ref, sem)
        for i in range(3):
            wait_whole(held.at[i], sem.at[i])


def attend_back(place_w, place, lengths, tokens, q, k, v, ctx, d_ctx, lse, d_res, pool, held):
    seqs, rows, _ = tokens.shape
    flat = tokens.reshape(seqs * rows, D)
    row_spec = pl.BlockSpec((rows, D), lambda s, *_: (s, 0))
    any_spec = pl.BlockSpec(memory_space=pl.ANY)
    return pl.pallas_call(
        attend_back_kernel,
        grid_spec=pltpu.PrefetchScalarGridSpec(
            num_scalar_prefetch=3,
            grid=(seqs,),
            in_specs=[row_spec] * 6
            + [pl.BlockSpec((1, 16, rows), lambda s, *_: (s, 0, 0)), row_spec, any_spec, any_spec],
            out_specs=[row_spec, pl.BlockSpec((8, D), lambda s, *_: (0, 0)), any_spec],
            scratch_shapes=[
                pltpu.VMEM((3 * D, D), jnp.bfloat16),
                pltpu.VMEM((rows, D), jnp.bfloat16),
                pltpu.VMEM((rows, D), jnp.bfloat16),
                pltpu.VMEM((rows, D), jnp.bfloat16),
                pltpu.VMEM((3 * D, D), jnp.float32),
                pltpu.VMEM((3, D // BLK, BLK, D), jnp.bfloat16),
                pltpu.SemaphoreType.DMA((3,)),
                pltpu.SemaphoreType.DMA,
            ],
        ),
        out_shape=[
            jax.ShapeDtypeStruct((seqs * rows, D), jnp.bfloat16),
            jax.ShapeDtypeStruct((8, D), jnp.float32),
            jax.ShapeDtypeStruct(held.shape, held.dtype),
        ],
        input_output_aliases={12: 2},
        compiler_params=pltpu.CompilerParams(vmem_limit_bytes=62 * MIB),
        cost_estimate=pl.CostEstimate(
            flops=12 * seqs * rows * D * D + 10 * seqs * rows * rows * D,
            bytes_accessed=20 * seqs * rows * D + 12 * D * D,
            transcendentals=seqs * rows * rows * H,
        ),
        name="attend_back",
    )(place_w, place, lengths, flat, q, k, v, ctx, d_ctx, lse, d_res, pool, held)


def adam_kernel(
    place_ref, has_ref, *refs, per
):
    moment_ref, second_ref, master_ref, dres_ref, part_ref, rms_ref, vec_ref = refs[per : per + 7]
    vec_moment_ref, vec_second_ref, vec_master_ref = refs[per + 7 : per + 10]
    ingrad_out, rms_out, grad_out, moment_out, second_out, master_out = refs[per + 10 : per + 16]
    vec_out, vec_moment_out, vec_second_out, vec_master_out = refs[per + 16 :]
    step = pl.program_id(0)
    for j, grad_in in enumerate(refs[:per]):
        got = grad_in[0].astype(jnp.float32)
        gradient = jnp.where(has_ref[per * step + j] > 0, got, jnp.zeros_like(got))
        grad_out[j] = gradient
        moment_out[j], second_out[j], master_out[j] = adam_step(
            gradient, moment_ref[j], second_ref[j], master_ref[j], matrix_rate
        )
    ingrad_out[...] = dres_ref[...].astype(jnp.float32) + part_ref[...].astype(jnp.float32)

    @pl.when(step == 0)
    def _():
        rms_out[...] = rms_ref[:, 0:2]
        gradient = vec_ref[0 : vec_out.shape[0], :]
        vec_out[...] = gradient
        vec_moment_out[...], vec_second_out[...], vec_master_out[...] = adam_step(
            gradient, vec_moment_ref[...], vec_second_ref[...], vec_master_ref[...], vector_rate
        )


def adam_all(place, has, reduced, moment, second, master, d_res, part, rms, vec, vec_moment, vec_second, vec_master):
    slots = master.shape[0]
    per = 3 if slots % 3 == 0 else 2
    steps = slots // per
    total = d_res.shape[0]
    pieces = 1
    while 2 * pieces <= steps:
        pieces *= 2
    some = pl.BlockSpec((per, BLK, D), lambda s, *_: (s, 0, 0))
    rows = pl.BlockSpec((total // pieces, D), lambda s, *_: (jnp.minimum(s, pieces - 1), 0))

    def whole(shape):
        return pl.BlockSpec(shape, lambda s, *_: (0, 0))

    full = jax.ShapeDtypeStruct(master.shape, jnp.float32)
    vec_full = jax.ShapeDtypeStruct(vec_master.shape, jnp.float32)
    return pl.pallas_call(
        partial(adam_kernel, per=per),
        grid_spec=pltpu.PrefetchScalarGridSpec(
            num_scalar_prefetch=2,
            grid=(steps,),
            in_specs=[
                pl.BlockSpec((1, BLK, D), partial(lambda j, s, place, has: (place[per * s + j], 0, 0), j))
                for j in range(per)
            ]
            + [some] * 3
            + [rows] * 2
            + [whole(rms.shape), whole(vec.shape)]
            + [whole(vec_master.shape)] * 3,
            out_specs=[rows, whole((rms.shape[0], 2))] + [some] * 4 + [whole(vec_master.shape)] * 4,
        ),
        out_shape=[
            jax.ShapeDtypeStruct(d_res.shape, jnp.float32),
            jax.ShapeDtypeStruct((rms.shape[0], 2), jnp.float32),
        ]
        + [full] * 4
        + [vec_full] * 4,
        compiler_params=pltpu.CompilerParams(vmem_limit_bytes=60 * MIB),
        cost_estimate=pl.CostEstimate(
            flops=20 * slots * BLK * D, bytes_accessed=30 * slots * BLK * D, transcendentals=2 * slots * BLK * D
        ),
        name="adam_all",
    )(place, has, *(reduced,) * per, moment, second, master, d_res, part, rms, vec, vec_moment, vec_second, vec_master)


class Plan:
    def __init__(self, early, middle, late, first, ids):
        self.early, self.middle, self.late, self.first, self.ids = early, middle, late, first, ids
        self.listed = early + middle + late


TIGHT = Plan(4, 8, 10, 10, (3, 4))
LOOSE = Plan(6, 8, 10, 10, (1, 2))
HEAD_BLOCKS = 3 * D // BLK
MESH = pl.DeviceIdType.MESH


class Place:
    def __init__(self):
        dp = lax.axis_index("dp")
        self.z = lax.axis_index("seq")
        self.core = dp % 2
        x = (dp // 2) % 2
        y = dp // 4
        self.chip = dp // 2
        self.chip_x = 2 * y + 1 - x
        self.chip_y = 2 * (1 - y) + x
        self.chip_xy = 2 * (1 - y) + 1 - x
        self.to_core = {"dp": dp + 1 - 2 * self.core}
        self.to_x = {"dp": dp + 2 - 4 * x}
        self.to_y = {"dp": dp + 4 - 8 * y}
        z = self.z
        self.z_hops = (z + 1 - 2 * (z % 2), (z + 2) % 4, 3 - z)
        self.to_z = tuple({"seq": hop} for hop in self.z_hops)
        self.partners = (self.to_core, self.to_x, self.to_y) + self.to_z

    def meet(self):
        barrier = pltpu.get_barrier_semaphore()
        for partner in self.partners:
            pl.semaphore_signal(barrier, inc=1, device_id=partner, device_id_type=MESH)
        pl.semaphore_wait(barrier, len(self.partners))


class Sender:
    def __init__(self, send_sem, recv_sem):
        self.send_sem, self.recv_sem = send_sem, recv_sem

    def copy(self, k, src, dst, partner):
        return pltpu.make_async_remote_copy(
            src_ref=src,
            dst_ref=dst,
            send_sem=self.send_sem.at[k],
            recv_sem=self.recv_sem.at[k],
            device_id=partner,
            device_id_type=MESH,
        )


class Gather:
    def __init__(self, here, sender, first_sem, count, own, own_row, pool, row_of):
        self.here, self.sender, self.k, self.n = here, sender, first_sem, count
        self.own, self.own_row, self.pool, self.row_of = own, own_row, pool, row_of
        self.half = count * BLK // 2

    def link(self, name):
        here, half = self.here, self.half

        def own(part):
            return self.own.at[pl.ds(self.own_row + part * half, half)]

        def piece(chip, part):
            return self.pool.at[pl.ds(self.row_of(chip, here.core) + part * half, half)]

        def whole(chip):
            return self.pool.at[pl.ds(self.row_of(chip, here.core), 2 * half)]

        order = ("x0", "x1", "y1", "y0", "y_on", "x_on", "share_x", "share_y", "share_xy", "share_me")
        src, dst, partner = {
            "x0": lambda: (own(0), piece(here.chip, 0), here.to_x),
            "x1": lambda: (own(1), piece(here.chip, 1), here.to_x),
            "y1": lambda: (own(1), piece(here.chip, 1), here.to_y),
            "y0": lambda: (own(0), piece(here.chip, 0), here.to_y),
            "y_on": lambda: (piece(here.chip_x, 0), piece(here.chip_x, 0), here.to_y),
            "x_on": lambda: (piece(here.chip_y, 1), piece(here.chip_y, 1), here.to_x),
            "share_x": lambda: (whole(here.chip_x), whole(here.chip_x), here.to_core),
            "share_y": lambda: (whole(here.chip_y), whole(here.chip_y), here.to_core),
            "share_xy": lambda: (whole(here.chip_xy), whole(here.chip_xy), here.to_core),
            "share_me": lambda: (
                self.own.at[pl.ds(self.own_row, 2 * half)], whole(here.chip), here.to_core
            ),
        }[name]()
        return self.sender.copy(self.k + order.index(name), src, dst, partner)

    def start(self):
        for name in ("x0", "y1", "x1", "y0", "share_me"):
            self.link(name).start()

    def pass_on(self):
        self.link("x0").wait_recv()
        self.link("y_on").start()
        self.link("y1").wait_recv()
        self.link("x_on").start()

    def share_near(self):
        self.link("x1").wait_recv()
        self.link("share_x").start()
        self.link("y0").wait_recv()
        self.link("share_y").start()

    def sent(self):
        for name in ("x0", "y1", "x1", "y0", "y_on", "x_on"):
            self.link(name).wait_send()

    def share_far(self):
        self.link("y_on").wait_recv()
        self.link("x_on").wait_recv()
        self.link("share_xy").start()

    def finish(self):
        for name in ("share_me", "share_x", "share_y", "share_xy"):
            self.link(name).wait_recv()

    def shared(self):
        for name in ("share_me", "share_x", "share_y", "share_xy"):
            self.link(name).wait_send()


def front_kernel(
    place_ref, mine_ref, lengths_ref, vec_ref, master_in, tokens_in,
    pool, q_out, k_out, v_out, ctx_out, w_out, tok_out, ctx_split, lse_ref,
    stage, give, take, near, pack, w, tok, qs, ks, vs, cs,
    send_sem, recv_sem, load_sem,
    *, plan,
):
    here = Place()
    z = here.z
    sender = Sender(send_sem, recv_sem)
    rows = SEQLEN
    own = tokens_in.shape[0] // 4
    part = tokens_in.shape[1]
    slots = master_in.shape[0]
    second = plan.listed - plan.first

    def local(src, dst, k):
        return pltpu.make_async_copy(src, dst, load_sem.at[k])

    load_master = local(master_in, stage, 0)
    load_master.start()
    own_tokens = [
        local(tokens_in.at[own * z + s], tok.at[pl.ds(s * rows + part * z, part)], 3 + s) for s in range(own)
    ]
    for load in own_tokens:
        load.start()
    here.meet()
    swaps = [
        sender.copy(
            own * hop + s,
            tokens_in.at[own * here.z_hops[hop] + s],
            tok.at[pl.ds(s * rows + part * z, part)],
            here.to_z[hop],
        )
        for hop in range(3)
        for s in range(own)
    ]
    for swap in swaps:
        swap.start()
    parts = (plan.first // 2, second // 2)
    starts = (0, plan.first)
    trades = [
        sender.copy(
            6 + i,
            give.at[pl.ds(i * parts[0] * BLK, parts[i] * BLK)],
            take.at[pl.ds(i * parts[0] * BLK, parts[i] * BLK)],
            here.to_core,
        )
        for i in range(2)
    ]
    load_master.wait()

    def held(entry):
        return stage[jnp.clip(mine_ref[entry] - here.core * slots, 0, slots - 1)].astype(jnp.bfloat16)

    for i in range(2):

        def fill_give(p, _):
            give[pl.ds((i * parts[0] + p) * BLK, BLK), :] = held(starts[i] + (1 - here.core) * parts[i] + p)
            return 0

        lax.fori_loop(0, parts[i], fill_give, 0)
        trades[i].start()

    def own_block(i, p):
        entry = starts[i] + here.core * parts[i] + p
        traded = take[pl.ds((i * parts[0] + p) * BLK, BLK), :]
        return jnp.where(mine_ref[entry] // slots == here.core, held(entry), traded)

    trades[0].wait_recv()

    def fill_near(p, _):
        near[pl.ds((here.chip * plan.first + here.core * parts[0] + p) * BLK, BLK), :] = own_block(0, p)
        return 0

    lax.fori_loop(0, parts[0], fill_near, 0)
    first = Gather(
        here, sender, 8, plan.first // 2, near, (here.chip * plan.first + here.core * (plan.first // 2)) * BLK, near,
        lambda chip, core: (chip * plan.first + core * (plan.first // 2)) * BLK,
    )
    then = Gather(
        here, sender, 18, second // 2, pack, 0, pool,
        lambda chip, core: (chip * plan.listed + plan.first + core * (second // 2)) * BLK,
    )
    first.start()

    trades[1].wait_recv()

    def fill_pack(p, _):
        pack[pl.ds(p * BLK, BLK), :] = own_block(1, p)
        return 0

    lax.fori_loop(0, parts[1], fill_pack, 0)
    own_second = local(
        pack, pool.at[pl.ds((here.chip * plan.listed + plan.first + here.core * parts[1]) * BLK, parts[1] * BLK)], 5
    )
    own_second.start()
    first.pass_on()
    first.share_near()
    first.sent()
    then.start()
    first.share_far()
    first.finish()

    def fill_w(b, _):
        at = place_ref[b]
        w[pl.ds(b * BLK, BLK), :] = near[pl.ds(((at // plan.listed) * plan.first + at % plan.listed) * BLK, BLK), :]
        return 0

    lax.fori_loop(0, HEAD_BLOCKS, fill_w, 0)
    keeps = [
        local(near.at[pl.ds(chip * plan.first * BLK, plan.first * BLK)], pool.at[pl.ds(chip * plan.listed * BLK, plan.first * BLK)], 6 + chip)
        for chip in range(4)
    ] + [local(w, w_out, 10)]
    for keep in keeps:
        keep.start()
    for load in own_tokens:
        load.wait()
    for swap in swaps:
        swap.wait_recv()
    keep_tok = local(tok, tok_out, 11)
    keep_tok.start()

    def send_ctx(s, hop):
        return sender.copy(
            28 + 3 * s + hop,
            cs.at[pl.ds(s * rows + part * here.z_hops[hop], part)],
            ctx_split.at[own * z + s],
            here.to_z[hop],
        )

    def keep_own(s):
        at = pl.ds(s * rows, rows)
        return [local(ref.at[at], out.at[at], 12 + k) for k, (ref, out) in enumerate(((qs, q_out), (ks, k_out), (vs, v_out), (cs, ctx_out)))] + [
            local(cs.at[pl.ds(s * rows + part * z, part)], ctx_split.at[own * z + s], 16)
        ]

    key = lax.broadcasted_iota(jnp.int32, (rows, 1), 0)

    def sequence(s, _):
        at = pl.ds(pl.multiple_of(s * rows, rows), rows)
        values = tok[at, :]
        qs[at, :] = ((mm(values, w[0:D, :]) + vec_ref[0:1, :]).astype(jnp.bfloat16) * 0.125).astype(jnp.bfloat16)
        ks[at, :] = mm(values, w[D : 2 * D, :]).astype(jnp.bfloat16)
        vs[at, :] = (mm(values, w[2 * D :, :]) + vec_ref[1:2, :]).astype(jnp.bfloat16)
        bias = jnp.where(key < lengths_ref[own * z + s], 0.0, MASKED)

        def pair(p, _):
            forward_pair(qs.at[at], ks.at[at], vs.at[at], cs.at[at], lse_ref, s, p, bias)
            return 0

        lax.fori_loop(0, PAIRS, pair, 0)
        for hop in range(3):
            send_ctx(s, hop).start()

        @pl.when(s > 0)
        def _():
            for keep in keep_own(s - 1):
                keep.wait()

        for keep in keep_own(s):
            keep.start()

        @pl.when(s == 0)
        def _():
            then.pass_on()

        return 0

    lax.fori_loop(0, own, sequence, 0)
    then.share_near()
    then.share_far()
    then.sent()
    then.finish()
    for keep in keep_own(own - 1) + keeps + [keep_tok, own_second]:
        keep.wait()
    for s in range(own):
        for hop in range(3):
            send_ctx(s, hop).wait_recv()
            send_ctx(s, hop).wait_send()
    for copy in swaps + trades:
        copy.wait_send()
    first.shared()
    then.shared()


def front(plan, place, mine, lengths, vec, master, tokens):
    seqs, part, _ = tokens.shape
    total = seqs * part
    own = total // SEQLEN
    any_spec = pl.BlockSpec(memory_space=pl.ANY)
    vmem = pl.BlockSpec(memory_space=pltpu.VMEM)
    smem = pl.BlockSpec(memory_space=pltpu.SMEM)
    low = jnp.bfloat16
    slots = master.shape[0]
    flat = jax.ShapeDtypeStruct((total, D), low)
    return pl.pallas_call(
        partial(front_kernel, plan=plan),
        in_specs=[smem] * 3 + [vmem] + [any_spec] * 2,
        out_specs=[any_spec] * 8 + [vmem],
        out_shape=[
            jax.ShapeDtypeStruct((4 * plan.listed * BLK, D), low),
            flat,
            flat,
            flat,
            flat,
            jax.ShapeDtypeStruct((3 * D, D), low),
            flat,
            jax.ShapeDtypeStruct(tokens.shape, low),
            jax.ShapeDtypeStruct((own, 16, SEQLEN), jnp.float32),
        ],
        scratch_shapes=[
            pltpu.VMEM(master.shape, jnp.float32),
            pltpu.VMEM((plan.listed // 2 * BLK, D), low),
            pltpu.VMEM((plan.listed // 2 * BLK, D), low),
            pltpu.VMEM((4 * plan.first * BLK, D), low),
            pltpu.VMEM(((plan.listed - plan.first) // 2 * BLK, D), low),
            pltpu.VMEM((3 * D, D), low),
        ]
        + [pltpu.VMEM((total, D), low)] * 5
        + [
            pltpu.SemaphoreType.DMA((34,)),
            pltpu.SemaphoreType.DMA((34,)),
            pltpu.SemaphoreType.DMA((17,)),
        ],
        compiler_params=pltpu.CompilerParams(
            vmem_limit_bytes=60 * MIB, collective_id=plan.ids[1], has_side_effects=True
        ),
        cost_estimate=pl.CostEstimate(
            flops=6 * total * D * D + 4 * total * SEQLEN * D,
            bytes_accessed=40 * total * D + 8 * slots * BLK * D,
            transcendentals=total * SEQLEN * H,
        ),
        name="front",
    )(place, mine, lengths, vec, master, tokens)


def add_rows(out_ref, out_row, terms, count, step=32):
    def body(i, _):
        value = None
        for ref, row in terms:
            part = ref[pl.ds(pl.multiple_of(row + i * step, step), step), :]
            value = part if value is None else value + part
        out_ref[pl.ds(pl.multiple_of(out_row + i * step, step), step), :] = value
        return 0

    lax.fori_loop(0, count // step, body, 0, unroll=2)


class Reduce:
    def __init__(self, plan, here, sender, first_sem, count, first, column, blk_ref, grad, pack, buffers, red):
        self.here, self.sender, self.k, self.listed = here, sender, first_sem, plan.listed
        self.n, self.first, self.blk, self.grad = count, first, blk_ref, grad
        self.acc, self.rx, self.ry, self.r2, self.z1, self.z2, self.fin = buffers
        self.red = red
        self.half = count * BLK // 2
        self.size = count * BLK
        self.cols = pl.ds(column, self.fin.shape[1])
        self.pack = pack.at[pl.ds(0, 4 * self.size), self.cols]

    def rows(self, ref, chip, half):
        return ref.at[pl.ds(chip * self.size + half * self.half, self.half)]

    def link(self, name):
        here, k, acc = self.here, self.k, self.acc
        keep = (here.z % 2) * self.half
        other = (1 - here.z % 2) * self.half
        mine = here.chip * self.size
        fin_keep = self.fin.at[pl.ds(keep, self.half)]
        order = (
            "core_xy", "core_x", "core_y", "core_me", "x_far", "x_near", "y_far", "y_near",
            "y_on", "x_on", "z_half", "z_far", "z_back", "share",
        )

        def across(chip):
            rows = pl.ds(chip * self.size, self.size)
            return self.pack.at[rows], acc.at[rows], here.to_core

        src, dst, partner = {
            "core_xy": lambda: across(here.chip_xy),
            "core_x": lambda: across(here.chip_x),
            "core_y": lambda: across(here.chip_y),
            "core_me": lambda: across(here.chip),
            "x_far": lambda: (self.rows(acc, here.chip_xy, 0), self.rx.at[1], here.to_x),
            "x_near": lambda: (self.rows(acc, here.chip_x, 0), self.rx.at[0], here.to_x),
            "y_far": lambda: (self.rows(acc, here.chip_xy, 1), self.ry.at[1], here.to_y),
            "y_near": lambda: (self.rows(acc, here.chip_y, 1), self.ry.at[0], here.to_y),
            "y_on": lambda: (self.rows(acc, here.chip_y, 0), self.r2.at[0], here.to_y),
            "x_on": lambda: (self.rows(acc, here.chip_x, 1), self.r2.at[1], here.to_x),
            "z_half": lambda: (acc.at[pl.ds(mine + other, self.half)], self.z1, here.to_z[0]),
            "z_far": lambda: (acc.at[pl.ds(mine + keep, self.half)], self.z2, here.to_z[1]),
            "z_back": lambda: (fin_keep, fin_keep, here.to_z[0]),
            "share": lambda: (self.fin, self.result(), here.to_core),
        }[name]()
        return self.sender.copy(k + order.index(name), src, dst, partner)

    def result(self):
        return self.red.at[pl.ds((self.first + self.here.core * self.n) * BLK, self.size), self.cols]

    def start_core(self):
        here, n = self.here, self.n
        chips = (here.chip_xy, here.chip_x, here.chip_y, here.chip)
        for chip, name in zip(chips, ("core_xy", "core_x", "core_y", "core_me")):

            def body(i, _):
                block = self.blk[chip * self.listed + self.first + (1 - here.core) * n + i]
                self.pack[pl.ds(chip * self.size + i * BLK, BLK), :] = self.grad[block, :, self.cols]
                return 0

            lax.fori_loop(0, n, body, 0)
            self.link(name).start()

    def sent_core(self):
        for name in ("core_xy", "core_x", "core_y", "core_me"):
            self.link(name).wait_send()

    def add_own(self, chip):
        here, n = self.here, self.n

        def body(i, _):
            entry = chip * self.listed + self.first + here.core * n + i
            block = self.blk[entry]
            for piece in range(0, BLK, 32):
                rows = pl.ds(pl.multiple_of(chip * self.size + i * BLK, BLK) + piece, 32)
                self.acc[rows, :] = self.acc[rows, :] + self.grad[block, piece : piece + 32, self.cols]
            return 0

        lax.fori_loop(0, n, body, 0)

    def start_far(self):
        self.link("core_xy").wait_recv()
        self.add_own(self.here.chip_xy)
        self.link("x_far").start()
        self.link("y_far").start()

    def start_near(self):
        self.link("core_x").wait_recv()
        self.add_own(self.here.chip_x)
        self.link("x_near").start()
        self.link("core_y").wait_recv()
        self.add_own(self.here.chip_y)
        self.link("y_near").start()

    def pass_plane(self):
        here = self.here
        self.link("x_far").wait_recv()
        at = here.chip_y * self.size
        add_rows(self.acc, at, ((self.acc, at), (self.rx.at[1], 0)), self.half)
        self.link("y_on").start()
        self.link("y_far").wait_recv()
        at = here.chip_x * self.size + self.half
        add_rows(self.acc, at, ((self.acc, at), (self.ry.at[1], 0)), self.half)
        self.link("x_on").start()

    def start_z(self):
        here = self.here
        mine = here.chip * self.size
        self.link("core_me").wait_recv()
        self.add_own(here.chip)
        self.link("x_near").wait_recv()
        self.link("y_on").wait_recv()
        add_rows(self.acc, mine, ((self.acc, mine), (self.rx.at[0], 0), (self.r2.at[0], 0)), self.half)
        self.link("y_near").wait_recv()
        self.link("x_on").wait_recv()
        low = mine + self.half
        add_rows(self.acc, low, ((self.acc, low), (self.ry.at[0], 0), (self.r2.at[1], 0)), self.half)
        self.link("z_half").start()

    def far_z(self):
        here = self.here
        keep = here.chip * self.size + (here.z % 2) * self.half
        self.link("z_half").wait_recv()
        add_rows(self.acc, keep, ((self.acc, keep), (self.z1, 0)), self.half)
        self.link("z_far").start()

    def back_z(self):
        here = self.here
        keep = (here.z % 2) * self.half
        self.link("z_far").wait_recv()
        add_rows(self.fin, keep, ((self.acc, here.chip * self.size + keep), (self.z2, 0)), self.half)
        self.link("z_back").start()

    def share(self, local_sem):
        red = self.result()
        self.link("z_back").wait_recv()
        self.link("z_back").wait_send()
        self.link("share").start()
        pltpu.make_async_copy(self.fin, red, local_sem).start()

    def finish(self, local_sem):
        red = self.result()
        self.link("share").wait_recv()
        pltpu.make_async_copy(self.fin, red, local_sem).wait()
        for name in ("x_far", "x_near", "y_far", "y_near", "y_on", "x_on", "z_half", "z_far", "share"):
            self.link(name).wait_send()


def back_pair(q_ref, k_ref, v_ref, ctx_ref, do_ref, lse_ref, seq, p, bias):
    rows = q_ref.shape[0]
    cols = pl.ds(pl.multiple_of(p * LANES, LANES), LANES)
    row8 = lax.broadcasted_iota(jnp.int32, (16, rows), 0)

    def extra_rows(lead, row):
        one, two, three = (part.astype(jnp.float32) for part in split3(row))
        return jnp.where(
            row8 == 0, lead, jnp.where(row8 == 1, one, jnp.where(row8 == 2, two, jnp.where(row8 == 3, three, 0.0)))
        )

    q2, k2, v2, do2 = q_ref[:, cols], k_ref[:, cols], v_ref[:, cols], do_ref[:, cols]
    q2t, k2t, do2t = q2.T, k2.T, do2.T
    prod = do2t.astype(jnp.float32) * ctx_ref[:, cols].T.astype(jnp.float32)
    dq_parts = []
    d_key = jnp.zeros((rows, LANES), jnp.float32)
    d_value = jnp.zeros((rows, LANES), jnp.float32)
    for half in range(2):
        head = slice(half * DH, half * DH + DH)
        inside, spare = spare_lanes(rows, half, bias)
        zero = jnp.zeros_like(k2)
        lse = lse_ref[seq, pl.ds(2 * p + half, 1), :]
        delta = jnp.sum(prod[head], axis=0, keepdims=True)
        scores = mm(jnp.where(inside, k2, spare), beside(q2t[head], extra_rows(1.0, -lse), half))
        probs = jnp.exp(scores)
        d_probs = mm(jnp.where(inside, v2, spare), beside(do2t[head], extra_rows(0.0, -delta), half))
        d_scores = (probs * d_probs).astype(jnp.bfloat16)
        d_value += mm(probs.astype(jnp.bfloat16), jnp.where(inside, do2, zero))
        d_key += mm(d_scores, jnp.where(inside, q2, zero))
        dq_parts.append(mm(k2t[head], d_scores))
    d_query = jnp.concatenate(dq_parts, axis=0).T * 0.125
    return cols, d_query.astype(jnp.bfloat16), d_key.astype(jnp.bfloat16), d_value.astype(jnp.bfloat16)


def tail_kernel(
    blk_ref, lengths_ref, vec_in, squares_in, lse_ref,
    dctx_in, ctx_split, dbranch, dinner, mid, act, dfeed, tok_in, q_in, k_in, v_in, ctx_in, w_in,
    red, ingrad, vec_out, rms_out,
    grad, pack, d3, att, tok, w, *rest, plan,
):
    here = Place()
    z = here.z
    phase_buffers = [rest[7 * i : 7 * i + 7] for i in range(4)]
    vec_src, vec_land, rms_src, rms_land, send_sem, recv_sem, load_sem = rest[28:]
    sender = Sender(send_sem, recv_sem)
    rows = SEQLEN
    own = dctx_in.shape[0] // 4
    part = dctx_in.shape[1]
    total = own * rows
    wide = D // 2

    def local(src, dst, k):
        return pltpu.make_async_copy(src, dst, load_sem.at[k])

    first_loads = (
        local(ctx_split, att.at[2], 0),
        local(dinner.at[:, pl.ds(0, D)], att.at[3], 1),
        local(dbranch, d3.at[0], 2),
        local(mid, d3.at[1], 3),
        local(dfeed, d3.at[2], 4),
        local(q_in, att.at[0], 5),
        local(k_in, att.at[1], 6),
        local(tok_in, tok, 7),
        local(w_in, w, 10),
    )
    for load in first_loads[:5]:
        load.start()
    here.meet()

    def swap(half, s, hop):
        cols = pl.ds(half * wide, wide)
        return sender.copy(
            6 * half + 3 * s + hop,
            dctx_in.at[own * here.z_hops[hop] + s, :, cols],
            att.at[4, pl.ds(s * rows + part * z, part), cols],
            here.to_z[hop],
        )

    swaps = [[swap(half, s, hop) for s in range(own) for hop in range(3)] for half in range(2)]
    own_swaps = [local(dctx_in.at[own * z + s], att.at[4, pl.ds(s * rows + part * z, part)], 8 + s) for s in range(own)]
    for copy in swaps[0] + own_swaps:
        copy.start()
    for load in first_loads[2:5]:
        load.wait()

    early, middle = (
        Reduce(plan, here, sender, 24 + 14 * i, count // 2, first, 0, blk_ref, grad, pack, phase_buffers[i], red)
        for i, (count, first) in enumerate(((plan.early, 0), (plan.middle, plan.early)))
    )
    late = [
        Reduce(plan, here, sender, 52 + 14 * i, plan.late // 2, plan.early + plan.middle, i * wide, blk_ref, grad, pack, phase_buffers[2 + i], red)
        for i in range(2)
    ]

    def grads(step, _):
        slot = 2 + step % 2
        held = att.at[slot]
        pltpu.make_async_copy(held, held, load_sem.at[step % 2]).wait()
        value = mm_tn(att[slot], d3[(step + 3) // 4])
        grad[pl.ds(HEAD_BLOCKS + step * (D // BLK), D // BLK)] = value.astype(jnp.bfloat16).reshape(D // BLK, BLK, D)

        @pl.when(step < CHUNKS - 1)
        def _():
            local(dinner.at[:, pl.ds((step + 1) * D, D)], held, step % 2).start()

        @pl.when((step >= CHUNKS - 1) & (step < 2 * CHUNKS - 1))
        def _():
            local(act.at[:, pl.ds((step - CHUNKS + 1) * D, D)], held, step % 2).start()

        @pl.when(step == CHUNKS)
        def _():
            early.start_core()

        @pl.when(step == CHUNKS + 1)
        def _():
            for copy in swaps[0]:
                copy.wait_send()
            for copy in swaps[1]:
                copy.start()

        @pl.when(step == CHUNKS + 2)
        def _():
            early.start_far()

        @pl.when(step == CHUNKS + 3)
        def _():
            early.start_near()

        return 0

    for load in first_loads[5:]:
        load.start()
    grad[0:HEAD_BLOCKS] = jnp.zeros((HEAD_BLOCKS, BLK, D), jnp.bfloat16)
    lax.fori_loop(0, 1 + 2 * CHUNKS, grads, 0)
    more_loads = (local(v_in, att.at[2], 0), local(ctx_in, att.at[3], 1))
    for load in more_loads:
        load.start()
    early.sent_core()
    middle.start_core()
    for load in first_loads[5:] + tuple(own_swaps) + more_loads:
        load.wait()
    for copy in swaps[0]:
        copy.wait_recv()

    key = lax.broadcasted_iota(jnp.int32, (rows, 1), 0)

    def head_grads(half):
        cols = pl.ds(half * wide, wide)
        for block, which in ((0, 1), (6, 2), (12, 0)):
            value = mm_tn(tok[...], d3[which, :, cols]).astype(jnp.bfloat16)
            grad[block : block + 6, :, cols] = value.reshape(D // BLK, BLK, wide)

    def send_ingrad(s, hop):
        return sender.copy(
            80 + 3 * s + hop,
            att.at[0, pl.ds(s * rows + part * here.z_hops[hop], part)],
            ingrad.at[own * z + s],
            here.to_z[hop],
        )

    def own_ingrad(s):
        return local(att.at[0, pl.ds(s * rows + part * z, part)], ingrad.at[own * z + s], 11 + s)

    def input_gradient(s):
        at = pl.ds(s * rows, rows)
        value = mm_nt(d3[1, at, :], w[0:D, :])
        value += mm_nt(d3[2, at, :], w[D : 2 * D, :])
        value += mm_nt(d3[0, at, :], w[2 * D :, :])
        att[0, at, :] = value.astype(jnp.bfloat16)
        for hop in range(3):
            send_ingrad(s, hop).start()
        own_ingrad(s).start()

    def second_half():
        for copy in swaps[1]:
            copy.wait_recv()

    group = PAIRS // 2

    def pair_step(i, _):
        s = (i // group) % own
        p = (i // (own * group)) * group + i % group
        bias = jnp.where(key < lengths_ref[own * z + s], 0.0, MASKED)
        at = pl.ds(pl.multiple_of(s * rows, rows), rows)
        cols, d_query, d_key, d_value = back_pair(*(att.at[k, at] for k in range(5)), lse_ref, s, p, bias)
        d3[1, at, cols] = d_query
        d3[2, at, cols] = d_key
        d3[0, at, cols] = d_value

        stages = {
            0: (early.pass_plane,),
            2: (middle.start_far,),
            4: (early.start_z, middle.start_near),
            5: (lambda: head_grads(0), second_half),
            6: (early.far_z, middle.pass_plane),
            8: (lambda: input_gradient(0),),
            9: (middle.sent_core, late[0].start_core, middle.start_z, late[0].start_far),
            10: (late[0].start_near,),
            11: (late[0].pass_plane,),
        }
        for at_step, calls in stages.items():

            @pl.when(i == at_step)
            def _():
                for call in calls:
                    call()

        return 0

    lax.fori_loop(0, own * PAIRS, pair_step, 0)

    head_grads(1)
    late[1].start_core()
    vec_src[0] = vec_in[...]
    vec_src[0, 0:1, :] = jnp.sum(d3[1].astype(jnp.float32), axis=0, keepdims=True)
    vec_src[0, 1:2, :] = jnp.sum(d3[0].astype(jnp.float32), axis=0, keepdims=True)
    for i in range(squares_in.shape[0]):
        sums = jnp.sum(squares_in[i], axis=-1, keepdims=True)
        rms_src[0, 8 * i : 8 * i + 8, :] = jnp.broadcast_to(sums, (8, LANES))
    ways = (here.to_z[0], here.to_z[1], here.to_core, here.to_x, here.to_y)
    vec_copies = [sender.copy(12 + w, vec_src.at[w], vec_land.at[w], way) for w, way in enumerate(ways)]
    rms_copies = [sender.copy(17 + w, rms_src.at[w], rms_land.at[w], ways[w]) for w in range(2)]

    def vec_step(w):
        if w > 0:
            vec_copies[w - 1].wait_recv()
            after = vec_src[w - 1] + vec_land[w - 1]
            if w < len(ways):
                vec_src[w] = after
            else:
                vec_out[...] = after
        if w < len(ways):
            vec_copies[w].start()
        if 0 < w <= 2:
            rms_copies[w - 1].wait_recv()
            after = rms_src[w - 1] + rms_land[w - 1]
            if w < 2:
                rms_src[w] = after
            else:
                lane = lax.broadcasted_iota(jnp.int32, (1, LANES), 1)
                tiles = squares_in.shape[0]
                each = dctx_in.shape[0] // tiles
                for n in range(dctx_in.shape[0]):
                    row = 8 * (n // each) + 2 * (n % each)
                    sums = jnp.where(lane == 0, after[row : row + 1], after[row + 1 : row + 2])
                    rms_out[n : n + 1, :] = jnp.sqrt(sums / (lengths_ref[n].astype(jnp.float32) * D))
        if w < 2:
            rms_copies[w].start()

    vec_step(0)
    late[1].start_far()
    early.back_z()
    middle.far_z()
    vec_step(1)
    late[0].start_z()
    late[1].start_near()
    late[1].pass_plane()
    vec_step(2)
    late[1].start_z()
    early.share(load_sem.at[13])
    vec_step(3)
    late[0].far_z()
    middle.back_z()
    vec_step(4)
    late[1].far_z()
    input_gradient(1)
    vec_step(5)
    late[0].back_z()
    late[1].back_z()
    late[0].share(load_sem.at[15])
    middle.share(load_sem.at[14])
    late[1].share(load_sem.at[16])
    for phase in late:
        phase.sent_core()
    for i, phase in enumerate((early, middle, late[0], late[1])):
        phase.finish(load_sem.at[13 + i])
    for copy in swaps[1] + vec_copies + rms_copies:
        copy.wait_send()
    for s in range(own):
        own_ingrad(s).wait()
        for hop in range(3):
            send_ingrad(s, hop).wait_recv()
            send_ingrad(s, hop).wait_send()


def tail(plan, blk, lengths, vec, squares, lse, d_ctx, ctx_split, d_branch, d_inner, mid, act, d_feed, tokens, q, k, v, ctx, w):
    total = tokens.shape[0]
    any_spec = pl.BlockSpec(memory_space=pl.ANY)
    vmem = pl.BlockSpec(memory_space=pltpu.VMEM)
    smem = pl.BlockSpec(memory_space=pltpu.SMEM)
    low = jnp.bfloat16
    sums = (8 * squares.shape[0], LANES)

    def phase(n, width):
        half = n * BLK // 2
        return [
            pltpu.VMEM((4 * n * BLK, width), low),
            pltpu.VMEM((2, half, width), low),
            pltpu.VMEM((2, half, width), low),
            pltpu.VMEM((2, half, width), low),
            pltpu.VMEM((half, width), low),
            pltpu.VMEM((half, width), low),
            pltpu.VMEM((n * BLK, width), low),
        ]

    return pl.pallas_call(
        partial(tail_kernel, plan=plan),
        in_specs=[smem] * 2 + [vmem] * 3 + [any_spec] * 13,
        out_specs=[any_spec] * 2 + [vmem] * 2,
        out_shape=[
            jax.ShapeDtypeStruct((LOOSE.listed * BLK, D), low),
            jax.ShapeDtypeStruct(d_ctx.shape, low),
            jax.ShapeDtypeStruct(vec.shape, jnp.float32),
            jax.ShapeDtypeStruct((d_ctx.shape[0], LANES), jnp.float32),
        ],
        scratch_shapes=[
            pltpu.VMEM((HEAD_BLOCKS + (D + 2 * FF) // BLK, BLK, D), low),
            pltpu.VMEM((2 * max(plan.early, plan.middle, plan.late) * BLK, D), low),
            pltpu.VMEM((3, total, D), low),
            pltpu.VMEM((5, total, D), low),
            pltpu.VMEM((total, D), low),
            pltpu.VMEM((3 * D, D), low),
        ]
        + phase(plan.early // 2, D)
        + phase(plan.middle // 2, D)
        + phase(plan.late // 2, D // 2)
        + phase(plan.late // 2, D // 2)
        + [
            pltpu.VMEM((5,) + vec.shape, jnp.float32),
            pltpu.VMEM((5,) + vec.shape, jnp.float32),
            pltpu.VMEM((2,) + sums, jnp.float32),
            pltpu.VMEM((2,) + sums, jnp.float32),
            pltpu.SemaphoreType.DMA((86,)),
            pltpu.SemaphoreType.DMA((86,)),
            pltpu.SemaphoreType.DMA((17,)),
        ],
        compiler_params=pltpu.CompilerParams(
            vmem_limit_bytes=63 * MIB, collective_id=plan.ids[0], has_side_effects=True
        ),
        cost_estimate=pl.CostEstimate(
            flops=2 * total * D * (6 * D + 2 * FF) + 10 * total * SEQLEN * D,
            bytes_accessed=total * (24 * D + 4 * FF) + 8 * FF * D,
            transcendentals=total * SEQLEN * H,
        ),
        name="tail",
    )(blk, lengths, vec, squares, lse, d_ctx, ctx_split, d_branch, d_inner, mid, act, d_feed, tokens, q, k, v, ctx, w)


def tables_kernel(owner_ref, place_ref, mine_ref, block_ref, spot_ref, has_ref, fits_ref, *, slots, plan):
    dp = lax.axis_index("dp")
    chip_slots = 2 * slots
    near_blocks = HEAD_BLOCKS + (D + FF) // BLK
    for ref in (mine_ref, block_ref, spot_ref, has_ref):
        for i in range(ref.shape[0]):
            ref[i] = 0

    def body(b, counts):
        listed, early, middle, late, bad = counts
        slot = owner_ref[b]
        chip = slot // chip_slots
        shift = 8 * chip
        one = jnp.left_shift(1, shift)

        def count(packed):
            return jnp.right_shift(packed, shift) & 255

        order = count(listed)
        n_early, n_middle, n_late = count(early), count(middle), count(late)
        body_block = b >= HEAD_BLOCKS
        in_early = body_block & (b < near_blocks) & (n_early < plan.early)
        in_middle = body_block & jnp.logical_not(in_early) & (n_middle < plan.middle)
        in_late = jnp.logical_not(in_early | in_middle)
        spot = jnp.where(in_early, n_early, jnp.where(in_middle, plan.early + n_middle, plan.early + plan.middle + n_late))
        wrong = (order >= plan.listed) | (spot >= plan.listed) | (jnp.logical_not(body_block) & (order >= plan.first))
        spot = jnp.minimum(spot, plan.listed - 1)
        place_ref[b] = chip * plan.listed + jnp.minimum(order, plan.listed - 1)
        block_ref[chip * plan.listed + spot] = b

        @pl.when(chip == dp // 2)
        def _():
            mine_ref[jnp.minimum(order, plan.listed - 1)] = slot - chip * chip_slots

            @pl.when(slot // slots == dp)
            def _():
                spot_ref[slot % slots] = spot
                has_ref[slot % slots] = 1

        return (
            listed + one,
            early + jnp.where(in_early, one, 0),
            middle + jnp.where(in_middle, one, 0),
            late + jnp.where(in_late, one, 0),
            bad | wrong.astype(jnp.int32),
        )

    zero = jnp.int32(0)
    counts = lax.fori_loop(0, owner_ref.shape[0], body, (zero,) * 5, unroll=4)
    fits_ref[0] = 1 - counts[4]


def tables(plan, owner, slots):
    chips = lax.axis_size("dp") // 2
    smem = pl.BlockSpec(memory_space=pltpu.SMEM)
    sizes = (owner.shape[0], plan.listed, chips * plan.listed, slots, slots, 1)
    return pl.pallas_call(
        partial(tables_kernel, slots=slots, plan=plan),
        in_specs=[smem],
        out_specs=[smem] * len(sizes),
        out_shape=[jax.ShapeDtypeStruct((n,), jnp.int32) for n in sizes],
        name="tables",
    )(owner)


def general(tokens, cotangent, lengths, owner, master, vec_master):
    slot_local = master.shape[0]
    gathered = lax.all_gather(master.astype(jnp.bfloat16), "dp", axis=0, tiled=True)
    seq_place = lax.axis_index("seq")
    slot_total = slot_local * lax.axis_size("dp")
    tokens = to_whole(tokens, "seq")
    cotangent = to_whole(cotangent, "seq")
    seq_count, seq_len, width = tokens.shape
    token_count = seq_count * seq_len
    lengths = lax.dynamic_slice_in_dim(lengths, seq_place * seq_count, seq_count)
    q, k, v, ctx, lse, _ = attend(owner, lengths, tokens, gathered, vec_master)
    flat = tokens.reshape(token_count, D)
    _, mid, out, act, d_inner, d_feed, d_branch, d_ctx, vec_feed, squares = feed_both(
        owner, lengths, seq_len,
        flat, ctx, cotangent.reshape(token_count, D), gathered, vec_master,
    )
    held = feed_grads(owner, slot_total, ctx, d_branch, d_inner, mid, act, d_feed)
    ingrad, vec_attend, held = attend_back(
        owner, owner, lengths, tokens, q, k, v, ctx, d_ctx, lse, d_branch, gathered, held
    )
    local_sums = jnp.sum(squares.reshape(seq_count, -1, 8, D)[:, :, :2], axis=(1, 3))
    own_rms = jnp.sqrt(local_sums / (lengths[:, None].astype(jnp.float32) * D))
    sublayer_rms = lax.all_gather(own_rms, "seq", axis=0, tiled=True)
    vec_local = jnp.concatenate([vec_attend[:2], vec_feed[2:12]], axis=0)
    vec_grad = lax.psum(vec_local, ("dp", "seq"))
    owned = lax.psum_scatter(held, "dp", scatter_dimension=0, tiled=True)
    reduced = lax.psum(owned, "seq")
    first_slot = lax.axis_index("dp") * slot_local
    slots = jnp.arange(slot_local, dtype=jnp.int32)
    has = jnp.any((first_slot + slots)[:, None] == owner[None, :], axis=1).astype(jnp.int32)
    whole = (seq_count, seq_len, D)
    return (
        to_split(out.reshape(whole), "seq"),
        jnp.zeros((token_count, D), jnp.bfloat16),
        to_split(ingrad.reshape(whole), "seq").reshape(token_count, D),
        to_split(mid.reshape(whole), "seq").astype(jnp.float32),
        jnp.pad(sublayer_rms, ((0, 0), (0, LANES - 2))),
        jnp.pad(vec_grad, ((0, 4), (0, 0))),
        reduced,
        slots,
        has,
    )


def listed(plan, tokens, cotangent, lengths, owner, master, vec_master, place, mine, block, spot, has):
    seqs, part, _ = tokens.shape
    total = seqs * part
    pool, q, k, v, ctx, w, whole, ctx_split, lse = front(
        plan, place, mine, lengths, vec_master, master, tokens
    )
    ctx_split = ctx_split.reshape(total, D)
    wide_mid, mid, out, act, d_inner, d_feed, d_branch, d_ctx, vec_feed, squares = feed_both(
        place, lengths, part,
        tokens.reshape(total, D), ctx_split, cotangent.reshape(total, D), pool.reshape(-1, BLK, D), vec_master,
    )
    reduced, ingrad, vec_grad, rms = tail(
        plan, block, lengths, vec_feed, squares, lse, d_ctx.reshape(seqs, part, D), ctx_split, d_branch, d_inner,
        mid, act, d_feed, whole, q, k, v, ctx, w,
    )
    return (
        out.reshape(tokens.shape),
        d_branch,
        ingrad.reshape(total, D),
        wide_mid.reshape(tokens.shape),
        rms,
        vec_grad,
        reduced.reshape(-1, BLK, D),
        spot,
        has,
    )


def per_device(
    tokens, cotangent, lengths, owner, master, moment, second, vec_master, vec_moment, vec_second
):
    slot_local = master.shape[0]
    given = (tokens, cotangent, lengths, owner, master, vec_master)
    if lax.axis_size("dp") == 8 and lax.axis_size("seq") == 4:

        def spread(*args):
            results = general(*args)
            pad = ((0, LOOSE.listed - slot_local), (0, 0), (0, 0))
            return results[:6] + (jnp.pad(results[6], pad),) + results[7:]

        def attempt(plan, otherwise, *args):
            place, mine, block, spot, has, fits = tables(plan, args[3], slot_local)

            def fitting(*every):
                return listed(plan, *every)

            def other(*every):
                return otherwise(*every[:6])

            return lax.cond(fits[0] > 0, fitting, other, *args, place, mine, block, spot, has)

        results = attempt(TIGHT, partial(attempt, LOOSE, spread), *given)
    else:
        results = general(*given)
    layer_out, d_res, ingrad, residual_mid, rms, vec_grad, reduced, spot, has = results
    updated = adam_all(
        spot, has, reduced, moment, second, master,
        d_res, ingrad, rms, vec_grad, vec_moment, vec_second, vec_master,
    )
    input_grad, sublayer_rms, slots, vectors = updated[0], updated[1], updated[2:6], updated[6:]
    return (layer_out, input_grad.reshape(tokens.shape), residual_mid, sublayer_rms, *slots, *vectors)


def solution(mesh):
    return jax.shard_map(
        per_device,
        mesh=mesh,
        in_specs=(
            P("dp", "seq", None),
            P("dp", "seq", None),
            P("dp"),
            P(),
            P("dp", None, None),
            P("dp", None, None),
            P("dp", None, None),
            P(),
            P(),
            P(),
        ),
        out_specs=(
            P("dp", "seq", None),
            P("dp", "seq", None),
            P("dp", "seq", None),
            P("dp", None),
            P("dp", None, None),
            P("dp", None, None),
            P("dp", None, None),
            P("dp", None, None),
            P(),
            P(),
            P(),
            P(),
        ),
        check_vma=False,
    )
```

```python
from functools import partial

import jax
import jax.numpy as jnp
from jax import lax
from jax.experimental import pallas as pl
from jax.experimental.pallas import tpu as pltpu
from jax.sharding import PartitionSpec as P

D = 768
H = 12
DH = 64
FF = 3072
BLK = 128
SEQLEN = 512
STEP = 5


first_decay = 0.5
second_decay = 0.5
matrix_rate = 0.02
vector_rate = 0.2
weight_decay = 0.01
adam_epsilon = 1e-08


def adam_step(gradient, moment, second, weight, rate):
    moment_new = first_decay * moment + (1.0 - first_decay) * gradient
    second_new = second_decay * second + (1.0 - second_decay) * gradient * gradient
    moment_hat = moment_new * (1.0 / (1.0 - first_decay**STEP))
    second_hat = second_new * (1.0 / (1.0 - second_decay**STEP))
    root = second_hat * lax.rsqrt(second_hat) + adam_epsilon
    inverse = pltpu.reciprocal(root, approx=True)
    inverse = inverse * (2.0 - root * inverse)
    weight_new = weight - rate * (moment_hat * inverse + weight_decay * weight)
    return (moment_new, second_new, weight_new)


def seq_swap(parts, axis):
    size = lax.axis_size(axis)
    me = lax.axis_index(axis)
    stacked = parts
    got = [None] * size
    mine = lax.dynamic_index_in_dim(stacked, me, 0, keepdims=False)
    out = [mine]
    for hop in range(1, size):
        there = jnp.bitwise_xor(me, hop)
        piece = lax.dynamic_index_in_dim(stacked, there, 0, keepdims=False)
        route = [(i, i ^ hop) for i in range(size)]
        out.append(lax.ppermute(piece, axis, route))
    return out


def from_hops(pieces, axis):
    size = lax.axis_size(axis)
    me = lax.axis_index(axis)
    stacked = jnp.stack(pieces, axis=0)
    order = jnp.bitwise_xor(jnp.arange(size, dtype=jnp.int32), me)
    return jnp.take(stacked, order, axis=0)


def to_whole(block, axis):
    size = lax.axis_size(axis)
    count, length, width = block.shape
    pieces = seq_swap(block.reshape(size, count // size, length, width), axis)
    stacked = from_hops(pieces, axis)
    return jnp.swapaxes(stacked, 0, 1).reshape(count // size, size * length, width)


def to_split(whole, axis):
    size = lax.axis_size(axis)
    own, full, width = whole.shape
    parts = jnp.swapaxes(whole.reshape(own, size, full // size, width), 0, 1)
    pieces = seq_swap(parts, axis)
    return from_hops(pieces, axis).reshape(size * own, full // size, width)


LANES = 128
PAIRS = D // LANES
CHUNKS = FF // D
MASKED = -1e30
NT = (((1,), (1,)), ((), ()))
TN = (((0,), (0,)), ((), ()))
MIB = 1 << 20


def mm(left, right):
    return jnp.dot(left, right, preferred_element_type=jnp.float32)


def mm_nt(left, right):
    return lax.dot_general(left, right, NT, preferred_element_type=jnp.float32)


def mm_tn(left, right):
    return lax.dot_general(left, right, TN, preferred_element_type=jnp.float32)


def load_blocks(pool_ref, place_ref, first, into_ref, sem):
    def start(i, _):
        pltpu.make_async_copy(
            pool_ref.at[place_ref[first + i]], into_ref.at[pl.ds(i * BLK, BLK)], sem
        ).start()
        return 0

    lax.fori_loop(0, into_ref.shape[0] // BLK, start, 0)


def wait_whole(ref, sem):
    pltpu.make_async_copy(ref, ref, sem).wait()


def spare_lanes(rows, half, bias_column):
    lane = lax.broadcasted_iota(jnp.int32, (rows, LANES), 1)
    first = DH * (1 - half)
    spare = jnp.where(lane == first, bias_column, jnp.where(lane < first + 4, 1.0, 0.0))
    inside = (lane >= DH * half) & (lane < DH * half + DH)
    return inside, spare.astype(jnp.bfloat16)


def split3(row):
    one = row.astype(jnp.bfloat16)
    rest = row - one.astype(jnp.float32)
    two = rest.astype(jnp.bfloat16)
    three = (rest - two.astype(jnp.float32)).astype(jnp.bfloat16)
    return one, two, three


def beside(head_rows, extra, half):
    columns = head_rows.shape[1]
    pad = jnp.zeros((DH - extra.shape[0], columns), jnp.bfloat16)
    parts = [extra.astype(jnp.bfloat16), pad]
    order = [head_rows] + parts if half == 0 else parts + [head_rows]
    return jnp.concatenate(order, axis=0)


def forward_pair(q_ref, k_ref, v_ref, ctx_ref, lse_ref, seq, p, bias):
    rows = q_ref.shape[0]
    cols = pl.ds(pl.multiple_of(p * LANES, LANES), LANES)
    row8 = lax.broadcasted_iota(jnp.int32, (16, rows), 0)
    q2t = q_ref[:, cols].T
    k2 = k_ref[:, cols]
    v2t = v_ref[:, cols].T
    outs = []
    for half in range(2):
        inside, spare = spare_lanes(rows, half, bias)
        k_aug = jnp.where(inside, k2, spare)
        head = slice(half * DH, half * DH + DH)
        q_aug = beside(q2t[head], jnp.where(row8 == 0, 1.0, 0.0), half)
        scores = mm(k_aug, q_aug)
        top = jnp.max(scores, axis=0, keepdims=True)
        expos = jnp.exp(scores - top).astype(jnp.bfloat16)
        v_aug = jnp.concatenate([v2t[head], jnp.ones((16, rows), jnp.bfloat16)], axis=0)
        both = mm(v_aug, expos)
        total = both[DH : DH + 1]
        outs.append(both[0:DH] / total)
        lse_ref[seq, pl.ds(2 * p + half, 1), :] = top + jnp.log(total)
    ctx_ref[:, cols] = jnp.concatenate(outs, axis=0).T.astype(jnp.bfloat16)


def attend_kernel(
    place_ref, lengths_ref, tokens_ref, pool_ref, vec_ref,
    q_ref, k_ref, v_ref, ctx_ref, lse_ref, w_scr,
    sem,
):
    seq = pl.program_id(0)
    rows = tokens_ref.shape[0]

    @pl.when(seq == 0)
    def _():
        load_blocks(pool_ref, place_ref, 0, w_scr, sem)
        wait_whole(w_scr, sem)

    tokens = tokens_ref[...]
    q_ref[...] = ((mm(tokens, w_scr[0:D, :]) + vec_ref[0:1, :]).astype(jnp.bfloat16) * 0.125).astype(jnp.bfloat16)
    k_ref[...] = mm(tokens, w_scr[D : 2 * D, :]).astype(jnp.bfloat16)
    v_ref[...] = (mm(tokens, w_scr[2 * D :, :]) + vec_ref[1:2, :]).astype(jnp.bfloat16)
    key = lax.broadcasted_iota(jnp.int32, (rows, 1), 0)
    bias = jnp.where(key < lengths_ref[seq], 0.0, MASKED)

    def pair(p, _):
        forward_pair(q_ref, k_ref, v_ref, ctx_ref, lse_ref, 0, p, bias)
        return 0

    lax.fori_loop(0, PAIRS, pair, 0)


def attend(place, lengths, tokens, pool, vec):
    seqs, rows, _ = tokens.shape
    flat = tokens.reshape(seqs * rows, D)
    row_spec = pl.BlockSpec((rows, D), lambda s, *_: (s, 0))
    any_spec = pl.BlockSpec(memory_space=pl.ANY)
    low = jax.ShapeDtypeStruct((seqs * rows, D), jnp.bfloat16)
    return pl.pallas_call(
        attend_kernel,
        grid_spec=pltpu.PrefetchScalarGridSpec(
            num_scalar_prefetch=2,
            grid=(seqs,),
            in_specs=[row_spec, any_spec, pl.BlockSpec(vec.shape, lambda s, *_: (0, 0))],
            out_specs=[row_spec] * 4
            + [
                pl.BlockSpec((1, 16, rows), lambda s, *_: (s, 0, 0)),
                pl.BlockSpec((3 * D, D), lambda s, *_: (0, 0)),
            ],
            scratch_shapes=[pltpu.SemaphoreType.DMA],
        ),
        out_shape=[low] * 4
        + [
            jax.ShapeDtypeStruct((seqs, 16, rows), jnp.float32),
            jax.ShapeDtypeStruct((3 * D, D), jnp.bfloat16),
        ],
        compiler_params=pltpu.CompilerParams(vmem_limit_bytes=48 * MIB),
        cost_estimate=pl.CostEstimate(
            flops=6 * seqs * rows * D * D + 4 * seqs * rows * rows * D,
            bytes_accessed=10 * seqs * rows * D + 6 * D * D,
            transcendentals=seqs * rows * rows * H,
        ),
        name="attend",
    )(place, lengths, flat, pool, vec)


def gelu_parts(x):
    t_in = 1.0 + (0.3275911 * 0.7071067811865476) * jnp.abs(x)
    t = pltpu.reciprocal(t_in, approx=True)
    t = t * (2.0 - t_in * t)
    e = jnp.exp2((-0.5 * 1.4426950408889634) * (x * x))
    poly = (0.5 * 1.061405429) * t - (0.5 * 1.453152027)
    poly = poly * t + (0.5 * 1.421413741)
    poly = poly * t - (0.5 * 0.284496736)
    poly = poly * t + (0.5 * 0.254829592)
    tail = (poly * t) * e
    dist = jnp.where(x >= 0, 1.0 - tail, tail)
    return dist, x * (e * 0.3989422804014327)


def norm_stats(resid):
    center = resid - jnp.mean(resid, axis=-1, keepdims=True)
    scale = lax.rsqrt(jnp.mean(center * center, axis=-1, keepdims=True) + 1e-05)
    return center * scale, scale


def norm_back(d_out, gain, hat, scale):
    d_hat = d_out * gain
    mean_one = jnp.mean(d_hat, axis=-1, keepdims=True)
    mean_hat = jnp.mean(d_hat * hat, axis=-1, keepdims=True)
    return scale * (d_hat - mean_one - hat * mean_hat)


def feed_kernel(
    place_ref, lengths_ref, tokens_ref, ctx_ref, cot_ref, pool_ref, vec_ref,
    wide_mid_ref, mid_ref, out_ref, act_ref, dinner_ref, dfeed_ref, dbranch_ref, dctx_ref, grad_ref, sq_ref,
    w_out, w_up, w_down, slope_scr, sem, *, seq_rows,
):
    step = pl.program_id(0)
    rows = tokens_ref.shape[0]
    tiles = sq_ref.shape[0]
    first = 3 * D // BLK

    @pl.when(step == 0)
    def _():
        load_blocks(pool_ref, place_ref, first, w_out, sem.at[0])
        load_blocks(pool_ref, place_ref, first + D // BLK, w_up, sem.at[1])
        load_blocks(pool_ref, place_ref, first + (D + FF) // BLK, w_down, sem.at[2])
        wait_whole(w_out, sem.at[0])
        grad_ref[...] = jnp.zeros_like(grad_ref)

    def add_row(row, value):
        grad_ref[row : row + 1, :] += jnp.sum(value, axis=0, keepdims=True)

    segment = min(rows, seq_rows)
    row = lax.broadcasted_iota(jnp.int32, (rows, 1), 0)
    length = jnp.zeros((rows, 1), jnp.int32)
    for j in range(rows // segment):
        length = jnp.where(row // segment == j, lengths_ref[(step * rows + j * segment) // seq_rows], length)
    place_in = (step * rows + row) % seq_rows
    if seq_rows < SEQLEN:
        place_in += lax.axis_index("seq") * seq_rows
    valid = (place_in < length).astype(jnp.float32)

    def square_sums(which, value):
        square = value * value * valid
        for j in range(rows // segment):
            sq_ref[0, 2 * j + which : 2 * j + which + 1, :] = jnp.sum(
                square[j * segment : (j + 1) * segment], axis=0, keepdims=True
            )

    branch = mm(ctx_ref[...], w_out[...]) + vec_ref[2:3, :]
    square_sums(0, branch)
    hat1, scale1 = norm_stats(tokens_ref[...].astype(jnp.float32) + branch)
    middle = hat1 * vec_ref[4:5, :] + vec_ref[5:6, :]
    wide_mid_ref[...] = middle
    mid_ref[...] = middle.astype(jnp.bfloat16)
    mid_low = mid_ref[...]

    @pl.when(step == 0)
    def _():
        wait_whole(w_up, sem.at[1])

    parts = [slice(c * D, (c + 1) * D) for c in range(CHUNKS)]

    @pl.when(step == 0)
    def _():
        wait_whole(w_down, sem.at[2])

    feed = jnp.zeros((rows, D), jnp.float32) + vec_ref[3:4, :]
    for c in range(CHUNKS):
        inner = mm_nt(mid_low, w_up[parts[c], :]) + vec_ref[8 + c : 9 + c, :]
        dist, bell = gelu_parts(inner)
        act = (inner * dist).astype(jnp.bfloat16)
        act_ref[:, parts[c]] = act
        slope_scr[:, parts[c]] = dist + bell
        feed += mm(act, w_down[parts[c], :])
    square_sums(1, feed)
    hat2, scale2 = norm_stats(middle + feed)
    gain2 = vec_ref[6:7, :]
    out_ref[...] = (hat2 * gain2 + vec_ref[7:8, :]).astype(jnp.bfloat16)
    upstream = cot_ref[...].astype(jnp.float32) * valid
    add_row(6, upstream * hat2)
    add_row(7, upstream)
    d_res2 = norm_back(upstream, gain2, hat2, scale2)
    d_feed = d_res2.astype(jnp.bfloat16)
    dfeed_ref[...] = d_feed
    add_row(3, d_feed.astype(jnp.float32))
    d_mid = d_res2
    for c in range(CHUNKS):
        d_inner = (mm_nt(d_feed, w_down[parts[c], :]) * slope_scr[:, parts[c]]).astype(jnp.bfloat16)
        dinner_ref[:, parts[c]] = d_inner
        add_row(8 + c, d_inner.astype(jnp.float32))
        d_mid += mm(d_inner, w_up[parts[c], :])
    add_row(4, d_mid * hat1)
    add_row(5, d_mid)
    d_res1 = norm_back(d_mid, vec_ref[4:5, :], hat1, scale1)
    d_branch = d_res1.astype(jnp.bfloat16)
    dbranch_ref[...] = d_branch
    add_row(2, d_branch.astype(jnp.float32))
    dctx_ref[...] = mm_nt(d_branch, w_out[...]).astype(jnp.bfloat16)


def feed_both(place, lengths, seq_rows, tokens, ctx, cot, pool, vec, tile=256):
    total = tokens.shape[0]
    steps = total // tile
    row_spec = pl.BlockSpec((tile, D), lambda s, *_: (s, 0))
    wide_spec = pl.BlockSpec((tile, FF), lambda s, *_: (s, 0))
    any_spec = pl.BlockSpec(memory_space=pl.ANY)
    low = jax.ShapeDtypeStruct((total, D), jnp.bfloat16)
    wide = jax.ShapeDtypeStruct((total, FF), jnp.bfloat16)
    return pl.pallas_call(
        partial(feed_kernel, seq_rows=seq_rows),
        grid_spec=pltpu.PrefetchScalarGridSpec(
            num_scalar_prefetch=2,
            grid=(steps,),
            in_specs=[row_spec] * 3 + [any_spec, pl.BlockSpec(vec.shape, lambda s, *_: (0, 0))],
            out_specs=[row_spec, row_spec, row_spec, wide_spec, wide_spec, row_spec, row_spec, row_spec,
                pl.BlockSpec((16, D), lambda s, *_: (0, 0)),
                pl.BlockSpec((1, 8, D), lambda s, *_: (s, 0, 0))],
            scratch_shapes=[
                pltpu.VMEM((D, D), jnp.bfloat16),
                pltpu.VMEM((FF, D), jnp.bfloat16),
                pltpu.VMEM((FF, D), jnp.bfloat16),
                pltpu.VMEM((tile, FF), jnp.float32),
                pltpu.SemaphoreType.DMA((3,)),
            ],
        ),
        out_shape=[jax.ShapeDtypeStruct((total, D), jnp.float32), low, low, wide, wide, low, low, low,
            jax.ShapeDtypeStruct((16, D), jnp.float32),
            jax.ShapeDtypeStruct((steps, 8, D), jnp.float32)],
        compiler_params=pltpu.CompilerParams(vmem_limit_bytes=62 * MIB),
        cost_estimate=pl.CostEstimate(
            flops=8 * total * D * FF + 4 * total * D * D,
            bytes_accessed=total * (16 * D + 4 * FF) + 12 * FF * D,
            transcendentals=total * FF,
        ),
        name="feed_both",
    )(place, lengths, tokens, ctx, cot, pool, vec)


def send_blocks(value, held, slot, first, place_ref, out_ref, sem):
    held[slot] = value.astype(jnp.bfloat16).reshape(D // BLK, BLK, D)
    for i in range(D // BLK):
        pltpu.make_async_copy(
            held.at[slot, i], out_ref.at[place_ref[first + i]], sem.at[slot]
        ).start()


def feed_grads_kernel(
    place_ref, ctx_ref, dbranch_ref, dinner_ref, mid_ref, act_ref, dfeed_ref, out_ref, held, sem
):
    step = pl.program_id(0)
    slot = lax.rem(step, 2)
    base = 3 * D // BLK

    @pl.when(step >= 2)
    def _():
        wait_whole(held.at[slot], sem.at[slot])

    first = base + step * (D // BLK)

    @pl.when(step == 0)
    def _():
        send_blocks(mm_tn(ctx_ref[...], dbranch_ref[...]), held, slot, first, place_ref, out_ref, sem)

    @pl.when((step >= 1) & (step <= CHUNKS))
    def _():
        send_blocks(mm_tn(dinner_ref[...], mid_ref[...]), held, slot, first, place_ref, out_ref, sem)

    @pl.when(step > CHUNKS)
    def _():
        send_blocks(mm_tn(act_ref[...], dfeed_ref[...]), held, slot, first, place_ref, out_ref, sem)

    @pl.when(step == 2 * CHUNKS)
    def _():
        wait_whole(held.at[slot], sem.at[slot])
        wait_whole(held.at[1 - slot], sem.at[1 - slot])


def feed_grads(place, places, ctx, d_branch, d_inner, mid, act, d_feed):
    total = ctx.shape[0]
    whole = pl.BlockSpec((total, D), lambda s, *_: (0, 0))
    return pl.pallas_call(
        feed_grads_kernel,
        grid_spec=pltpu.PrefetchScalarGridSpec(
            num_scalar_prefetch=1,
            grid=(1 + 2 * CHUNKS,),
            in_specs=[
                whole,
                whole,
                pl.BlockSpec((total, D), lambda s, *_: (0, jnp.clip(s - 1, 0, CHUNKS - 1))),
                whole,
                pl.BlockSpec((total, D), lambda s, *_: (0, jnp.clip(s - 1 - CHUNKS, 0, CHUNKS - 1))),
                whole,
            ],
            out_specs=pl.BlockSpec(memory_space=pl.ANY),
            scratch_shapes=[
                pltpu.VMEM((2, D // BLK, BLK, D), jnp.bfloat16),
                pltpu.SemaphoreType.DMA((2,)),
            ],
        ),
        out_shape=jax.ShapeDtypeStruct((places, BLK, D), jnp.bfloat16),
        compiler_params=pltpu.CompilerParams(vmem_limit_bytes=48 * MIB),
        cost_estimate=pl.CostEstimate(
            flops=4 * total * D * FF + 2 * total * D * D,
            bytes_accessed=total * (8 * D + 4 * FF) + 4 * FF * D,
            transcendentals=0,
        ),
        name="feed_grads",
    )(place, ctx, d_branch, d_inner, mid, act, d_feed)


def attend_back_kernel(
    place_w_ref, place_ref, lengths_ref, tokens_ref, q_ref, k_ref, v_ref, ctx_ref, dctx_ref, lse_ref, dres_ref, pool_ref, held_in,
    ingrad_ref, vec_ref, out_ref,
    w_scr, dq_scr, dk_scr, dv_scr, total_scr, held, sem, w_sem,
):
    seq = pl.program_id(0)
    last = pl.num_programs(0) - 1
    rows = tokens_ref.shape[0]

    @pl.when(seq == 0)
    def _():
        load_blocks(pool_ref, place_w_ref, 0, w_scr, w_sem)
        vec_ref[...] = jnp.zeros_like(vec_ref)

    key = lax.broadcasted_iota(jnp.int32, (rows, 1), 0)
    bias = jnp.where(key < lengths_ref[seq], 0.0, MASKED)

    def pair(p, _):
        cols, d_query, d_key, d_value = back_pair(q_ref, k_ref, v_ref, ctx_ref, dctx_ref, lse_ref, 0, p, bias)
        dq_scr[:, cols] = d_query
        dk_scr[:, cols] = d_key
        dv_scr[:, cols] = d_value
        return 0

    lax.fori_loop(0, PAIRS, pair, 0)

    @pl.when(seq == 0)
    def _():
        wait_whole(w_scr, w_sem)

    dq, dk, dv = dq_scr[...], dk_scr[...], dv_scr[...]
    vec_ref[0:1, :] += jnp.sum(dq.astype(jnp.float32), axis=0, keepdims=True)
    vec_ref[1:2, :] += jnp.sum(dv.astype(jnp.float32), axis=0, keepdims=True)
    ingrad = dres_ref[...].astype(jnp.float32) + mm_nt(dq, w_scr[0:D, :])
    ingrad += mm_nt(dk, w_scr[D : 2 * D, :])
    ingrad += mm_nt(dv, w_scr[2 * D :, :])
    ingrad_ref[...] = ingrad.astype(jnp.bfloat16)
    tokens = tokens_ref[...]
    for i, right in enumerate((dq, dk, dv)):
        part = slice(i * D, (i + 1) * D)

        @pl.when(seq == 0)
        def _():
            total_scr[part, :] = mm_tn(tokens, right)

        @pl.when(seq > 0)
        def _():
            total_scr[part, :] += mm_tn(tokens, right)

    @pl.when(seq == last)
    def _():
        for i in range(3):
            send_blocks(total_scr[i * D : (i + 1) * D, :], held, i, i * (D // BLK), place_ref, out_ref, sem)
        for i in range(3):
            wait_whole(held.at[i], sem.at[i])


def attend_back(place_w, place, lengths, tokens, q, k, v, ctx, d_ctx, lse, d_res, pool, held):
    seqs, rows, _ = tokens.shape
    flat = tokens.reshape(seqs * rows, D)
    row_spec = pl.BlockSpec((rows, D), lambda s, *_: (s, 0))
    any_spec = pl.BlockSpec(memory_space=pl.ANY)
    return pl.pallas_call(
        attend_back_kernel,
        grid_spec=pltpu.PrefetchScalarGridSpec(
            num_scalar_prefetch=3,
            grid=(seqs,),
            in_specs=[row_spec] * 6
            + [pl.BlockSpec((1, 16, rows), lambda s, *_: (s, 0, 0)), row_spec, any_spec, any_spec],
            out_specs=[row_spec, pl.BlockSpec((8, D), lambda s, *_: (0, 0)), any_spec],
            scratch_shapes=[
                pltpu.VMEM((3 * D, D), jnp.bfloat16),
                pltpu.VMEM((rows, D), jnp.bfloat16),
                pltpu.VMEM((rows, D), jnp.bfloat16),
                pltpu.VMEM((rows, D), jnp.bfloat16),
                pltpu.VMEM((3 * D, D), jnp.float32),
                pltpu.VMEM((3, D // BLK, BLK, D), jnp.bfloat16),
                pltpu.SemaphoreType.DMA((3,)),
                pltpu.SemaphoreType.DMA,
            ],
        ),
        out_shape=[
            jax.ShapeDtypeStruct((seqs * rows, D), jnp.bfloat16),
            jax.ShapeDtypeStruct((8, D), jnp.float32),
            jax.ShapeDtypeStruct(held.shape, held.dtype),
        ],
        input_output_aliases={12: 2},
        compiler_params=pltpu.CompilerParams(vmem_limit_bytes=62 * MIB),
        cost_estimate=pl.CostEstimate(
            flops=12 * seqs * rows * D * D + 10 * seqs * rows * rows * D,
            bytes_accessed=20 * seqs * rows * D + 12 * D * D,
            transcendentals=seqs * rows * rows * H,
        ),
        name="attend_back",
    )(place_w, place, lengths, flat, q, k, v, ctx, d_ctx, lse, d_res, pool, held)


RING = 4


def adam_kernel(
    place_ref, has_ref, rms_ref, vec_ref, vec_moment_ref, vec_second_ref, vec_master_ref,
    reduced, moment, second, master, dres, part,
    rms_out, vec_out, vec_moment_out, vec_second_out, vec_master_out,
    ingrad_out, grad_out, moment_out, second_out, master_out,
    red_buf, wide_in, rows_in, wide_out, rows_out, in_sem, out_sem,
):
    slots = master.shape[0]
    piece = rows_in.shape[2]
    pieces = dres.shape[0] // piece

    def loads(s):
        r = s % RING
        wide = [
            pltpu.make_async_copy(ref.at[s], wide_in.at[k, r], in_sem.at[k, r])
            for k, ref in enumerate((moment, second, master))
        ]
        return wide + [pltpu.make_async_copy(reduced.at[place_ref[s]], red_buf.at[r], in_sem.at[3, r])]

    def stores(s):
        r = s % RING
        return [
            pltpu.make_async_copy(wide_out.at[k, r], ref.at[s], out_sem.at[k, r])
            for k, ref in enumerate((grad_out, moment_out, second_out, master_out))
        ]

    def row_loads(s):
        r = s % RING
        return [
            pltpu.make_async_copy(ref.at[pl.ds(s * piece, piece)], rows_in.at[k, r], in_sem.at[4 + k, r])
            for k, ref in enumerate((dres, part))
        ]

    def row_store(s):
        r = s % RING
        return pltpu.make_async_copy(rows_out.at[r], ingrad_out.at[pl.ds(s * piece, piece)], out_sem.at[4, r])

    def begin(s):
        for copy in loads(s):
            copy.start()

        @pl.when(s < pieces)
        def _():
            for copy in row_loads(s):
                copy.start()

    ahead = min(RING - 1, slots)
    for s in range(ahead):
        begin(s)
    rms_out[...] = rms_ref[:, 0:2]
    vec_gradient = vec_ref[0 : vec_out.shape[0], :]
    vec_out[...] = vec_gradient
    vec_moment_out[...], vec_second_out[...], vec_master_out[...] = adam_step(
        vec_gradient, vec_moment_ref[...], vec_second_ref[...], vec_master_ref[...], vector_rate
    )

    def step(s, _):
        r = s % RING

        @pl.when(s + ahead < slots)
        def _():
            begin(s + ahead)

        for copy in loads(s):
            copy.wait()

        @pl.when(s >= RING)
        def _():
            for copy in stores(s - RING):
                copy.wait()

        got = red_buf[r].astype(jnp.float32)
        gradient = jnp.where(has_ref[s] > 0, got, jnp.zeros_like(got))
        wide_out[0, r] = gradient
        wide_out[1, r], wide_out[2, r], wide_out[3, r] = adam_step(
            gradient, wide_in[0, r], wide_in[1, r], wide_in[2, r], matrix_rate
        )
        for copy in stores(s):
            copy.start()

        @pl.when(s < pieces)
        def _():
            for copy in row_loads(s):
                copy.wait()

            @pl.when(s >= RING)
            def _():
                row_store(s - RING).wait()

            rows_out[r] = rows_in[0, r].astype(jnp.float32) + rows_in[1, r].astype(jnp.float32)
            row_store(s).start()

        return 0

    lax.fori_loop(0, slots, step, 0)
    for s in range(max(slots - RING, 0), slots):
        for copy in stores(s):
            copy.wait()
    for s in range(max(pieces - RING, 0), pieces):
        row_store(s).wait()


def adam_all(place, has, reduced, moment, second, master, d_res, part, rms, vec, vec_moment, vec_second, vec_master):
    slots = master.shape[0]
    total = d_res.shape[0]
    pieces = 1
    while 2 * pieces <= min(slots, 8):
        pieces *= 2
    piece = total // pieces
    smem = pl.BlockSpec(memory_space=pltpu.SMEM)
    vmem = pl.BlockSpec(memory_space=pltpu.VMEM)
    any_spec = pl.BlockSpec(memory_space=pl.ANY)
    full = jax.ShapeDtypeStruct(master.shape, jnp.float32)
    vec_full = jax.ShapeDtypeStruct(vec_master.shape, jnp.float32)
    results = pl.pallas_call(
        adam_kernel,
        in_specs=[smem] * 2 + [vmem] * 5 + [any_spec] * 6,
        out_specs=[vmem] * 5 + [any_spec] * 5,
        out_shape=[jax.ShapeDtypeStruct((rms.shape[0], 2), jnp.float32)]
        + [vec_full] * 4
        + [jax.ShapeDtypeStruct(d_res.shape, jnp.float32)]
        + [full] * 4,
        scratch_shapes=[
            pltpu.VMEM((RING, BLK, D), jnp.bfloat16),
            pltpu.VMEM((3, RING, BLK, D), jnp.float32),
            pltpu.VMEM((2, RING, piece, D), jnp.bfloat16),
            pltpu.VMEM((4, RING, BLK, D), jnp.float32),
            pltpu.VMEM((RING, piece, D), jnp.float32),
            pltpu.SemaphoreType.DMA((6, RING)),
            pltpu.SemaphoreType.DMA((5, RING)),
        ],
        compiler_params=pltpu.CompilerParams(vmem_limit_bytes=60 * MIB),
        cost_estimate=pl.CostEstimate(
            flops=20 * slots * BLK * D, bytes_accessed=30 * slots * BLK * D, transcendentals=2 * slots * BLK * D
        ),
        name="adam_all",
    )(place, has, rms, vec, vec_moment, vec_second, vec_master, reduced, moment, second, master, d_res, part)
    return (results[5], results[0], *results[6:], *results[1:5])


class Plan:
    def __init__(self, early, middle, late, first, ids):
        self.early, self.middle, self.late, self.first, self.ids = early, middle, late, first, ids
        self.listed = early + middle + late


LOOSE = Plan(6, 8, 10, 10, (1, 2))
HEAD_BLOCKS = 3 * D // BLK
MESH = pl.DeviceIdType.MESH


class Place:
    def __init__(self):
        dp = lax.axis_index("dp")
        self.z = lax.axis_index("seq")
        self.core = dp % 2
        x = (dp // 2) % 2
        y = dp // 4
        self.chip = dp // 2
        self.chip_x = 2 * y + 1 - x
        self.chip_y = 2 * (1 - y) + x
        self.chip_xy = 2 * (1 - y) + 1 - x
        self.to_core = {"dp": dp + 1 - 2 * self.core}
        self.to_x = {"dp": dp + 2 - 4 * x}
        self.to_y = {"dp": dp + 4 - 8 * y}
        z = self.z
        self.z_hops = (z + 1 - 2 * (z % 2), (z + 2) % 4, 3 - z)
        self.to_z = tuple({"seq": hop} for hop in self.z_hops)
        self.partners = (self.to_core, self.to_x, self.to_y) + self.to_z

    def meet(self):
        barrier = pltpu.get_barrier_semaphore()
        for partner in self.partners:
            pl.semaphore_signal(barrier, inc=1, device_id=partner, device_id_type=MESH)
        pl.semaphore_wait(barrier, len(self.partners))


class Sender:
    def __init__(self, send_sem, recv_sem):
        self.send_sem, self.recv_sem = send_sem, recv_sem

    def copy(self, k, src, dst, partner):
        return pltpu.make_async_remote_copy(
            src_ref=src,
            dst_ref=dst,
            send_sem=self.send_sem.at[k],
            recv_sem=self.recv_sem.at[k],
            device_id=partner,
            device_id_type=MESH,
        )


class Gather:
    def __init__(self, here, sender, first_sem, count, own, own_row, pool, row_of):
        self.here, self.sender, self.k, self.n = here, sender, first_sem, count
        self.own, self.own_row, self.pool, self.row_of = own, own_row, pool, row_of
        self.half = count * BLK // 2

    def link(self, name):
        here, half = self.here, self.half

        def own(part):
            return self.own.at[pl.ds(self.own_row + part * half, half)]

        def piece(chip, part):
            return self.pool.at[pl.ds(self.row_of(chip, here.core) + part * half, half)]

        def whole(chip):
            return self.pool.at[pl.ds(self.row_of(chip, here.core), 2 * half)]

        order = ("x0", "x1", "y1", "y0", "y_on", "x_on", "share_x", "share_y", "share_xy", "share_me")
        src, dst, partner = {
            "x0": lambda: (own(0), piece(here.chip, 0), here.to_x),
            "x1": lambda: (own(1), piece(here.chip, 1), here.to_x),
            "y1": lambda: (own(1), piece(here.chip, 1), here.to_y),
            "y0": lambda: (own(0), piece(here.chip, 0), here.to_y),
            "y_on": lambda: (piece(here.chip_x, 0), piece(here.chip_x, 0), here.to_y),
            "x_on": lambda: (piece(here.chip_y, 1), piece(here.chip_y, 1), here.to_x),
            "share_x": lambda: (whole(here.chip_x), whole(here.chip_x), here.to_core),
            "share_y": lambda: (whole(here.chip_y), whole(here.chip_y), here.to_core),
            "share_xy": lambda: (whole(here.chip_xy), whole(here.chip_xy), here.to_core),
            "share_me": lambda: (
                self.own.at[pl.ds(self.own_row, 2 * half)], whole(here.chip), here.to_core
            ),
        }[name]()
        return self.sender.copy(self.k + order.index(name), src, dst, partner)

    def start(self):
        for name in ("x0", "y1", "x1", "y0", "share_me"):
            self.link(name).start()

    def pass_on(self):
        self.link("x0").wait_recv()
        self.link("y_on").start()
        self.link("y1").wait_recv()
        self.link("x_on").start()

    def share_near(self):
        self.link("x1").wait_recv()
        self.link("share_x").start()
        self.link("y0").wait_recv()
        self.link("share_y").start()

    def sent(self):
        for name in ("x0", "y1", "x1", "y0", "y_on", "x_on"):
            self.link(name).wait_send()

    def share_far(self):
        self.link("y_on").wait_recv()
        self.link("x_on").wait_recv()
        self.link("share_xy").start()

    def finish(self):
        for name in ("share_me", "share_x", "share_y", "share_xy"):
            self.link(name).wait_recv()

    def shared(self):
        for name in ("share_me", "share_x", "share_y", "share_xy"):
            self.link(name).wait_send()


def front_kernel(
    place_ref, mine_ref, lengths_ref, vec_ref, master_in, tokens_in,
    pool, q_out, k_out, v_out, ctx_out, w_out, tok_out, ctx_split, lse_ref,
    stage, give, take, near, pack, w, tok, qs, ks, vs, cs,
    send_sem, recv_sem, load_sem,
    *, plan,
):
    here = Place()
    z = here.z
    sender = Sender(send_sem, recv_sem)
    rows = SEQLEN
    own = tokens_in.shape[0] // 4
    part = tokens_in.shape[1]
    slots = master_in.shape[0]
    second = plan.listed - plan.first

    def local(src, dst, k):
        return pltpu.make_async_copy(src, dst, load_sem.at[k])

    load_master = local(master_in, stage, 0)
    load_master.start()
    own_tokens = [
        local(tokens_in.at[own * z + s], tok.at[pl.ds(s * rows + part * z, part)], 3 + s) for s in range(own)
    ]
    for load in own_tokens:
        load.start()
    here.meet()
    swaps = [
        sender.copy(
            own * hop + s,
            tokens_in.at[own * here.z_hops[hop] + s],
            tok.at[pl.ds(s * rows + part * z, part)],
            here.to_z[hop],
        )
        for hop in range(3)
        for s in range(own)
    ]
    for swap in swaps:
        swap.start()
    parts = (plan.first // 2, second // 2)
    starts = (0, plan.first)
    trades = [
        sender.copy(
            6 + i,
            give.at[pl.ds(i * parts[0] * BLK, parts[i] * BLK)],
            take.at[pl.ds(i * parts[0] * BLK, parts[i] * BLK)],
            here.to_core,
        )
        for i in range(2)
    ]
    load_master.wait()

    def held(entry):
        return stage[jnp.clip(mine_ref[entry] - here.core * slots, 0, slots - 1)].astype(jnp.bfloat16)

    for i in range(2):

        def fill_give(p, _):
            give[pl.ds((i * parts[0] + p) * BLK, BLK), :] = held(starts[i] + (1 - here.core) * parts[i] + p)
            return 0

        lax.fori_loop(0, parts[i], fill_give, 0)
        trades[i].start()

    def own_block(i, p):
        entry = starts[i] + here.core * parts[i] + p
        traded = take[pl.ds((i * parts[0] + p) * BLK, BLK), :]
        return jnp.where(mine_ref[entry] // slots == here.core, held(entry), traded)

    trades[0].wait_recv()

    def fill_near(p, _):
        near[pl.ds((here.chip * plan.first + here.core * parts[0] + p) * BLK, BLK), :] = own_block(0, p)
        return 0

    lax.fori_loop(0, parts[0], fill_near, 0)
    first = Gather(
        here, sender, 8, plan.first // 2, near, (here.chip * plan.first + here.core * (plan.first // 2)) * BLK, near,
        lambda chip, core: (chip * plan.first + core * (plan.first // 2)) * BLK,
    )
    then = Gather(
        here, sender, 18, second // 2, pack, 0, pool,
        lambda chip, core: (chip * plan.listed + plan.first + core * (second // 2)) * BLK,
    )
    first.start()

    trades[1].wait_recv()

    def fill_pack(p, _):
        pack[pl.ds(p * BLK, BLK), :] = own_block(1, p)
        return 0

    lax.fori_loop(0, parts[1], fill_pack, 0)
    own_second = local(
        pack, pool.at[pl.ds((here.chip * plan.listed + plan.first + here.core * parts[1]) * BLK, parts[1] * BLK)], 5
    )
    own_second.start()
    first.pass_on()
    first.share_near()
    first.sent()
    then.start()
    first.share_far()
    first.finish()

    def fill_w(b, _):
        at = place_ref[b]
        w[pl.ds(b * BLK, BLK), :] = near[pl.ds(((at // plan.listed) * plan.first + at % plan.listed) * BLK, BLK), :]
        return 0

    lax.fori_loop(0, HEAD_BLOCKS, fill_w, 0)
    keeps = [
        local(near.at[pl.ds(chip * plan.first * BLK, plan.first * BLK)], pool.at[pl.ds(chip * plan.listed * BLK, plan.first * BLK)], 6 + chip)
        for chip in range(4)
    ] + [local(w, w_out, 10)]
    for keep in keeps:
        keep.start()
    for load in own_tokens:
        load.wait()
    for swap in swaps:
        swap.wait_recv()
    keep_tok = local(tok, tok_out, 11)
    keep_tok.start()

    def send_ctx(s, hop):
        return sender.copy(
            28 + 3 * s + hop,
            cs.at[pl.ds(s * rows + part * here.z_hops[hop], part)],
            ctx_split.at[own * z + s],
            here.to_z[hop],
        )

    def keep_own(s):
        at = pl.ds(s * rows, rows)
        return [local(ref.at[at], out.at[at], 12 + k) for k, (ref, out) in enumerate(((qs, q_out), (ks, k_out), (vs, v_out), (cs, ctx_out)))] + [
            local(cs.at[pl.ds(s * rows + part * z, part)], ctx_split.at[own * z + s], 16)
        ]

    key = lax.broadcasted_iota(jnp.int32, (rows, 1), 0)

    def sequence(s, _):
        at = pl.ds(pl.multiple_of(s * rows, rows), rows)
        values = tok[at, :]
        qs[at, :] = ((mm(values, w[0:D, :]) + vec_ref[0:1, :]).astype(jnp.bfloat16) * 0.125).astype(jnp.bfloat16)
        ks[at, :] = mm(values, w[D : 2 * D, :]).astype(jnp.bfloat16)
        vs[at, :] = (mm(values, w[2 * D :, :]) + vec_ref[1:2, :]).astype(jnp.bfloat16)
        bias = jnp.where(key < lengths_ref[own * z + s], 0.0, MASKED)

        def pair(p, _):
            forward_pair(qs.at[at], ks.at[at], vs.at[at], cs.at[at], lse_ref, s, p, bias)
            return 0

        lax.fori_loop(0, PAIRS, pair, 0)
        for hop in range(3):
            send_ctx(s, hop).start()

        @pl.when(s > 0)
        def _():
            for keep in keep_own(s - 1):
                keep.wait()

        for keep in keep_own(s):
            keep.start()

        @pl.when(s == 0)
        def _():
            then.pass_on()

        return 0

    lax.fori_loop(0, own, sequence, 0)
    then.share_near()
    then.share_far()
    then.sent()
    then.finish()
    for keep in keep_own(own - 1) + keeps + [keep_tok, own_second]:
        keep.wait()
    for s in range(own):
        for hop in range(3):
            send_ctx(s, hop).wait_recv()
            send_ctx(s, hop).wait_send()
    for copy in swaps + trades:
        copy.wait_send()
    first.shared()
    then.shared()


def front(plan, place, mine, lengths, vec, master, tokens):
    seqs, part, _ = tokens.shape
    total = seqs * part
    own = total // SEQLEN
    any_spec = pl.BlockSpec(memory_space=pl.ANY)
    vmem = pl.BlockSpec(memory_space=pltpu.VMEM)
    smem = pl.BlockSpec(memory_space=pltpu.SMEM)
    low = jnp.bfloat16
    slots = master.shape[0]
    flat = jax.ShapeDtypeStruct((total, D), low)
    return pl.pallas_call(
        partial(front_kernel, plan=plan),
        in_specs=[smem] * 3 + [vmem] + [any_spec] * 2,
        out_specs=[any_spec] * 8 + [vmem],
        out_shape=[
            jax.ShapeDtypeStruct((4 * plan.listed * BLK, D), low),
            flat,
            flat,
            flat,
            flat,
            jax.ShapeDtypeStruct((3 * D, D), low),
            flat,
            jax.ShapeDtypeStruct(tokens.shape, low),
            jax.ShapeDtypeStruct((own, 16, SEQLEN), jnp.float32),
        ],
        scratch_shapes=[
            pltpu.VMEM(master.shape, jnp.float32),
            pltpu.VMEM((plan.listed // 2 * BLK, D), low),
            pltpu.VMEM((plan.listed // 2 * BLK, D), low),
            pltpu.VMEM((4 * plan.first * BLK, D), low),
            pltpu.VMEM(((plan.listed - plan.first) // 2 * BLK, D), low),
            pltpu.VMEM((3 * D, D), low),
        ]
        + [pltpu.VMEM((total, D), low)] * 5
        + [
            pltpu.SemaphoreType.DMA((34,)),
            pltpu.SemaphoreType.DMA((34,)),
            pltpu.SemaphoreType.DMA((17,)),
        ],
        compiler_params=pltpu.CompilerParams(
            vmem_limit_bytes=60 * MIB, collective_id=plan.ids[1], has_side_effects=True
        ),
        cost_estimate=pl.CostEstimate(
            flops=6 * total * D * D + 4 * total * SEQLEN * D,
            bytes_accessed=40 * total * D + 8 * slots * BLK * D,
            transcendentals=total * SEQLEN * H,
        ),
        name="front",
    )(place, mine, lengths, vec, master, tokens)


def add_rows(out_ref, out_row, terms, count, step=32):
    def body(i, _):
        value = None
        for ref, row in terms:
            part = ref[pl.ds(pl.multiple_of(row + i * step, step), step), :]
            value = part if value is None else value + part
        out_ref[pl.ds(pl.multiple_of(out_row + i * step, step), step), :] = value
        return 0

    lax.fori_loop(0, count // step, body, 0, unroll=2)


class Reduce:
    def __init__(self, plan, here, sender, first_sem, count, first, column, blk_ref, grad, pack, buffers, red):
        self.here, self.sender, self.k, self.listed = here, sender, first_sem, plan.listed
        self.n, self.first, self.blk, self.grad = count, first, blk_ref, grad
        self.acc, self.rx, self.ry, self.r2, self.z1, self.z2, self.fin = buffers
        self.red = red
        self.half = count * BLK // 2
        self.size = count * BLK
        self.cols = pl.ds(column, self.fin.shape[1])
        self.pack = pack.at[pl.ds(0, 4 * self.size), self.cols]

    def rows(self, ref, chip, half):
        return ref.at[pl.ds(chip * self.size + half * self.half, self.half)]

    def link(self, name):
        here, k, acc = self.here, self.k, self.acc
        keep = (here.z % 2) * self.half
        other = (1 - here.z % 2) * self.half
        mine = here.chip * self.size
        fin_keep = self.fin.at[pl.ds(keep, self.half)]
        order = (
            "core_xy", "core_x", "core_y", "core_me", "x_far", "x_near", "y_far", "y_near",
            "y_on", "x_on", "z_half", "z_far", "z_back", "share",
        )

        def across(chip):
            rows = pl.ds(chip * self.size, self.size)
            return self.pack.at[rows], acc.at[rows], here.to_core

        src, dst, partner = {
            "core_xy": lambda: across(here.chip_xy),
            "core_x": lambda: across(here.chip_x),
            "core_y": lambda: across(here.chip_y),
            "core_me": lambda: across(here.chip),
            "x_far": lambda: (self.rows(acc, here.chip_xy, 0), self.rx.at[1], here.to_x),
            "x_near": lambda: (self.rows(acc, here.chip_x, 0), self.rx.at[0], here.to_x),
            "y_far": lambda: (self.rows(acc, here.chip_xy, 1), self.ry.at[1], here.to_y),
            "y_near": lambda: (self.rows(acc, here.chip_y, 1), self.ry.at[0], here.to_y),
            "y_on": lambda: (self.rows(acc, here.chip_y, 0), self.r2.at[0], here.to_y),
            "x_on": lambda: (self.rows(acc, here.chip_x, 1), self.r2.at[1], here.to_x),
            "z_half": lambda: (acc.at[pl.ds(mine + other, self.half)], self.z1, here.to_z[0]),
            "z_far": lambda: (acc.at[pl.ds(mine + keep, self.half)], self.z2, here.to_z[1]),
            "z_back": lambda: (fin_keep, fin_keep, here.to_z[0]),
            "share": lambda: (self.fin, self.result(), here.to_core),
        }[name]()
        return self.sender.copy(k + order.index(name), src, dst, partner)

    def result(self):
        return self.red.at[pl.ds((self.first + self.here.core * self.n) * BLK, self.size), self.cols]

    def start_core(self):
        here, n = self.here, self.n
        chips = (here.chip_xy, here.chip_x, here.chip_y, here.chip)
        for chip, name in zip(chips, ("core_xy", "core_x", "core_y", "core_me")):

            def body(i, _):
                block = self.blk[chip * self.listed + self.first + (1 - here.core) * n + i]
                self.pack[pl.ds(chip * self.size + i * BLK, BLK), :] = self.grad[block, :, self.cols]
                return 0

            lax.fori_loop(0, n, body, 0)
            self.link(name).start()

    def sent_core(self):
        for name in ("core_xy", "core_x", "core_y", "core_me"):
            self.link(name).wait_send()

    def add_own(self, chip):
        here, n = self.here, self.n

        def body(i, _):
            entry = chip * self.listed + self.first + here.core * n + i
            block = self.blk[entry]
            for piece in range(0, BLK, 32):
                rows = pl.ds(pl.multiple_of(chip * self.size + i * BLK, BLK) + piece, 32)
                self.acc[rows, :] = self.acc[rows, :] + self.grad[block, piece : piece + 32, self.cols]
            return 0

        lax.fori_loop(0, n, body, 0)

    def start_far(self):
        self.link("core_xy").wait_recv()
        self.add_own(self.here.chip_xy)
        self.link("x_far").start()
        self.link("y_far").start()

    def start_near(self):
        self.link("core_x").wait_recv()
        self.add_own(self.here.chip_x)
        self.link("x_near").start()
        self.link("core_y").wait_recv()
        self.add_own(self.here.chip_y)
        self.link("y_near").start()

    def pass_plane(self):
        here = self.here
        self.link("x_far").wait_recv()
        at = here.chip_y * self.size
        add_rows(self.acc, at, ((self.acc, at), (self.rx.at[1], 0)), self.half)
        self.link("y_on").start()
        self.link("y_far").wait_recv()
        at = here.chip_x * self.size + self.half
        add_rows(self.acc, at, ((self.acc, at), (self.ry.at[1], 0)), self.half)
        self.link("x_on").start()

    def start_z(self):
        here = self.here
        mine = here.chip * self.size
        self.link("core_me").wait_recv()
        self.add_own(here.chip)
        self.link("x_near").wait_recv()
        self.link("y_on").wait_recv()
        add_rows(self.acc, mine, ((self.acc, mine), (self.rx.at[0], 0), (self.r2.at[0], 0)), self.half)
        self.link("y_near").wait_recv()
        self.link("x_on").wait_recv()
        low = mine + self.half
        add_rows(self.acc, low, ((self.acc, low), (self.ry.at[0], 0), (self.r2.at[1], 0)), self.half)
        self.link("z_half").start()

    def far_z(self):
        here = self.here
        keep = here.chip * self.size + (here.z % 2) * self.half
        self.link("z_half").wait_recv()
        add_rows(self.acc, keep, ((self.acc, keep), (self.z1, 0)), self.half)
        self.link("z_far").start()

    def back_z(self):
        here = self.here
        keep = (here.z % 2) * self.half
        self.link("z_far").wait_recv()
        add_rows(self.fin, keep, ((self.acc, here.chip * self.size + keep), (self.z2, 0)), self.half)
        self.link("z_back").start()

    def share(self, local_sem):
        red = self.result()
        self.link("z_back").wait_recv()
        self.link("z_back").wait_send()
        self.link("share").start()
        pltpu.make_async_copy(self.fin, red, local_sem).start()

    def finish(self, local_sem):
        red = self.result()
        self.link("share").wait_recv()
        pltpu.make_async_copy(self.fin, red, local_sem).wait()
        for name in ("x_far", "x_near", "y_far", "y_near", "y_on", "x_on", "z_half", "z_far", "share"):
            self.link(name).wait_send()


def back_pair(q_ref, k_ref, v_ref, ctx_ref, do_ref, lse_ref, seq, p, bias):
    rows = q_ref.shape[0]
    cols = pl.ds(pl.multiple_of(p * LANES, LANES), LANES)
    row8 = lax.broadcasted_iota(jnp.int32, (16, rows), 0)

    def extra_rows(lead, row):
        one, two, three = (part.astype(jnp.float32) for part in split3(row))
        return jnp.where(
            row8 == 0, lead, jnp.where(row8 == 1, one, jnp.where(row8 == 2, two, jnp.where(row8 == 3, three, 0.0)))
        )

    q2, k2, v2, do2 = q_ref[:, cols], k_ref[:, cols], v_ref[:, cols], do_ref[:, cols]
    q2t, k2t, do2t = q2.T, k2.T, do2.T
    prod = do2t.astype(jnp.float32) * ctx_ref[:, cols].T.astype(jnp.float32)
    dq_parts = []
    d_key = jnp.zeros((rows, LANES), jnp.float32)
    d_value = jnp.zeros((rows, LANES), jnp.float32)
    for half in range(2):
        head = slice(half * DH, half * DH + DH)
        inside, spare = spare_lanes(rows, half, bias)
        zero = jnp.zeros_like(k2)
        lse = lse_ref[seq, pl.ds(2 * p + half, 1), :]
        delta = jnp.sum(prod[head], axis=0, keepdims=True)
        scores = mm(jnp.where(inside, k2, spare), beside(q2t[head], extra_rows(1.0, -lse), half))
        probs = jnp.exp(scores)
        d_probs = mm(jnp.where(inside, v2, spare), beside(do2t[head], extra_rows(0.0, -delta), half))
        d_scores = (probs * d_probs).astype(jnp.bfloat16)
        d_value += mm(probs.astype(jnp.bfloat16), jnp.where(inside, do2, zero))
        d_key += mm(d_scores, jnp.where(inside, q2, zero))
        dq_parts.append(mm(k2t[head], d_scores))
    d_query = jnp.concatenate(dq_parts, axis=0).T * 0.125
    return cols, d_query.astype(jnp.bfloat16), d_key.astype(jnp.bfloat16), d_value.astype(jnp.bfloat16)


def tail_kernel(
    blk_ref, lengths_ref, vec_in, squares_in, lse_ref,
    dctx_in, ctx_split, dbranch, dinner, mid, act, dfeed, tok_in, q_in, k_in, v_in, ctx_in, w_in,
    red, ingrad, vec_out, rms_out,
    grad, pack, d3, att, tok, w, *rest, plan,
):
    here = Place()
    z = here.z
    phase_buffers = [rest[7 * i : 7 * i + 7] for i in range(4)]
    vec_src, vec_land, rms_src, rms_land, send_sem, recv_sem, load_sem = rest[28:]
    sender = Sender(send_sem, recv_sem)
    rows = SEQLEN
    own = dctx_in.shape[0] // 4
    part = dctx_in.shape[1]
    total = own * rows
    wide = D // 2

    def local(src, dst, k):
        return pltpu.make_async_copy(src, dst, load_sem.at[k])

    first_loads = (
        local(ctx_split, att.at[2], 0),
        local(dinner.at[:, pl.ds(0, D)], att.at[3], 1),
        local(dbranch, d3.at[0], 2),
        local(mid, d3.at[1], 3),
        local(dfeed, d3.at[2], 4),
        local(q_in, att.at[0], 5),
        local(k_in, att.at[1], 6),
        local(tok_in, tok, 7),
        local(w_in, w, 10),
    )
    for load in first_loads[:5]:
        load.start()
    here.meet()

    def swap(half, s, hop):
        cols = pl.ds(half * wide, wide)
        return sender.copy(
            6 * half + 3 * s + hop,
            dctx_in.at[own * here.z_hops[hop] + s, :, cols],
            att.at[4, pl.ds(s * rows + part * z, part), cols],
            here.to_z[hop],
        )

    swaps = [[swap(half, s, hop) for s in range(own) for hop in range(3)] for half in range(2)]
    own_swaps = [local(dctx_in.at[own * z + s], att.at[4, pl.ds(s * rows + part * z, part)], 8 + s) for s in range(own)]
    for copy in swaps[0] + own_swaps:
        copy.start()
    for load in first_loads[2:5]:
        load.wait()

    early, middle = (
        Reduce(plan, here, sender, 24 + 14 * i, count // 2, first, 0, blk_ref, grad, pack, phase_buffers[i], red)
        for i, (count, first) in enumerate(((plan.early, 0), (plan.middle, plan.early)))
    )
    late = [
        Reduce(plan, here, sender, 52 + 14 * i, plan.late // 2, plan.early + plan.middle, i * wide, blk_ref, grad, pack, phase_buffers[2 + i], red)
        for i in range(2)
    ]

    def grads(step, _):
        slot = 2 + step % 2
        held = att.at[slot]
        pltpu.make_async_copy(held, held, load_sem.at[step % 2]).wait()
        value = mm_tn(att[slot], d3[(step + 3) // 4])
        grad[pl.ds(HEAD_BLOCKS + step * (D // BLK), D // BLK)] = value.astype(jnp.bfloat16).reshape(D // BLK, BLK, D)

        @pl.when(step < CHUNKS - 1)
        def _():
            local(dinner.at[:, pl.ds((step + 1) * D, D)], held, step % 2).start()

        @pl.when((step >= CHUNKS - 1) & (step < 2 * CHUNKS - 1))
        def _():
            local(act.at[:, pl.ds((step - CHUNKS + 1) * D, D)], held, step % 2).start()

        @pl.when(step == CHUNKS)
        def _():
            early.start_core()

        @pl.when(step == CHUNKS + 2)
        def _():
            early.start_far()

        return 0

    for load in first_loads[5:]:
        load.start()
    grad[0:HEAD_BLOCKS] = jnp.zeros((HEAD_BLOCKS, BLK, D), jnp.bfloat16)
    lax.fori_loop(0, 1 + 2 * CHUNKS, grads, 0)
    more_loads = (local(v_in, att.at[2], 0), local(ctx_in, att.at[3], 1))
    for load in more_loads:
        load.start()
    early.sent_core()
    middle.start_core()
    early.start_near()
    for copy in swaps[0]:
        copy.wait_send()
    for copy in swaps[1]:
        copy.start()
    for load in first_loads[5:] + tuple(own_swaps) + more_loads:
        load.wait()
    for copy in swaps[0]:
        copy.wait_recv()

    key = lax.broadcasted_iota(jnp.int32, (rows, 1), 0)

    def head_grads(half):
        cols = pl.ds(half * wide, wide)
        for block, which in ((0, 1), (6, 2), (12, 0)):
            value = mm_tn(tok[...], d3[which, :, cols]).astype(jnp.bfloat16)
            grad[block : block + 6, :, cols] = value.reshape(D // BLK, BLK, wide)

    def send_ingrad(s, hop):
        return sender.copy(
            80 + 3 * s + hop,
            att.at[0, pl.ds(s * rows + part * here.z_hops[hop], part)],
            ingrad.at[own * z + s],
            here.to_z[hop],
        )

    def own_ingrad(s):
        return local(att.at[0, pl.ds(s * rows + part * z, part)], ingrad.at[own * z + s], 11 + s)

    def input_gradient(s):
        at = pl.ds(s * rows, rows)
        value = mm_nt(d3[1, at, :], w[0:D, :])
        value += mm_nt(d3[2, at, :], w[D : 2 * D, :])
        value += mm_nt(d3[0, at, :], w[2 * D :, :])
        att[0, at, :] = value.astype(jnp.bfloat16)
        for hop in range(3):
            send_ingrad(s, hop).start()
        own_ingrad(s).start()

    def second_half():
        for copy in swaps[1]:
            copy.wait_recv()

    group = PAIRS // 2

    def pair_step(i, _):
        s = (i // group) % own
        p = (i // (own * group)) * group + i % group
        bias = jnp.where(key < lengths_ref[own * z + s], 0.0, MASKED)
        at = pl.ds(pl.multiple_of(s * rows, rows), rows)
        cols, d_query, d_key, d_value = back_pair(*(att.at[k, at] for k in range(5)), lse_ref, s, p, bias)
        d3[1, at, cols] = d_query
        d3[2, at, cols] = d_key
        d3[0, at, cols] = d_value

        stages = {
            0: (early.pass_plane,),
            3: (middle.start_far,),
            4: (early.start_z, middle.start_near),
            5: (lambda: head_grads(0), second_half),
            6: (early.far_z, middle.pass_plane),
            8: (middle.sent_core, late[0].start_core, lambda: input_gradient(0)),
            9: (middle.start_z, late[0].start_far),
            10: (late[0].start_near,),
            11: (late[0].pass_plane,),
        }
        for at_step, calls in stages.items():

            @pl.when(i == at_step)
            def _():
                for call in calls:
                    call()

        return 0

    lax.fori_loop(0, own * PAIRS, pair_step, 0)

    head_grads(1)
    late[1].start_core()
    vec_src[0] = vec_in[...]
    vec_src[0, 0:1, :] = jnp.sum(d3[1].astype(jnp.float32), axis=0, keepdims=True)
    vec_src[0, 1:2, :] = jnp.sum(d3[0].astype(jnp.float32), axis=0, keepdims=True)
    for i in range(squares_in.shape[0]):
        sums = jnp.sum(squares_in[i], axis=-1, keepdims=True)
        rms_src[0, 8 * i : 8 * i + 8, :] = jnp.broadcast_to(sums, (8, LANES))
    ways = (here.to_z[0], here.to_z[1], here.to_core, here.to_x, here.to_y)
    vec_copies = [sender.copy(12 + w, vec_src.at[w], vec_land.at[w], way) for w, way in enumerate(ways)]
    rms_copies = [sender.copy(17 + w, rms_src.at[w], rms_land.at[w], ways[w]) for w in range(2)]

    def vec_step(w):
        if w > 0:
            vec_copies[w - 1].wait_recv()
            after = vec_src[w - 1] + vec_land[w - 1]
            if w < len(ways):
                vec_src[w] = after
            else:
                vec_out[...] = after
        if w < len(ways):
            vec_copies[w].start()
        if 0 < w <= 2:
            rms_copies[w - 1].wait_recv()
            after = rms_src[w - 1] + rms_land[w - 1]
            if w < 2:
                rms_src[w] = after
            else:
                lane = lax.broadcasted_iota(jnp.int32, (1, LANES), 1)
                tiles = squares_in.shape[0]
                each = dctx_in.shape[0] // tiles
                for n in range(dctx_in.shape[0]):
                    row = 8 * (n // each) + 2 * (n % each)
                    sums = jnp.where(lane == 0, after[row : row + 1], after[row + 1 : row + 2])
                    rms_out[n : n + 1, :] = jnp.sqrt(sums / (lengths_ref[n].astype(jnp.float32) * D))
        if w < 2:
            rms_copies[w].start()

    vec_step(0)
    late[1].start_far()
    early.back_z()
    middle.far_z()
    vec_step(1)
    late[0].start_z()
    late[1].start_near()
    late[1].pass_plane()
    vec_step(2)
    late[1].start_z()
    late[0].far_z()
    vec_step(3)
    early.share(load_sem.at[13])
    middle.back_z()
    vec_step(4)
    late[1].far_z()
    input_gradient(1)
    vec_step(5)
    late[0].back_z()
    late[1].back_z()
    middle.share(load_sem.at[14])
    late[0].share(load_sem.at[15])
    late[1].share(load_sem.at[16])
    for phase in late:
        phase.sent_core()
    for i, phase in enumerate((early, middle, late[0], late[1])):
        phase.finish(load_sem.at[13 + i])
    for copy in swaps[1] + vec_copies + rms_copies:
        copy.wait_send()
    for s in range(own):
        own_ingrad(s).wait()
        for hop in range(3):
            send_ingrad(s, hop).wait_recv()
            send_ingrad(s, hop).wait_send()


def tail(plan, blk, lengths, vec, squares, lse, d_ctx, ctx_split, d_branch, d_inner, mid, act, d_feed, tokens, q, k, v, ctx, w):
    total = tokens.shape[0]
    any_spec = pl.BlockSpec(memory_space=pl.ANY)
    vmem = pl.BlockSpec(memory_space=pltpu.VMEM)
    smem = pl.BlockSpec(memory_space=pltpu.SMEM)
    low = jnp.bfloat16
    sums = (8 * squares.shape[0], LANES)

    def phase(n, width):
        half = n * BLK // 2
        return [
            pltpu.VMEM((4 * n * BLK, width), low),
            pltpu.VMEM((2, half, width), low),
            pltpu.VMEM((2, half, width), low),
            pltpu.VMEM((2, half, width), low),
            pltpu.VMEM((half, width), low),
            pltpu.VMEM((half, width), low),
            pltpu.VMEM((n * BLK, width), low),
        ]

    return pl.pallas_call(
        partial(tail_kernel, plan=plan),
        in_specs=[smem] * 2 + [vmem] * 3 + [any_spec] * 13,
        out_specs=[any_spec] * 2 + [vmem] * 2,
        out_shape=[
            jax.ShapeDtypeStruct((LOOSE.listed * BLK, D), low),
            jax.ShapeDtypeStruct(d_ctx.shape, low),
            jax.ShapeDtypeStruct(vec.shape, jnp.float32),
            jax.ShapeDtypeStruct((d_ctx.shape[0], LANES), jnp.float32),
        ],
        scratch_shapes=[
            pltpu.VMEM((HEAD_BLOCKS + (D + 2 * FF) // BLK, BLK, D), low),
            pltpu.VMEM((2 * max(plan.early, plan.middle, plan.late) * BLK, D), low),
            pltpu.VMEM((3, total, D), low),
            pltpu.VMEM((5, total, D), low),
            pltpu.VMEM((total, D), low),
            pltpu.VMEM((3 * D, D), low),
        ]
        + phase(plan.early // 2, D)
        + phase(plan.middle // 2, D)
        + phase(plan.late // 2, D // 2)
        + phase(plan.late // 2, D // 2)
        + [
            pltpu.VMEM((5,) + vec.shape, jnp.float32),
            pltpu.VMEM((5,) + vec.shape, jnp.float32),
            pltpu.VMEM((2,) + sums, jnp.float32),
            pltpu.VMEM((2,) + sums, jnp.float32),
            pltpu.SemaphoreType.DMA((86,)),
            pltpu.SemaphoreType.DMA((86,)),
            pltpu.SemaphoreType.DMA((17,)),
        ],
        compiler_params=pltpu.CompilerParams(
            vmem_limit_bytes=63 * MIB, collective_id=plan.ids[0], has_side_effects=True
        ),
        cost_estimate=pl.CostEstimate(
            flops=2 * total * D * (6 * D + 2 * FF) + 10 * total * SEQLEN * D,
            bytes_accessed=total * (24 * D + 4 * FF) + 8 * FF * D,
            transcendentals=total * SEQLEN * H,
        ),
        name="tail",
    )(blk, lengths, vec, squares, lse, d_ctx, ctx_split, d_branch, d_inner, mid, act, d_feed, tokens, q, k, v, ctx, w)


def tables_kernel(owner_ref, place_ref, mine_ref, block_ref, spot_ref, has_ref, fits_ref, *, slots, plan):
    dp = lax.axis_index("dp")
    chip_slots = 2 * slots
    near_blocks = HEAD_BLOCKS + (D + FF) // BLK
    for ref in (mine_ref, block_ref, spot_ref, has_ref):
        for i in range(ref.shape[0]):
            ref[i] = 0

    def body(b, counts):
        listed, early, middle, late, bad = counts
        slot = owner_ref[b]
        chip = slot // chip_slots
        shift = 8 * chip
        one = jnp.left_shift(1, shift)

        def count(packed):
            return jnp.right_shift(packed, shift) & 255

        order = count(listed)
        n_early, n_middle, n_late = count(early), count(middle), count(late)
        body_block = b >= HEAD_BLOCKS
        in_early = body_block & (b < near_blocks) & (n_early < plan.early)
        in_middle = body_block & jnp.logical_not(in_early) & (n_middle < plan.middle)
        in_late = jnp.logical_not(in_early | in_middle)
        spot = jnp.where(in_early, n_early, jnp.where(in_middle, plan.early + n_middle, plan.early + plan.middle + n_late))
        wrong = (order >= plan.listed) | (spot >= plan.listed) | (jnp.logical_not(body_block) & (order >= plan.first))
        spot = jnp.minimum(spot, plan.listed - 1)
        place_ref[b] = chip * plan.listed + jnp.minimum(order, plan.listed - 1)
        block_ref[chip * plan.listed + spot] = b

        mine_ref[jnp.where(chip == dp // 2, jnp.minimum(order, plan.listed - 1), plan.listed)] = slot - chip * chip_slots
        own_slot = jnp.where(slot // slots == dp, slot % slots, slots)
        spot_ref[own_slot] = spot
        has_ref[own_slot] = 1

        return (
            listed + one,
            early + jnp.where(in_early, one, 0),
            middle + jnp.where(in_middle, one, 0),
            late + jnp.where(in_late, one, 0),
            bad | wrong.astype(jnp.int32),
        )

    zero = jnp.int32(0)
    counts = lax.fori_loop(0, owner_ref.shape[0], body, (zero,) * 5, unroll=8)
    fits_ref[0] = 1 - counts[4]


def tables(plan, owner, slots):
    chips = lax.axis_size("dp") // 2
    smem = pl.BlockSpec(memory_space=pltpu.SMEM)
    sizes = (owner.shape[0], plan.listed + 1, chips * plan.listed, slots + 1, slots + 1, 1)
    return pl.pallas_call(
        partial(tables_kernel, slots=slots, plan=plan),
        in_specs=[smem],
        out_specs=[smem] * len(sizes),
        out_shape=[jax.ShapeDtypeStruct((n,), jnp.int32) for n in sizes],
        name="tables",
    )(owner)


def general(tokens, cotangent, lengths, owner, master, vec_master):
    slot_local = master.shape[0]
    gathered = lax.all_gather(master.astype(jnp.bfloat16), "dp", axis=0, tiled=True)
    seq_place = lax.axis_index("seq")
    slot_total = slot_local * lax.axis_size("dp")
    tokens = to_whole(tokens, "seq")
    cotangent = to_whole(cotangent, "seq")
    seq_count, seq_len, width = tokens.shape
    token_count = seq_count * seq_len
    lengths = lax.dynamic_slice_in_dim(lengths, seq_place * seq_count, seq_count)
    q, k, v, ctx, lse, _ = attend(owner, lengths, tokens, gathered, vec_master)
    flat = tokens.reshape(token_count, D)
    _, mid, out, act, d_inner, d_feed, d_branch, d_ctx, vec_feed, squares = feed_both(
        owner, lengths, seq_len,
        flat, ctx, cotangent.reshape(token_count, D), gathered, vec_master,
    )
    held = feed_grads(owner, slot_total, ctx, d_branch, d_inner, mid, act, d_feed)
    ingrad, vec_attend, held = attend_back(
        owner, owner, lengths, tokens, q, k, v, ctx, d_ctx, lse, d_branch, gathered, held
    )
    local_sums = jnp.sum(squares.reshape(seq_count, -1, 8, D)[:, :, :2], axis=(1, 3))
    own_rms = jnp.sqrt(local_sums / (lengths[:, None].astype(jnp.float32) * D))
    sublayer_rms = lax.all_gather(own_rms, "seq", axis=0, tiled=True)
    vec_local = jnp.concatenate([vec_attend[:2], vec_feed[2:12]], axis=0)
    vec_grad = lax.psum(vec_local, ("dp", "seq"))
    owned = lax.psum_scatter(held, "dp", scatter_dimension=0, tiled=True)
    reduced = lax.psum(owned, "seq")
    first_slot = lax.axis_index("dp") * slot_local
    slots = jnp.arange(slot_local + 1, dtype=jnp.int32)
    has = jnp.any((first_slot + slots)[:, None] == owner[None, :], axis=1).astype(jnp.int32)
    whole = (seq_count, seq_len, D)
    return (
        to_split(out.reshape(whole), "seq"),
        jnp.zeros((token_count, D), jnp.bfloat16),
        to_split(ingrad.reshape(whole), "seq").reshape(token_count, D),
        to_split(mid.reshape(whole), "seq").astype(jnp.float32),
        jnp.pad(sublayer_rms, ((0, 0), (0, LANES - 2))),
        jnp.pad(vec_grad, ((0, 4), (0, 0))),
        reduced,
        slots,
        has,
    )


def listed(plan, tokens, cotangent, lengths, owner, master, vec_master, place, mine, block, spot, has):
    seqs, part, _ = tokens.shape
    total = seqs * part
    pool, q, k, v, ctx, w, whole, ctx_split, lse = front(
        plan, place, mine, lengths, vec_master, master, tokens
    )
    ctx_split = ctx_split.reshape(total, D)
    wide_mid, mid, out, act, d_inner, d_feed, d_branch, d_ctx, vec_feed, squares = feed_both(
        place, lengths, part,
        tokens.reshape(total, D), ctx_split, cotangent.reshape(total, D), pool.reshape(-1, BLK, D), vec_master,
    )
    reduced, ingrad, vec_grad, rms = tail(
        plan, block, lengths, vec_feed, squares, lse, d_ctx.reshape(seqs, part, D), ctx_split, d_branch, d_inner,
        mid, act, d_feed, whole, q, k, v, ctx, w,
    )
    return (
        out.reshape(tokens.shape),
        d_branch,
        ingrad.reshape(total, D),
        wide_mid.reshape(tokens.shape),
        rms,
        vec_grad,
        reduced.reshape(-1, BLK, D),
        spot,
        has,
    )


def per_device(
    tokens, cotangent, lengths, owner, master, moment, second, vec_master, vec_moment, vec_second
):
    slot_local = master.shape[0]
    given = (tokens, cotangent, lengths, owner, master, vec_master)
    if lax.axis_size("dp") == 8 and lax.axis_size("seq") == 4:

        def spread(*args):
            results = general(*args)
            pad = ((0, LOOSE.listed - slot_local), (0, 0), (0, 0))
            return results[:6] + (jnp.pad(results[6], pad),) + results[7:]

        def attempt(plan, otherwise, *args):
            place, mine, block, spot, has, fits = tables(plan, args[3], slot_local)

            def fitting(*every):
                return listed(plan, *every)

            def other(*every):
                return otherwise(*every[:6])

            return lax.cond(fits[0] > 0, fitting, other, *args, place, mine, block, spot, has)

        results = attempt(LOOSE, spread, *given)
    else:
        results = general(*given)
    layer_out, d_res, ingrad, residual_mid, rms, vec_grad, reduced, spot, has = results
    updated = adam_all(
        spot, has, reduced, moment, second, master,
        d_res, ingrad, rms, vec_grad, vec_moment, vec_second, vec_master,
    )
    input_grad, sublayer_rms, slots, vectors = updated[0], updated[1], updated[2:6], updated[6:]
    return (layer_out, input_grad.reshape(tokens.shape), residual_mid, sublayer_rms, *slots, *vectors)


def solution(mesh):
    return jax.shard_map(
        per_device,
        mesh=mesh,
        in_specs=(
            P("dp", "seq", None),
            P("dp", "seq", None),
            P("dp"),
            P(),
            P("dp", None, None),
            P("dp", None, None),
            P("dp", None, None),
            P(),
            P(),
            P(),
        ),
        out_specs=(
            P("dp", "seq", None),
            P("dp", "seq", None),
            P("dp", "seq", None),
            P("dp", None),
            P("dp", None, None),
            P("dp", None, None),
            P("dp", None, None),
            P("dp", None, None),
            P(),
            P(),
            P(),
            P(),
        ),
        check_vma=False,
    )
```
